32 devices in a mesh: dp: 4 (over y, core), expert: 8 (over z, x).
Axes of the slice: x: 2, y: 2, z: 4, core: 2. Of those that a mesh axis runs over, the one named last changes fastest.
Arguments:
- tokens: bfloat16 [16384, 768], P(('dp', 'expert')), may hold values from -6 to 6
- cotangent: bfloat16 [16384, 768], P(('dp', 'expert')), may hold values from -6 to 6
- norm1_gain: float32 [768], replicated, may hold values from 0.1 to 1.9
- qkv_weight: bfloat16 [768, 2304], replicated, may hold values from -0.21875 to 0.21875
- out_weight: bfloat16 [768, 768], replicated, may hold values from -2.5 to 2.5
- norm2_gain: float32 [768], replicated, may hold values from 0.1 to 1.9
- router_weight: float32 [768, 8], replicated, may hold values from -0.15625 to 0.15625
- up_weight: bfloat16 [8, 768, 3072], P('expert'), may hold values from -0.21875 to 0.21875
- down_weight: bfloat16 [8, 3072, 768], P('expert'), may hold values from -0.21875 to 0.21875
- routes: int32 [16384], P(('dp', 'expert')), may hold values from 0 to 7, as said below
- capacity: int32 [8], replicated, may hold values from 48 to 96, as said below
Outputs:
- block_out: bfloat16 [16384, 768], P(('dp', 'expert'))
- tokens_grad: float32 [16384, 768], P(('dp', 'expert'))
- norm1_gain_grad: float32 [768], P(('dp', 'expert'))
- qkv_weight_grad: float32 [768, 2304], P(('dp', 'expert'))
- out_weight_grad: float32 [768, 768], P(('dp', 'expert'))
- norm2_gain_grad: float32 [768], P(('dp', 'expert'))
- router_weight_grad: float32 [768, 8], P(('dp', 'expert'))
- up_weight_grad: float32 [8, 768, 3072], P('expert', None, 'dp')
- down_weight_grad: float32 [8, 3072, 768], P('expert', 'dp')
The draws below stay inside these ranges and needn't reach their ends.
Inputs may be any that keep to these rules, and one draw needn't show every extreme that they name: `routes`: on each device's 512 tokens no expert is named more than 96 times; one expert, the same on every device, is named exactly 96 times on each device. The expert named 96 times on every device has capacity 96.
All inputs are finite; a program needn't handle non-finite values.
Results may differ from the reference program's by a relative error of at most 0.013.
Values may be sent and summed in bfloat16 or wider, within the bound.
No kernel may reach another device: no remote copies, remote signals or barrier semaphores. Data moves between devices by JAX's collectives and lax.ppermute only.
A program may use at most 192 MiB of HBM per device.

```python
import math
import jax
import jax.numpy as jnp
from jax import lax

D = 768
HEADS = 12
HDIM = 64
FF = 3072
TOK_DEV = 512
EXPERTS = 8
CAP = 96
TOKENS = 16384


def pick_full(key):
    return jax.random.randint(key, (), 0, EXPERTS)


def draw_routes(key, part):
    full = pick_full(key)
    key = jax.random.fold_in(key, 11)
    key_rank, key_blocks = jax.random.split(key)
    order = jax.random.permutation(key_rank, EXPERTS)
    ranking = jnp.argsort(order).astype(jnp.int32)
    expert_ids = jnp.arange(EXPERTS, dtype=jnp.int32)
    ranking = jnp.where(expert_ids == full, 0, ranking + 1)
    factor = jnp.maximum(64 // (ranking + 2), 1)
    slot_total = EXPERTS * CAP
    slot_expert = jnp.arange(slot_total, dtype=jnp.int32) // CAP

    def one_block(block_key):
        key_score, key_order = jax.random.split(block_key)
        raw = jax.random.randint(key_score, (slot_total,), 0, 1 << 12)
        score = raw * factor[slot_expert]
        score = jnp.where(slot_expert == full, (1 << 18) + raw, score)
        score = score * slot_total + jnp.arange(slot_total, dtype=jnp.int32)
        chosen_vals, chosen = lax.top_k(score, TOK_DEV)
        picked = chosen // CAP
        shuffle = jax.random.permutation(key_order, TOK_DEV)
        return picked[shuffle].astype(jnp.int32)
    block_keys = jax.random.split(key_blocks, TOKENS // TOK_DEV)
    return jax.vmap(one_block)(block_keys).reshape(TOKENS).astype(jnp.int32)


def draw_capacity(key, part):
    full = pick_full(key)
    key = jax.random.fold_in(key, 23)
    limits = jax.random.randint(key, (EXPERTS,), CAP // 2, CAP + 1)
    return jnp.where(jnp.arange(EXPERTS, dtype=jnp.int32) == full, CAP, limits).astype(jnp.int32)


def raised(entries, own_key, source, target, shards_of, factor):
    owner, partner = [(jnp.arange(entries.shape[axis_at]) // (entries.shape[axis_at] // shards_of)).reshape([-1 if axis == axis_at else 1 for axis in range(entries.ndim)]) for axis_at in (source, target)]
    chosen = jax.random.permutation(own_key, shards_of)[partner]
    strong = (owner == chosen) | (owner == (partner + shards_of // 2) % shards_of)
    return jnp.where(strong, factor * entries, entries)


def steps_of(own_key, extent, shards, least, top_value):
    level, own = 1.0, jax.random.fold_in(own_key, 6)
    for dim, shards_of in shards:
        draws = jnp.exp(jax.random.uniform(jax.random.fold_in(own, dim), (shards_of,), jnp.float32, least / len(shards), top_value / len(shards)))
        level = level * jnp.repeat(draws, extent[dim] // shards_of).reshape([-1 if axis == dim else 1 for axis in range(len(extent))])
    return level


def centred(key, dims, scale, most, cuts=(), kind=jnp.bfloat16):
    level = steps_of(key, dims, cuts, -0.22, 0.18) if cuts else 1.0
    values = jax.random.normal(key, dims, jnp.float32) * scale * level
    return jnp.minimum(jnp.maximum(values, -most), most).astype(kind)


def heavy_noise(stream_key, dims, scale, bound, shards, heavy, kind=jnp.bfloat16):
    values = scale * jax.random.normal(stream_key, dims, jnp.float32)
    if shards:
        values = values * steps_of(stream_key, dims, shards, -0.22, 0.18)
    return jnp.clip(raised(values, jax.random.fold_in(stream_key, 3), *heavy), -bound, bound).astype(kind)


def setup_inputs(seed: int = 0) -> dict:
    key_list = jax.random.split(jax.random.key(seed), 12)
    return {
        "tokens": heavy_noise(key_list[0], (TOKENS, D), 1.0, 6.0, ((0, 32),), (0, 1, 32, 2.75)),
        "cotangent": centred(key_list[1], (TOKENS, D), 1.0, 6.0, ((0, 32),)),
        "norm1_gain": jnp.clip(1.0 + 0.18 * jax.random.normal(key_list[2], (D,), jnp.float32), 0.1, 1.9),
        "qkv_weight": centred(key_list[3], (D, 3 * D), D ** -0.5, 0.21875),
        "out_weight": centred(key_list[4], (D, D), (D // 128) ** -0.5, 2.5),
        "norm2_gain": jnp.clip(1.0 + 0.18 * jax.random.normal(key_list[5], (D,), jnp.float32), 0.1, 1.9),
        "router_weight": centred(key_list[6], (D, EXPERTS), (2 * D) ** -0.5, 0.15625, (), jnp.float32),
        "up_weight": centred(key_list[7], (EXPERTS, D, FF), D ** -0.5, 0.21875, ((0, 8),)),
        "down_weight": centred(key_list[8], (EXPERTS, FF, D), (FF // 4) ** -0.5, 0.21875, ((0, 8),)),
        "routes": draw_routes(jax.random.fold_in(key_list[11], 71), 0),
        "capacity": draw_capacity(jax.random.fold_in(key_list[11], 71), 0),
    }


EPS = 1e-05
HIGH = lax.Precision.HIGHEST

@jax.custom_vjp
def low(v):
    return lax.optimization_barrier(v.astype(jnp.bfloat16)).astype(jnp.float32)

@jax.custom_vjp
def low_back(v):
    return v

def low_keep(v):
    return (low(v), None)

def low_pass(kept, grad):
    return (grad,)

def back_keep(v):
    return (v, None)

def back_low(kept, grad):
    return (low(grad),)
low.defvjp(low_keep, low_pass)
low_back.defvjp(back_keep, back_low)

def layer_norm(value, gain):
    center = value - lax.optimization_barrier(jnp.mean(value, -1, keepdims=True))
    spread = lax.optimization_barrier(jnp.mean(center * center, -1, keepdims=True))
    return center * lax.rsqrt(spread + EPS) * gain

def both_ways(value):
    return low(low_back(value))

def attend_group(group, norm1_gain, qkv_weight, out_weight):
    count, length, width = group.shape
    act = low(layer_norm(group, norm1_gain))
    qkv = both_ways(jnp.einsum('gtd,de->gte', act, qkv_weight, precision=HIGH))
    query = qkv[..., :width].reshape(count, length, HEADS, HDIM)
    keys = qkv[..., width:2 * width].reshape(count, length, HEADS, HDIM)
    values = qkv[..., 2 * width:].reshape(count, length, HEADS, HDIM)
    scores = jnp.einsum('gqhd,gkhd->ghqk', query, keys, precision=HIGH) * (1.0 / math.sqrt(HDIM))
    scores = low_back(scores)
    rows = jnp.arange(length)[:, None]
    cols = jnp.arange(length)[None, :]
    scores = jnp.where(rows >= cols, scores, -1e+30)
    top = lax.optimization_barrier(jnp.max(scores, -1, keepdims=True))
    expo = jnp.exp(scores - top)
    probs = expo / lax.optimization_barrier(jnp.sum(expo, -1, keepdims=True))
    mixed = jnp.einsum('ghqk,gkhd->gqhd', low(probs), values, precision=HIGH).reshape(count, length, width)
    mixed = both_ways(mixed)
    return group + low_back(jnp.einsum('gtd,de->gte', mixed, out_weight, precision=HIGH))

def reference(tokens, cotangent, norm1_gain, qkv_weight, out_weight, norm2_gain, router_weight, up_weight, down_weight, routes, capacity):
    devices_all = TOKENS // TOK_DEV
    route_blocks = routes.reshape(devices_all, TOK_DEV)
    onehot = (route_blocks[..., None] == jnp.arange(EXPERTS, dtype=jnp.int32)).astype(jnp.int32)
    position = lax.optimization_barrier(jnp.sum((jnp.cumsum(onehot, 1) - 1) * onehot, -1)).astype(jnp.int32)
    kept_blocks = position < capacity[route_blocks]
    token_ids = jnp.arange(TOKENS, dtype=jnp.int32).reshape(devices_all, TOK_DEV)
    device_ids = jnp.broadcast_to(jnp.arange(devices_all, dtype=jnp.int32)[:, None], (devices_all, TOK_DEV))
    table = jnp.zeros((devices_all, EXPERTS, CAP), jnp.int32)
    table = table.at[device_ids, route_blocks, position].set(jnp.where(kept_blocks, token_ids, 0))
    valid = jnp.zeros((devices_all, EXPERTS, CAP), jnp.float32)
    valid = valid.at[device_ids, route_blocks, position].set(kept_blocks.astype(jnp.float32))
    table_t = jnp.transpose(table, (1, 0, 2)).reshape(EXPERTS, devices_all * CAP)
    valid_t = jnp.transpose(valid, (1, 0, 2)).reshape(EXPERTS, devices_all * CAP)
    kept_flat = kept_blocks.reshape(TOKENS).astype(jnp.float32)
    group_size = math.gcd(devices_all, max(1, 4096 // TOK_DEV))

    def forward(inputs, gain_one, w_qkv, w_out, gain_two, w_router, w_up, w_down):

        def one_group(group):
            return attend_group(group, gain_one, w_qkv, w_out)
        grouped = inputs.reshape(devices_all // group_size, group_size, TOK_DEV, D)
        resid = lax.map(jax.checkpoint(one_group), grouped).reshape(TOKENS, D)
        normed = layer_norm(resid, gain_two)
        logits = jnp.dot(normed, w_router, precision=HIGH)
        score = jnp.take_along_axis(logits, routes[:, None], 1)[:, 0]
        gate = jax.nn.sigmoid(score) * kept_flat
        expert_in = low_back(low(normed))

        def one_expert(item):
            index, usable, weight_up, weight_down = item
            rows = expert_in[index]
            upper = low_back(jnp.dot(rows, weight_up, precision=HIGH))
            hidden = low(jax.nn.gelu(upper, approximate=False))
            result = both_ways(jnp.dot(hidden, weight_down, precision=HIGH))
            return result * usable[:, None]
        slots = lax.map(jax.checkpoint(one_expert), (table_t, valid_t, w_up, w_down))
        merged = jnp.zeros((TOKENS, D), jnp.float32).at[table_t.reshape(-1)].add(slots.reshape(-1, D))
        return resid + gate[:, None] * merged
    primals = (tokens.astype(jnp.float32), norm1_gain.astype(jnp.float32), qkv_weight.astype(jnp.float32), out_weight.astype(jnp.float32), norm2_gain.astype(jnp.float32), router_weight.astype(jnp.float32), up_weight.astype(jnp.float32), down_weight.astype(jnp.float32))
    output, pullback = jax.vjp(forward, *primals)
    grads = pullback(cotangent.astype(jnp.float32))
    return (output.astype(jnp.bfloat16), grads[0], grads[1], grads[2], grads[3], grads[4], grads[5], grads[6], grads[7])
```

```python
import functools

import jax
import jax.numpy as jnp
from jax import lax
from jax.experimental import pallas as pl
from jax.experimental.pallas import tpu as pltpu
from jax.sharding import PartitionSpec as P

HEADS = 12
HDIM = 64
EPS = 1e-05
F32 = jnp.float32
BF = jnp.bfloat16
NT = (((1,), (1,)), ((), ()))
TN = (((0,), (0,)), ((), ()))
MIB = 2**20
VMEM = pl.BlockSpec(memory_space=pltpu.VMEM)
SMEM = pl.BlockSpec(memory_space=pltpu.SMEM)
GROUPS = 2


def out(shape, dtype):
    return jax.ShapeDtypeStruct(shape, dtype)


def params(mib=56):
    return pltpu.CompilerParams(vmem_limit_bytes=mib * MIB)


def cost(flops, nbytes):
    return pl.CostEstimate(flops=int(flops), bytes_accessed=int(nbytes), transcendentals=0)


def dot(a, b, dims=None):
    if dims is None:
        return jnp.dot(a, b, preferred_element_type=F32)
    return lax.dot_general(a, b, dims, preferred_element_type=F32)


def norm(value, gain):
    center = value - jnp.mean(value, -1, keepdims=True)
    inverse = lax.rsqrt(jnp.mean(center * center, -1, keepdims=True) + EPS)
    normed = center * inverse
    return normed, inverse, normed * gain


def norm_pull(scaled, normed, inverse):
    return inverse * (
        scaled
        - jnp.mean(scaled, -1, keepdims=True)
        - normed * jnp.mean(scaled * normed, -1, keepdims=True)
    )


def slot_matrix(slot, slots):
    ids = lax.broadcasted_iota(jnp.int32, (slots, slot.shape[1]), 0)
    return jnp.where(ids == slot, 1.0, 0.0).astype(BF)


def plan_body(experts, cap, cap_ref, routes_ref, cot_ref, slot_ref, send_ref):
    tok = routes_ref.shape[1]
    ids = lax.broadcasted_iota(jnp.int32, (experts, tok), 0)
    hot = routes_ref[...] == ids
    limit = jnp.zeros((experts, tok), F32)
    for e in range(experts):
        limit = jnp.where(ids == e, cap_ref[e].astype(F32), limit)
    before = lax.broadcasted_iota(jnp.int32, (tok, tok), 0) < lax.broadcasted_iota(
        jnp.int32, (tok, tok), 1
    )
    position = dot(
        jnp.where(hot, 1.0, 0.0).astype(BF), jnp.where(before, 1.0, 0.0).astype(BF)
    )
    kept = jnp.logical_and(hot, position < limit)
    number = position + (ids * cap).astype(F32) + 1.0
    slot = (jnp.sum(jnp.where(kept, number, 0.0), 0, keepdims=True) - 1.0).astype(jnp.int32)
    slot_ref[...] = slot
    send_ref[...] = dot(slot_matrix(slot, experts * cap), cot_ref[...]).astype(BF)


def plan(routes, capacity, cotangent, experts, cap):
    tok, width = cotangent.shape
    slots = experts * cap
    return pl.pallas_call(
        functools.partial(plan_body, experts, cap),
        in_specs=[SMEM, VMEM, VMEM],
        out_specs=[VMEM, VMEM],
        out_shape=[out((1, tok), jnp.int32), out((slots, width), BF)],
        compiler_params=params(),
        cost_estimate=cost(2 * slots * tok * width, 4 * slots * width),
    )(capacity, routes.reshape(1, tok), cotangent)


def attend_body(
    slots,
    tok_ref,
    gain1_ref,
    wqkv_ref,
    wout_ref,
    gain2_ref,
    slot_ref,
    act_ref,
    qkv_ref,
    mixed_ref,
    lse_ref,
    resid_ref,
    send_ref,
):
    tok, width = tok_ref.shape
    inputs = tok_ref[...].astype(F32)
    act = norm(inputs, gain1_ref[...])[2].astype(BF)
    act_ref[...] = act
    for j in range(3):
        cols = pl.ds(j * width, width)
        qkv_ref[:, cols] = dot(act, wqkv_ref[:, cols]).astype(BF)
    lane = lax.broadcasted_iota(jnp.int32, (1, 128), 1)
    causal = lax.broadcasted_iota(jnp.int32, (tok, tok), 0) >= lax.broadcasted_iota(
        jnp.int32, (tok, tok), 1
    )
    lse = jnp.zeros((tok, 128), F32)
    for p in range(HEADS // 2):
        query = qkv_ref[:, 128 * p : 128 * p + 128] * jnp.asarray(HDIM**-0.5, BF)
        keys = qkv_ref[:, width + 128 * p : width + 128 * p + 128]
        values = qkv_ref[:, 2 * width + 128 * p : 2 * width + 128 * p + 128]
        parts = []
        for h in range(2):
            mine = (lane < HDIM) if h == 0 else (lane >= HDIM)
            scores = dot(jnp.where(mine, query, jnp.zeros_like(query)), keys, NT)
            scores = jnp.where(causal, scores, -1e30)
            top = jnp.max(scores, -1, keepdims=True)
            expo = jnp.exp(scores - top)
            total = jnp.sum(expo, -1, keepdims=True)
            parts.append(dot(expo.astype(BF), values) * (1.0 / total))
            lse = jnp.where(lane == 2 * p + h, top + jnp.log(total), lse)
        mixed_ref[:, 128 * p : 128 * p + 128] = jnp.where(lane < HDIM, *parts).astype(BF)
    lse_ref[...] = lse
    resid = inputs + dot(mixed_ref[...], wout_ref[...])
    resid_ref[...] = resid
    rows = norm(resid, gain2_ref[...])[2].astype(BF)
    send_ref[...] = dot(slot_matrix(slot_ref[...], slots), rows).astype(BF)


def attend(tokens, gain1, wqkv, wout, gain2, slot, slots):
    tok, width = tokens.shape
    return pl.pallas_call(
        functools.partial(attend_body, slots),
        in_specs=[VMEM] * 6,
        out_specs=[VMEM] * 6,
        out_shape=[
            out((tok, width), BF),
            out((tok, 3 * width), BF),
            out((tok, width), BF),
            out((tok, 128), F32),
            out((tok, width), F32),
            out((slots, width), BF),
        ],
        compiler_params=params(),
        cost_estimate=cost(12e9, 12e6),
    )(tokens, gain1, wqkv, wout, gain2, slot)


def expert_body(
    steps,
    rows_ref,
    cot_ref,
    router_ref,
    up_ref,
    down_ref,
    out_ref,
    back_ref,
    hid_ref,
    du_ref,
    dy_ref,
    dscore_ref,
    sum_ref,
    grad_ref,
    gate_ref,
):
    step = pl.program_id(0)

    @pl.when(step == 0)
    def _():
        score = jnp.sum(rows_ref[...].astype(F32) * router_ref[...], -1, keepdims=True)
        gate = jax.nn.sigmoid(score)
        gate_ref[...] = gate
        dy_ref[...] = (cot_ref[...].astype(F32) * gate).astype(BF)

    upper = dot(rows_ref[...], up_ref[...])
    hidden_grad = dot(dy_ref[...], down_ref[...], NT)
    cdf = 0.5 + 0.5 * lax.erf(upper * 0.7071067811865476)
    density = jnp.exp(-0.5 * upper * upper) * 0.3989422804014327
    hidden = (upper * cdf).astype(BF)
    upper_grad = (hidden_grad * (cdf + upper * density)).astype(BF)
    hid_ref[...] = hidden
    du_ref[...] = upper_grad
    part = dot(hidden, down_ref[...])
    part_grad = dot(upper_grad, up_ref[...], NT)

    @pl.when(step == 0)
    def _():
        sum_ref[...] = part
        grad_ref[...] = part_grad

    @pl.when(step > 0)
    def _():
        sum_ref[...] += part
        grad_ref[...] += part_grad

    @pl.when(step == steps - 1)
    def _():
        gate = gate_ref[...]
        gated = sum_ref[...] * gate
        out_ref[...] = gated.astype(BF)
        dscore = jnp.sum(cot_ref[...].astype(F32) * gated, -1, keepdims=True) * (1.0 - gate)
        back_ref[...] = (grad_ref[...] + dscore * router_ref[...]).astype(BF)
        dscore_ref[...] = jnp.broadcast_to(dscore, dscore_ref.shape)


def expert(rows, cot, router, up, down):
    count, width = rows.shape
    hidden = up.shape[1]
    tile = 768
    steps = hidden // tile
    whole = lambda *s: pl.BlockSpec(s, lambda f: (0, 0))
    cols = pl.BlockSpec((count, tile), lambda f: (0, f))
    return pl.pallas_call(
        functools.partial(expert_body, steps),
        grid=(steps,),
        in_specs=[
            whole(count, width),
            whole(count, width),
            whole(1, width),
            pl.BlockSpec((width, tile), lambda f: (0, f)),
            pl.BlockSpec((tile, width), lambda f: (f, 0)),
        ],
        out_specs=[
            whole(count, width),
            whole(count, width),
            cols,
            cols,
            whole(count, width),
            whole(count, 128),
        ],
        out_shape=[
            out((count, width), BF),
            out((count, width), BF),
            out((count, hidden), BF),
            out((count, hidden), BF),
            out((count, width), BF),
            out((count, 128), F32),
        ],
        scratch_shapes=[
            pltpu.VMEM((count, width), F32),
            pltpu.VMEM((count, width), F32),
            pltpu.VMEM((count, 1), F32),
        ],
        compiler_params=params(),
        cost_estimate=cost(8 * count * width * hidden, 10 * width * hidden),
    )(rows, cot, router, up, down)


def expert_grads_body(ids_ref, rows_ref, du_ref, hid_ref, dy_ref, up_ref, down_ref):
    up_ref[0] = dot(rows_ref[...], du_ref[...], TN).astype(BF)
    down_ref[0] = dot(hid_ref[...], dy_ref[...], TN).astype(BF)


def expert_grads(rows, du, hid, dy, ids, other, ny):
    count, width = rows.shape
    hidden = du.shape[1]
    part = hidden // (2 * ny)

    def chunk(j, ids):
        return jnp.bitwise_xor(j, ids[0]) * 2 + jnp.bitwise_xor(other, ids[1])

    whole = pl.BlockSpec((count, width), lambda j, ids: (0, 0))
    cols = pl.BlockSpec((count, part), lambda j, ids: (0, chunk(j, ids)))
    return pl.pallas_call(
        expert_grads_body,
        grid_spec=pltpu.PrefetchScalarGridSpec(
            num_scalar_prefetch=1,
            grid=(ny,),
            in_specs=[whole, cols, cols, whole],
            out_specs=[
                pl.BlockSpec((1, width, part), lambda j, ids: (j, 0, 0)),
                pl.BlockSpec((1, part, width), lambda j, ids: (j, 0, 0)),
            ],
        ),
        out_shape=[out((ny, width, part), BF), out((ny, part, width), BF)],
        compiler_params=params(),
        cost_estimate=cost(2 * count * width * hidden, 6 * count * hidden),
    )(ids, rows, du, hid, dy)


def combine_body(slot_ref, resid_ref, rows_ref, out_ref):
    select = slot_matrix(slot_ref[...], rows_ref.shape[0])
    out_ref[...] = (resid_ref[...] + dot(select, rows_ref[...], TN)).astype(BF)


def combine(slot, resid, rows):
    return pl.pallas_call(
        combine_body,
        in_specs=[VMEM] * 3,
        out_specs=VMEM,
        out_shape=out(resid.shape, BF),
        compiler_params=params(),
        cost_estimate=cost(2 * rows.size * resid.shape[0], 4 * rows.size),
    )(slot, resid, rows)


def spread_rows(full, ids_ref, own_ref, send_ref):
    ny, rows = own_ref.shape[:2]
    for y in range(ny):
        first = full[2 * y * rows : (2 * y + 1) * rows]
        second = full[(2 * y + 1) * rows : (2 * y + 2) * rows]
        away = jnp.bitwise_xor(y, ids_ref[0])
        own_ref[away] = jnp.where(ids_ref[1] == 0, first, second)
        send_ref[away] = jnp.where(ids_ref[1] == 0, second, first)


def back_out_body(
    ids_ref,
    back_ref,
    slot_ref,
    resid_ref,
    cot_ref,
    gain_ref,
    wout_ref,
    mixed_ref,
    router_ref,
    dresid_ref,
    dmixed_ref,
    own_ref,
    send_ref,
):
    slots, width = back_ref.shape
    grad = dot(slot_matrix(slot_ref[...], slots), back_ref[...], TN)
    gain = gain_ref[...]
    normed, inverse, _ = norm(resid_ref[...], gain)
    gain_grad = jnp.sum(grad * normed, 0, keepdims=True)
    dresid = cot_ref[...].astype(F32) + norm_pull(grad * gain, normed, inverse)
    dresid_ref[...] = dresid
    low = dresid.astype(BF)
    dmixed_ref[...] = dot(low, wout_ref[...], NT).astype(BF)
    weight_grad = dot(mixed_ref[...], low, TN)
    lane = lax.broadcasted_iota(jnp.int32, (width, 128), 1)
    column = jnp.transpose(jnp.broadcast_to(gain_grad, (128, width)))
    extra = jnp.where(lane == 0, column, router_ref[...])
    full = jnp.concatenate([weight_grad, extra], 1).astype(BF)
    spread_rows(full, ids_ref, own_ref, send_ref)


def back_out(ids, back, slot, resid, cot, gain, wout, mixed, router, ny):
    tok, width = cot.shape
    half = out((ny, width // (2 * ny), width + 128), BF)
    return pl.pallas_call(
        back_out_body,
        in_specs=[SMEM] + [VMEM] * 8,
        out_specs=[VMEM] * 4,
        out_shape=[out((tok, width), F32), out((tok, width), BF), half, half],
        compiler_params=params(),
        cost_estimate=cost(8e9, 8e6),
    )(ids, back, slot, resid, cot, gain, wout, mixed, router)


def back_heads_body(
    first,
    ids_ref,
    query_ref,
    key_ref,
    value_ref,
    dmixed_ref,
    mixed_ref,
    lse_ref,
    act_ref,
    dqkv_ref,
    own_ref,
    send_ref,
):
    tok, width = query_ref.shape
    pairs = width // 128
    lane = lax.broadcasted_iota(jnp.int32, (1, 128), 1)
    causal = lax.broadcasted_iota(jnp.int32, (tok, tok), 1) >= lax.broadcasted_iota(
        jnp.int32, (tok, tok), 0
    )
    lse = jnp.transpose(lse_ref[...])
    shift = jnp.zeros((tok, 128), F32)
    for p in range(pairs):
        cols = slice(128 * p, 128 * p + 128)
        product = dmixed_ref[:, cols].astype(F32) * mixed_ref[:, cols].astype(F32)
        for h in range(2):
            mine = (lane < HDIM) if h == 0 else (lane >= HDIM)
            total = jnp.sum(jnp.where(mine, product, 0.0), -1, keepdims=True)
            shift = jnp.where(lane == 2 * p + h, total, shift)
    shift = jnp.transpose(shift)
    for p in range(pairs):
        cols = slice(128 * p, 128 * p + 128)
        query = query_ref[:, cols] * jnp.asarray(HDIM**-0.5, BF)
        keys, values, dmixed = key_ref[:, cols], value_ref[:, cols], dmixed_ref[:, cols]
        dquery, dkeys, dvalues = [], [], []
        for h in range(2):
            mine = (lane < HDIM) if h == 0 else (lane >= HDIM)
            own_keys = jnp.where(mine, keys, jnp.zeros_like(keys))
            own_values = jnp.where(mine, values, jnp.zeros_like(values))
            i = 2 * p + h
            scores = dot(own_keys, query, NT)
            probs = jnp.where(causal, jnp.exp(scores - lse[first + i : first + i + 1]), 0.0)
            dprobs = dot(own_values, dmixed, NT)
            dscores = (probs * (dprobs - shift[i : i + 1])).astype(BF)
            dvalues.append(dot(probs.astype(BF), dmixed))
            dkeys.append(dot(dscores, query))
            dquery.append(dot(dscores, keys, TN))
        dquery = jnp.where(lane < HDIM, *dquery) * HDIM**-0.5
        parts = (dquery, jnp.where(lane < HDIM, *dkeys), jnp.where(lane < HDIM, *dvalues))
        for j, part in enumerate(parts):
            start = j * width + 128 * p
            dqkv_ref[:, start : start + 128] = part.astype(BF)
    full = dot(act_ref[...], dqkv_ref[...], TN).astype(BF)
    spread_rows(full, ids_ref, own_ref, send_ref)


def back_heads(group, ids, qkv, dmixed, mixed, lse, act, ny):
    tok, width = act.shape
    cols = width // GROUPS
    block = lambda j: pl.BlockSpec((tok, cols), lambda i: (0, j))
    whole = lambda *s: pl.BlockSpec(s, lambda i: (0,) * len(s))
    half = (ny, width // (2 * ny), 3 * cols)
    return pl.pallas_call(
        functools.partial(back_heads_body, group * HEADS // GROUPS),
        grid=(1,),
        in_specs=[
            SMEM,
            block(group),
            block(GROUPS + group),
            block(2 * GROUPS + group),
            block(group),
            block(group),
            whole(tok, 128),
            whole(tok, width),
        ],
        out_specs=[whole(tok, 3 * cols), whole(*half), whole(*half)],
        out_shape=[out((tok, 3 * cols), BF), out(half, BF), out(half, BF)],
        compiler_params=params(),
        cost_estimate=cost(18e9 / GROUPS, 10e6 / GROUPS),
    )(ids, qkv, qkv, qkv, dmixed, mixed, lse, act)


def back_in_body(dqkv_refs, wqkv_ref, tok_ref, gain_ref, dresid_ref, out_ref):
    tok, width = tok_ref.shape
    cols = width // GROUPS
    grad = jnp.zeros((tok, width), F32)
    for g, ref in enumerate(dqkv_refs):
        for j in range(3):
            start = j * width + g * cols
            grad += dot(ref[:, j * cols : (j + 1) * cols], wqkv_ref[:, start : start + cols], NT)
    gain = gain_ref[...]
    normed, inverse, _ = norm(tok_ref[...].astype(F32), gain)
    out_ref[...] = dresid_ref[...] + norm_pull(grad * gain, normed, inverse)


def back_in(dqkv, wqkv, tokens, gain, dresid):
    def body(*refs):
        back_in_body(refs[:GROUPS], *refs[GROUPS:])

    return pl.pallas_call(
        body,
        in_specs=[VMEM] * (GROUPS + 4),
        out_specs=VMEM,
        out_shape=out(tokens.shape, F32),
        compiler_params=params(),
        cost_estimate=cost(4e9, 10e6),
    )(*dqkv, wqkv, tokens, gain, dresid)


def per_device(
    sizes,
    tokens,
    cotangent,
    norm1_gain,
    qkv_weight,
    out_weight,
    norm2_gain,
    router_weight,
    up_weight,
    down_weight,
    routes,
    capacity,
):
    n_dp, n_ex = sizes
    ny = n_dp // 2
    tok, width = tokens.shape
    experts = router_weight.shape[1]
    cap = 3 * tok // (2 * experts)
    slots = experts * cap
    dp = lax.axis_index("dp")
    ex = lax.axis_index("expert")
    ids = jnp.stack([dp // 2, dp % 2]).astype(jnp.int32)
    gain1, gain2 = norm1_gain.reshape(1, width), norm2_gain.reshape(1, width)
    router = lax.dynamic_slice(router_weight, (0, ex), (width, 1)).reshape(1, width)
    up, down = up_weight[0], down_weight[0]

    def exchange(value):
        return lax.all_to_all(value, "expert", split_axis=0, concat_axis=0, tiled=True)

    def to_core(value):
        return lax.ppermute(value, "dp", [(i, i ^ 1) for i in range(n_dp)])

    def to_y(value, away):
        return lax.ppermute(value, "dp", [(i, i ^ (2 * away)) for i in range(n_dp)])

    def sum_y(own, received):
        far = [
            to_y((own[j].astype(F32) + received[j].astype(F32)).astype(BF), j)
            for j in range(1, ny)
        ]
        total = own[0].astype(F32) + received[0].astype(F32)
        for part in far:
            total = total + part.astype(F32)
        return total

    def reduce_rows(own, send):
        total = sum_y(own, to_core(send)).astype(BF)
        rows, cols = total.shape
        return jnp.sum(exchange(total).reshape(n_ex, rows // n_ex, cols).astype(F32), 0)

    slot, cot_send = plan(routes, capacity, cotangent, experts, cap)
    cot_rows = exchange(cot_send)
    act, qkv, mixed, lse, resid, send = attend(
        tokens, gain1, qkv_weight, out_weight, gain2, slot, slots
    )
    rows = exchange(send)
    gated, back, hid, du, dy, dscore = expert(rows, cot_rows, router, up, down)
    back = exchange(back)
    gated = exchange(gated)

    up_send, down_send = expert_grads(rows, du, hid, dy, ids, 1, ny)
    up_own, down_own = expert_grads(rows, du, hid, dy, ids, 0, ny)
    up_grad = sum_y(up_own, to_core(up_send))
    down_grad = sum_y(down_own, to_core(down_send))
    lanes = jnp.arange(128, dtype=jnp.int32)[None, :]
    router_part = dot(
        rows, jnp.where(lanes == ex + 1, dscore, 0.0).astype(BF), TN
    )

    dresid, dmixed, own, sent = back_out(
        ids, back, slot, resid, cotangent, gain2, out_weight, mixed, router_part, ny
    )
    out_all = reduce_rows(own, sent)
    dqkv, qkv_all = [], []
    for group in range(GROUPS):
        part, own, sent = back_heads(group, ids, qkv, dmixed, mixed, lse, act, ny)
        dqkv.append(part)
        qkv_all.append(reduce_rows(own, sent))
    tokens_grad = back_in(dqkv, qkv_weight, tokens, gain1, dresid)
    block_out = combine(slot, resid, gated)

    cols = width // GROUPS
    qkv_grad = jnp.concatenate(
        [part[:, j * cols : (j + 1) * cols] for j in range(3) for part in qkv_all], 1
    )
    rows_dev = width // (n_dp * n_ex)
    start = (dp * n_ex + ex) * rows_dev
    weight_rows = lax.dynamic_slice(qkv_weight, (start, 0), (rows_dev, 3 * width)).astype(F32)
    gain1_grad = jnp.sum(weight_rows * qkv_grad, 1) / lax.dynamic_slice(
        norm1_gain, (start,), (rows_dev,)
    )
    return (
        block_out,
        tokens_grad,
        gain1_grad,
        qkv_grad,
        out_all[:, :width],
        out_all[:, width],
        out_all[:, width + 1 : width + 1 + experts],
        up_grad[None],
        down_grad[None],
    )


def solution(mesh):
    sizes = (mesh.shape["dp"], mesh.shape["expert"])
    return jax.shard_map(
        functools.partial(per_device, sizes),
        mesh=mesh,
        in_specs=(
            P(("dp", "expert"), None),
            P(("dp", "expert"), None),
            P(),
            P(),
            P(),
            P(),
            P(),
            P("expert", None, None),
            P("expert", None, None),
            P(("dp", "expert")),
            P(),
        ),
        out_specs=(
            P(("dp", "expert"), None),
            P(("dp", "expert"), None),
            P(("dp", "expert")),
            P(("dp", "expert"), None),
            P(("dp", "expert"), None),
            P(("dp", "expert")),
            P(("dp", "expert"), None),
            P("expert", None, "dp"),
            P("expert", "dp", None),
        ),
        check_vma=False,
    )
```

```python
import functools

import jax
import jax.numpy as jnp
from jax import lax
from jax.experimental import pallas as pl
from jax.experimental.pallas import tpu as pltpu
from jax.sharding import PartitionSpec as P

HEADS = 12
HDIM = 64
EPS = 1e-05
F32 = jnp.float32
BF = jnp.bfloat16
NT = (((1,), (1,)), ((), ()))
TN = (((0,), (0,)), ((), ()))
MIB = 2**20
VMEM = pl.BlockSpec(memory_space=pltpu.VMEM)
SMEM = pl.BlockSpec(memory_space=pltpu.SMEM)
GROUPS = 2
SCALE = 1
LIMIT = 56
ANY = pl.BlockSpec(memory_space=pl.ANY)


def out(shape, dtype):
    return jax.ShapeDtypeStruct(shape, dtype)


def params(mib=LIMIT):
    return pltpu.CompilerParams(vmem_limit_bytes=mib * MIB)


def cost(flops, nbytes):
    return pl.CostEstimate(
        flops=int(flops / SCALE), bytes_accessed=int(nbytes / SCALE), transcendentals=0
    )


def dot(a, b, dims=None):
    if dims is None:
        return jnp.dot(a, b, preferred_element_type=F32)
    return lax.dot_general(a, b, dims, preferred_element_type=F32)


def norm(value, gain):
    center = value - jnp.mean(value, -1, keepdims=True)
    inverse = lax.rsqrt(jnp.mean(center * center, -1, keepdims=True) + EPS)
    normed = center * inverse
    return normed, inverse, normed * gain


def as_row(ref):
    return ref[...].reshape(1, ref.shape[0])


def norm_pull(scaled, normed, inverse):
    return inverse * (
        scaled
        - jnp.mean(scaled, -1, keepdims=True)
        - normed * jnp.mean(scaled * normed, -1, keepdims=True)
    )


def slot_matrix(slot, slots):
    ids = lax.broadcasted_iota(jnp.int32, (slots, slot.shape[1]), 0)
    return jnp.where(ids == slot, 1.0, 0.0).astype(BF)


def plan_body(cap, cap_ref, routes_ref, cot_ref, slot_ref, send_ref):
    experts = cap_ref.shape[0]
    tok, width = cot_ref.shape
    count = experts * cap
    ids = lax.broadcasted_iota(jnp.int32, (experts, tok), 0)
    hot = routes_ref[...] == ids
    limit = jnp.zeros((experts, tok), F32)
    for e in range(experts):
        limit = jnp.where(ids == e, cap_ref[e].astype(F32), limit)
    before = lax.broadcasted_iota(jnp.int32, (tok, tok), 0) < lax.broadcasted_iota(
        jnp.int32, (tok, tok), 1
    )
    position = dot(
        jnp.where(hot, 1.0, 0.0).astype(BF), jnp.where(before, 1.0, 0.0).astype(BF)
    )
    kept = jnp.logical_and(hot, position < limit)
    number = position + (ids * cap).astype(F32) + 1.0
    number += jnp.where(position < cap, 0.0, float(count - cap))
    slot = (jnp.sum(jnp.where(kept, number, 0.0), 0, keepdims=True) - 1.0).astype(jnp.int32)
    slot_ref[...] = slot
    rows = dot(slot_matrix(slot, 2 * count), cot_ref[...]).astype(BF)
    send_ref[:, :width] = rows[:count]
    send_ref[:, width:] = rows[count:]


def plan(routes, capacity, cotangent, cap):
    tok, width = cotangent.shape
    count = capacity.shape[0] * cap
    return pl.pallas_call(
        functools.partial(plan_body, cap),
        in_specs=[SMEM, VMEM, VMEM],
        out_specs=[VMEM] * 2,
        out_shape=[out((1, tok), jnp.int32), out((count, 2 * width), BF)],
        compiler_params=params(),
        cost_estimate=cost(4 * count * tok * width, 8 * count * width),
    )(capacity, routes.reshape(1, tok), cotangent)


def attend_body(
    tok_ref,
    gain1_ref,
    wqkv_ref,
    wout_ref,
    gain2_ref,
    slot_ref,
    act_ref,
    qkv_ref,
    mixed_ref,
    lse_ref,
    resid_ref,
    first_ref,
    second_ref,
):
    tok, width = tok_ref.shape
    inputs = tok_ref[...].astype(F32)
    act = norm(inputs, as_row(gain1_ref))[2].astype(BF)
    act_ref[...] = act
    for j in range(3):
        cols = pl.ds(j * width, width)
        qkv_ref[:, cols] = dot(act, wqkv_ref[:, cols]).astype(BF)
    lane = lax.broadcasted_iota(jnp.int32, (1, 128), 1)
    causal = lax.broadcasted_iota(jnp.int32, (tok, tok), 0) >= lax.broadcasted_iota(
        jnp.int32, (tok, tok), 1
    )
    lse = jnp.zeros((tok, 128), F32)
    for p in range(HEADS // 2):
        query = qkv_ref[:, 128 * p : 128 * p + 128] * jnp.asarray(HDIM**-0.5, BF)
        keys = qkv_ref[:, width + 128 * p : width + 128 * p + 128]
        values = qkv_ref[:, 2 * width + 128 * p : 2 * width + 128 * p + 128]
        parts = []
        for h in range(2):
            mine = (lane < HDIM) if h == 0 else (lane >= HDIM)
            scores = dot(jnp.where(mine, query, jnp.zeros_like(query)), keys, NT)
            scores = jnp.where(causal, scores, -1e30)
            top = jnp.max(scores, -1, keepdims=True)
            expo = jnp.exp(scores - top)
            total = jnp.sum(expo, -1, keepdims=True)
            parts.append(dot(expo.astype(BF), values) * (1.0 / total))
            lse = jnp.where(lane == 2 * p + h, top + jnp.log(total), lse)
        mixed_ref[:, 128 * p : 128 * p + 128] = jnp.where(lane < HDIM, *parts).astype(BF)
    lse_ref[...] = lse
    resid = inputs + dot(mixed_ref[...], wout_ref[...])
    resid_ref[...] = resid
    rows = norm(resid, as_row(gain2_ref))[2].astype(BF)
    count = first_ref.shape[0]
    send = dot(slot_matrix(slot_ref[...], 2 * count), rows).astype(BF)
    first_ref[...] = send[:count]
    second_ref[...] = send[count:]


def attend(tokens, gain1, wqkv, wout, gain2, slot, count):
    tok, width = tokens.shape
    return pl.pallas_call(
        attend_body,
        in_specs=[VMEM] * 6,
        out_specs=[VMEM] * 7,
        out_shape=[
            out((tok, width), BF),
            out((tok, 3 * width), BF),
            out((tok, width), BF),
            out((tok, 128), F32),
            out((tok, width), F32),
            out((count, width), BF),
            out((count, width), BF),
        ],
        compiler_params=params(),
        cost_estimate=cost(12e9, 12e6),
    )(tokens, gain1, wqkv, wout, gain2, slot)


def turn_body(order_ref, act_ref, mixed_ref, act_turned_ref, mixed_turned_ref):
    order = order_matrix(order_ref)
    act_turned_ref[...] = dot(order, act_ref[...], NT).astype(BF)
    mixed_turned_ref[...] = dot(order, mixed_ref[...], NT).astype(BF)


def order_matrix(order_ref):
    width = order_ref.shape[1]
    ids = lax.broadcasted_iota(jnp.int32, (width, width), 0)
    return jnp.where(ids == order_ref[...], 1.0, 0.0).astype(BF)


def turn(order, act, mixed):
    tok, width = act.shape
    return pl.pallas_call(
        turn_body,
        in_specs=[VMEM] * 3,
        out_specs=[VMEM] * 2,
        out_shape=[out((width, tok), BF)] * 2,
        compiler_params=params(),
        cost_estimate=cost(4 * tok * width * width, 8 * tok * width),
    )(order, act, mixed)


def expert_body(
    steps,
    ids_ref,
    rows_ref,
    cot_ref,
    router_ref,
    up_ref,
    down_ref,
    put,
    hid_ref,
    du_ref,
    rows_turned_ref,
    dy_turned_ref,
    dscore_ref,
    dy_ref,
    sum_ref,
    grad_ref,
    gate_ref,
):
    step = pl.program_id(0)

    @pl.when(step == 0)
    def _():
        score = jnp.sum(rows_ref[...].astype(F32) * router_ref[...], -1, keepdims=True)
        gate = jax.nn.sigmoid(score)
        gate_ref[...] = gate
        dy = (cot_ref[...].astype(F32) * gate).astype(BF)
        dy_ref[...] = dy
        rows_turned_ref[...] = jnp.transpose(rows_ref[...])
        dy_turned_ref[...] = jnp.transpose(dy)

    upper = dot(rows_ref[...], up_ref[...])
    hidden_grad = dot(dy_ref[...], down_ref[...], NT)
    cdf = 0.5 + 0.5 * lax.erf(upper * 0.7071067811865476)
    density = jnp.exp(-0.5 * upper * upper) * 0.3989422804014327
    hidden = (upper * cdf).astype(BF)
    upper_grad = (hidden_grad * (cdf + upper * density)).astype(BF)
    hid_ref[...] = hidden
    du_ref[...] = upper_grad
    part = dot(hidden, down_ref[...])
    part_grad = dot(upper_grad, up_ref[...], NT)

    @pl.when(step == 0)
    def _():
        sum_ref[...] = part
        grad_ref[...] = part_grad

    @pl.when(step > 0)
    def _():
        sum_ref[...] += part
        grad_ref[...] += part_grad

    @pl.when(step == steps - 1)
    def _():
        gate = gate_ref[...]
        gated = sum_ref[...] * gate
        dscore = jnp.sum(cot_ref[...].astype(F32) * gated, -1, keepdims=True) * (1.0 - gate)
        put(grad_ref[...] + dscore * router_ref[...], gated)
        lane = lax.broadcasted_iota(jnp.int32, dscore_ref.shape, 1)
        dscore_ref[...] = jnp.where(lane == ids_ref[2] + 1, dscore, 0.0).astype(BF)


def batch_body(first, steps, *refs):
    *ins, back_ref, gated_ref = refs[: (8 if first else 14)]

    def put(back, gated):
        back_ref[...] = back.astype(BF)
        gated_ref[...] = gated.astype(BF)

    expert_body(steps, *ins[:6], put, *refs[8 if first else 14 :])


def expert(ids, rows, cots, router, up, down, kept):
    i = 0 if kept is None else 1
    width, hidden = up.shape
    tile = 768
    steps = hidden // tile
    count = rows.shape[0]
    whole = lambda *s: pl.BlockSpec(s, lambda f: (0,) * len(s))
    side = pl.BlockSpec((count, width), lambda f: (0, i))
    tiles = pl.BlockSpec((count, tile), lambda f: (i, f))
    turned = pl.BlockSpec((width, count), lambda f: (0, i))
    return pl.pallas_call(
        functools.partial(batch_body, kept is None, steps),
        grid=(steps,),
        in_specs=[
            SMEM,
            whole(count, width),
            side,
            whole(1, width),
            pl.BlockSpec((width, tile), lambda f: (0, f)),
            pl.BlockSpec((tile, width), lambda f: (f, 0)),
        ]
        + [ANY] * (6 * i),
        out_specs=[
            whole(count, width),
            side,
            tiles,
            tiles,
            turned,
            turned,
            pl.BlockSpec((count, 128), lambda f: (i, 0)),
        ],
        out_shape=[
            out((count, width), BF),
            out((count, 2 * width), BF),
            out((2 * count, hidden), BF),
            out((2 * count, hidden), BF),
            out((width, 2 * count), BF),
            out((width, 2 * count), BF),
            out((2 * count, 128), BF),
        ],
        scratch_shapes=[
            pltpu.VMEM((count, width), BF),
            pltpu.VMEM((count, width), F32),
            pltpu.VMEM((count, width), F32),
            pltpu.VMEM((count, 1), F32),
        ],
        input_output_aliases={6 + j: 1 + j for j in range(6 * i)},
        compiler_params=params(),
        cost_estimate=cost(8 * count * width * hidden, 10 * width * hidden),
    )(ids, rows, cots, router, up, down, *(kept or ()))


def expert_grads_body(ids_ref, turned_ref, du_ref, hid_ref, dy_ref, _, grad_ref):
    grad_ref[0, 0] = dot(turned_ref[...], du_ref[...]).astype(BF)
    grad_ref[0, 1] = dot(dy_ref[...], hid_ref[...]).astype(BF)


def expert_grads(kept, ids, other, first, number, ny, after):
    hid, du, rows, dy, _ = kept
    count, hidden = hid.shape
    width = rows.shape[0]
    part = hidden // (2 * ny)

    def chunk(j, ids):
        return jnp.bitwise_xor(j + first, ids[0]) * 2 + jnp.bitwise_xor(other, ids[1])

    whole = lambda *s: pl.BlockSpec(s, lambda j, ids: (0, 0))
    cols = pl.BlockSpec((count, part), lambda j, ids: (0, chunk(j, ids)))
    return pl.pallas_call(
        expert_grads_body,
        grid_spec=pltpu.PrefetchScalarGridSpec(
            num_scalar_prefetch=1,
            grid=(number,),
            in_specs=[whole(width, count), cols, cols, whole(width, count), ANY],
            out_specs=pl.BlockSpec((1, 2, width, part), lambda j, ids: (j, 0, 0, 0)),
        ),
        out_shape=out((number, 2, width, part), BF),
        compiler_params=params(),
        cost_estimate=cost(1e6, 1e5),
    )(ids, rows, du, hid, dy, after)


def near_pair_body(ids_ref, turned_ref, du_ref, hid_ref, dy_ref, _, send_ref, own_ref):
    up = dot(turned_ref[...], du_ref[...]).astype(BF)
    down = dot(dy_ref[...], hid_ref[...]).astype(BF)

    @pl.when(pl.program_id(0) == 0)
    def _():
        send_ref[0] = up
        send_ref[1] = down

    @pl.when(pl.program_id(0) == 1)
    def _():
        own_ref[0] = up
        own_ref[1] = down


def near_pair(kept, ids, ny, after):
    hid, du, rows, dy, _ = kept
    count, hidden = hid.shape
    width = rows.shape[0]
    part = hidden // (2 * ny)
    whole = lambda *s: pl.BlockSpec(s, lambda j, ids: (0,) * len(s))
    cols = pl.BlockSpec(
        (count, part), lambda j, ids: (0, ids[0] * 2 + jnp.bitwise_xor(1 - j, ids[1]))
    )
    return pl.pallas_call(
        near_pair_body,
        grid_spec=pltpu.PrefetchScalarGridSpec(
            num_scalar_prefetch=1,
            grid=(2,),
            in_specs=[whole(width, count), cols, cols, whole(width, count), ANY],
            out_specs=[whole(2, width, part)] * 2,
        ),
        out_shape=[out((2, width, part), BF)] * 2,
        compiler_params=params(),
        cost_estimate=cost(5e9, 5e6),
    )(ids, rows, du, hid, dy, after)


def far_grads_body(own_ref, received_ref, _, out_ref):
    out_ref[...] = (own_ref[...].astype(F32) + received_ref[...].astype(F32)).astype(BF)


def far_grads(own, received, after):
    number, _, width, part = own.shape
    tall = width // 2
    block = pl.BlockSpec((1, 2, tall, part), lambda j, r: (j, 0, r, 0))
    return pl.pallas_call(
        far_grads_body,
        grid=(number, 2),
        in_specs=[block, block, ANY],
        out_specs=block,
        out_shape=out(own.shape, BF),
        compiler_params=params(),
        cost_estimate=cost(1e6, 1e5),
    )(own, received, after)


def near_grads_body(own_ref, received_ref, *refs):
    parts, (_, up_ref, down_ref) = refs[:-3], refs[-3:]
    total = own_ref[...].astype(F32) + received_ref[...].astype(F32)
    for ref in parts:
        total = total + ref[...].astype(F32)
    up_ref[...] = total[0]
    down_ref[...] = jnp.transpose(total[1])


def near_grads(own, received, parts, after):
    _, width, part = own.shape
    tall = 384
    block = pl.BlockSpec((2, tall, part), lambda j: (0, j, 0))
    return pl.pallas_call(
        near_grads_body,
        grid=(width // tall,),
        in_specs=[block] * (2 + len(parts)) + [ANY],
        out_specs=[
            pl.BlockSpec((tall, part), lambda j: (j, 0)),
            pl.BlockSpec((part, tall), lambda j: (0, j)),
        ],
        out_shape=[out((width, part), F32), out((part, width), F32)],
        compiler_params=params(),
        cost_estimate=cost(own.size, 3 * own.size),
    )(own, received, *parts, after)


def gather_rows(slot_ref, first, second):
    count = first.shape[0]
    select = slot_matrix(slot_ref[...], 2 * count)
    return dot(select[:count], first, TN) + dot(select[count:], second, TN)


def combine_body(slot_ref, resid_ref, rows_ref, _, out_ref):
    width = resid_ref.shape[1]
    rows = gather_rows(slot_ref, rows_ref[:, :width], rows_ref[:, width:])
    out_ref[...] = (resid_ref[...] + rows).astype(BF)


def combine(slot, resid, rows, after):
    return pl.pallas_call(
        combine_body,
        in_specs=[VMEM] * 3 + [ANY],
        out_specs=VMEM,
        out_shape=out(resid.shape, BF),
        compiler_params=params(),
        cost_estimate=cost(2 * rows.size * resid.shape[0], 4 * rows.size),
    )(slot, resid, rows, after)


def back_out_body(
    first_ref,
    second_ref,
    slot_ref,
    order_ref,
    resid_ref,
    cot_ref,
    gain_ref,
    wout_ref,
    mixed_ref,
    turned_ref,
    score_ref,
    _,
    dresid_ref,
    dmixed_ref,
    own_ref,
    send_ref,
):
    width = first_ref.shape[1]
    grad = gather_rows(slot_ref, first_ref[...], second_ref[...])
    gain = as_row(gain_ref)
    normed, inverse, _ = norm(resid_ref[...], gain)
    gain_grad = jnp.sum(grad * normed, 0, keepdims=True)
    dresid = cot_ref[...].astype(F32) + norm_pull(grad * gain, normed, inverse)
    dresid_ref[...] = dresid
    low = dresid.astype(BF)
    dmixed_ref[...] = dot(low, wout_ref[...], NT).astype(BF)
    lane = lax.broadcasted_iota(jnp.int32, (width, 128), 1)
    column = jnp.transpose(jnp.broadcast_to(gain_grad, (128, width)))
    router_grad = dot(turned_ref[...], score_ref[...])
    extra = jnp.where(lane == 0, column, router_grad).astype(BF)
    extra = dot(order_matrix(order_ref), extra).astype(BF)
    rows = width // 2
    for ref, part in ((own_ref, slice(0, rows)), (send_ref, slice(rows, width))):
        ref[:, :width] = dot(mixed_ref[part], low).astype(BF)
        ref[:, width:] = extra[part]


def back_out(first, second, slot, order, resid, cot, gain, wout, mixed, turned, score, after):
    tok, width = cot.shape
    half_shape = (width // 2, width + 128)
    return pl.pallas_call(
        back_out_body,
        in_specs=[VMEM] * 11 + [ANY],
        out_specs=[VMEM] * 4,
        out_shape=[
            out((tok, width), F32),
            out((tok, width), BF),
            out(half_shape, BF),
            out(half_shape, BF),
        ],
        compiler_params=params(),
        cost_estimate=cost(30e9, 8e6),
    )(first, second, slot, order, resid, cot, gain, wout, mixed, turned, score, after)


def back_heads_body(
    first,
    query_ref,
    key_ref,
    value_ref,
    dmixed_ref,
    mixed_ref,
    lse_ref,
    act_ref,
    _,
    dqkv_ref,
    own_ref,
    send_ref,
):
    tok, width = query_ref.shape
    pairs = width // 128
    lane = lax.broadcasted_iota(jnp.int32, (1, 128), 1)
    causal = lax.broadcasted_iota(jnp.int32, (tok, tok), 1) >= lax.broadcasted_iota(
        jnp.int32, (tok, tok), 0
    )
    lse = jnp.transpose(lse_ref[...])
    shift = jnp.zeros((tok, 128), F32)
    for p in range(pairs):
        cols = slice(128 * p, 128 * p + 128)
        product = dmixed_ref[:, cols].astype(F32) * mixed_ref[:, cols].astype(F32)
        for h in range(2):
            mine = (lane < HDIM) if h == 0 else (lane >= HDIM)
            total = jnp.sum(jnp.where(mine, product, 0.0), -1, keepdims=True)
            shift = jnp.where(lane == 2 * p + h, total, shift)
    shift = jnp.transpose(shift)
    for p in range(pairs):
        cols = slice(128 * p, 128 * p + 128)
        query = query_ref[:, cols] * jnp.asarray(HDIM**-0.5, BF)
        keys, values, dmixed = key_ref[:, cols], value_ref[:, cols], dmixed_ref[:, cols]
        dquery, dkeys, dvalues = [], [], []
        for h in range(2):
            mine = (lane < HDIM) if h == 0 else (lane >= HDIM)
            own_keys = jnp.where(mine, keys, jnp.zeros_like(keys))
            own_values = jnp.where(mine, values, jnp.zeros_like(values))
            i = 2 * p + h
            scores = dot(own_keys, query, NT)
            probs = jnp.where(causal, jnp.exp(scores - lse[first + i : first + i + 1]), 0.0)
            dprobs = dot(own_values, dmixed, NT)
            dscores = (probs * (dprobs - shift[i : i + 1])).astype(BF)
            dvalues.append(dot(probs.astype(BF), dmixed))
            dkeys.append(dot(dscores, query))
            dquery.append(dot(dscores, keys, TN))
        dquery = jnp.where(lane < HDIM, *dquery) * HDIM**-0.5
        parts = (dquery, jnp.where(lane < HDIM, *dkeys), jnp.where(lane < HDIM, *dvalues))
        for j, part in enumerate(parts):
            start = j * width + 128 * p
            dqkv_ref[:, start : start + 128] = part.astype(BF)
    rows = act_ref.shape[0] // 2
    own_ref[...] = dot(act_ref[:rows], dqkv_ref[...]).astype(BF)
    send_ref[...] = dot(act_ref[rows:], dqkv_ref[...]).astype(BF)


def back_heads(group, qkv, dmixed, mixed, lse, act, after):
    width, tok = act.shape
    cols = width // GROUPS
    block = lambda j: pl.BlockSpec((tok, cols), lambda i: (0, j))
    whole = lambda *s: pl.BlockSpec(s, lambda i: (0,) * len(s))
    half = (width // 2, 3 * cols)
    return pl.pallas_call(
        functools.partial(back_heads_body, group * HEADS // GROUPS),
        grid=(1,),
        in_specs=[
            block(group),
            block(GROUPS + group),
            block(2 * GROUPS + group),
            block(group),
            block(group),
            whole(tok, 128),
            whole(width, tok),
            ANY,
        ],
        out_specs=[whole(tok, 3 * cols), whole(*half), whole(*half)],
        out_shape=[out((tok, 3 * cols), BF), out(half, BF), out(half, BF)],
        compiler_params=params(),
        cost_estimate=cost(9e9 / (1 + group), 5e6 / (1 + group)),
    )(qkv, qkv, qkv, dmixed, mixed, lse, act, after)


def back_in_body(dqkv_refs, wqkv_ref, tok_ref, gain_ref, dresid_ref, _, out_ref):
    tok, width = tok_ref.shape
    cols = width // GROUPS
    grad = jnp.zeros((tok, width), F32)
    for g, ref in enumerate(dqkv_refs):
        for j in range(3):
            start = j * width + g * cols
            grad += dot(ref[:, j * cols : (j + 1) * cols], wqkv_ref[:, start : start + cols], NT)
    gain = as_row(gain_ref)
    normed, inverse, _ = norm(tok_ref[...].astype(F32), gain)
    out_ref[...] = dresid_ref[...] + norm_pull(grad * gain, normed, inverse)


def back_in(dqkv, wqkv, tokens, gain, dresid, after):
    def body(*refs):
        back_in_body(refs[:GROUPS], *refs[GROUPS:])

    return pl.pallas_call(
        body,
        in_specs=[VMEM] * (GROUPS + 4) + [ANY],
        out_specs=VMEM,
        out_shape=out(tokens.shape, F32),
        compiler_params=params(),
        cost_estimate=cost(4e9, 10e6),
    )(*dqkv, wqkv, tokens, gain, dresid, after)


def core_sum_body(number, *refs):
    own_refs, received_refs, (near_ref, far_ref) = refs[:number], refs[number:-2], refs[-2:]
    rows = near_ref.shape[0]
    start = 0
    for own_ref, received_ref in zip(own_refs, received_refs):
        total = (own_ref[...].astype(F32) + received_ref[...].astype(F32)).astype(BF)
        place = slice(start, start + total.shape[1])
        start = place.stop
        near_ref[:, place] = total[:rows]
        far_ref[:, place] = total[rows:]


def core_sum(own, received):
    rows = own[0].shape[0] // 2
    cols = sum(part.shape[1] for part in own)
    return pl.pallas_call(
        functools.partial(core_sum_body, len(own)),
        in_specs=[VMEM] * (2 * len(own)),
        out_specs=[VMEM] * 2,
        out_shape=[out((rows, cols), BF)] * 2,
        compiler_params=params(),
        cost_estimate=cost(rows * cols, rows * cols),
    )(*own, *received)


def pair_sum_body(first_ref, second_ref, _, out_ref):
    out_ref[...] = (first_ref[...].astype(F32) + second_ref[...].astype(F32)).astype(BF)


def pair_sum(first, second, after):
    return pl.pallas_call(
        pair_sum_body,
        in_specs=[VMEM] * 2 + [ANY],
        out_specs=VMEM,
        out_shape=out(first.shape, BF),
        compiler_params=params(),
        cost_estimate=cost(first.size, first.size),
    )(first, second, after)


def z_sum_body(blocks_ref, near_ref, *far_refs):
    near_ref[...] = jnp.sum(blocks_ref[:, 0].astype(F32), 0)
    for j, ref in enumerate(far_refs):
        ref[...] = jnp.sum(blocks_ref[:, j + 1].astype(F32), 0).astype(BF)


def z_sum(blocks):
    _, ny, rows, cols = blocks.shape
    return pl.pallas_call(
        z_sum_body,
        in_specs=[VMEM],
        out_specs=[VMEM] * ny,
        out_shape=[out((rows, cols), F32)] + [out((rows, cols), BF)] * (ny - 1),
        compiler_params=params(),
        cost_estimate=cost(blocks.size, blocks.size),
    )(blocks)


def finish_body(ny, weight_ref, gain_ref, *refs):
    part_refs, refs = refs[: 2 * ny], refs[2 * ny :]
    grad_ref, out_ref, router_ref, gain1_ref, gain2_ref = refs
    rows, width = out_ref.shape
    cols = width // GROUPS
    first, second = (
        sum(ref[...].astype(F32) for ref in part_refs[i : i + ny]) for i in (0, ny)
    )
    out_ref[...] = first[:, :width]
    extra = first[:, width : width + 128]
    router_ref[...] = extra[:, 1 : 1 + router_ref.shape[1]]
    groups = [first[:, width + 128 :], second]
    gain_grad = 0.0
    for g, total in enumerate(groups):
        for j in range(3):
            piece = total[:, j * cols : (j + 1) * cols]
            place = slice((j * GROUPS + g) * cols, (j * GROUPS + g + 1) * cols)
            grad_ref[:, place] = piece
            weight = weight_ref[:, place].astype(F32)
            gain_grad += jnp.sum(piece * weight, -1, keepdims=True)
    lane = lax.broadcasted_iota(jnp.int32, (rows, 128), 1)
    both = jnp.where(lane == 0, extra, gain_grad / gain_ref[...])
    turned = jnp.transpose(both)
    gain2_ref[...] = turned[:1]
    gain1_ref[...] = turned[1:2]


def finish(weight, gain, first, second, experts):
    rows, width = weight.shape
    return pl.pallas_call(
        functools.partial(finish_body, len(first)),
        in_specs=[VMEM] * (2 + len(first) + len(second)),
        out_specs=[VMEM] * 5,
        out_shape=[
            out((rows, width), F32),
            out((rows, width // 3), F32),
            out((rows, experts), F32),
            out((1, rows), F32),
            out((1, rows), F32),
        ],
        compiler_params=params(),
        cost_estimate=cost(first[0].size, 4 * first[0].size),
    )(weight, gain, *first, *second)


def per_device(
    sizes,
    tokens,
    cotangent,
    norm1_gain,
    qkv_weight,
    out_weight,
    norm2_gain,
    router_weight,
    up_weight,
    down_weight,
    routes,
    capacity,
):
    n_dp, n_ex = sizes
    ny = n_dp // 2
    tok, width = tokens.shape
    experts = router_weight.shape[1]
    cap = 3 * tok // (4 * experts)
    dp = lax.axis_index("dp")
    ex = lax.axis_index("expert")
    ids = jnp.stack([dp // 2, dp % 2, ex]).astype(jnp.int32)
    gain1, gain2 = norm1_gain, norm2_gain
    router = lax.dynamic_slice(router_weight, (0, ex), (width, 1)).reshape(1, width)
    up, down = up_weight[0], down_weight[0]
    rows_dev = width // (n_dp * n_ex)
    start = (dp * n_ex + ex) * rows_dev
    weight_rows = lax.dynamic_slice(qkv_weight, (start, 0), (rows_dev, 3 * width))
    gain_rows = lax.dynamic_slice(norm1_gain, (start,), (rows_dev,)).reshape(rows_dev, 1)
    nz = n_ex // 2
    row = jnp.arange(width, dtype=jnp.int32)
    chunk = row // rows_dev
    y, core, z, x = chunk // (2 * n_ex), chunk // n_ex % 2, chunk // 2 % nz, chunk % 2
    order = ((core ^ (dp % 2)) * 2 + (x ^ (ex % 2))) * nz + z
    order = ((order * ny + (y ^ (dp // 2))) * rows_dev + row % rows_dev).reshape(1, width)

    z_groups = [list(range(0, n_ex, 2)), list(range(1, n_ex, 2))]

    def exchange(value):
        return lax.all_to_all(value, "expert", split_axis=0, concat_axis=0, tiled=True)

    def exchange_z(value):
        return lax.all_to_all(
            value, "expert", split_axis=0, concat_axis=0, tiled=True, axis_index_groups=z_groups
        )

    def to_core(value):
        return lax.ppermute(value, "dp", [(i, i ^ 1) for i in range(n_dp)])

    def to_y(values):
        return [
            lax.ppermute(values[j - 1], "dp", [(i, i ^ (2 * j)) for i in range(n_dp)])
            for j in range(1, ny)
        ]

    def sum_core(own, sent):
        near, far = core_sum(own, [to_core(value) for value in sent])
        return near, lax.ppermute(far, "expert", [(i, i ^ 1) for i in range(n_ex)])

    def sum_z(total):
        blocks = exchange_z(total)
        near, *far = z_sum(blocks.reshape(nz, ny, rows_dev, blocks.shape[1]))
        return [near] + to_y(far)

    slot, cots = plan(routes, capacity, cotangent, cap)
    cots = exchange(cots)
    act, qkv, mixed, lse, resid, first, second = attend(
        tokens, gain1, qkv_weight, out_weight, gain2, slot, experts * cap
    )
    first, cots = lax.optimization_barrier((first, cots))
    first = exchange(first)
    act, mixed_turned = turn(order, act, mixed)
    first, order, weight_rows, gain_rows, second, act, mixed_turned, ids = lax.optimization_barrier(
        (first, order, weight_rows, gain_rows, second, act, mixed_turned, ids)
    )
    second = exchange(second)
    first, *kept = expert(ids, first, cots, router, up, down, None)
    first = exchange(first)
    second, gated, *kept = expert(ids, second, cots, router, up, down, kept)
    second = exchange(second)

    far_send = expert_grads(kept, ids, 1, 1, ny - 1, ny, first)
    far_own = expert_grads(kept, ids, 0, 1, ny - 1, ny, far_send)
    second, gated = lax.optimization_barrier((second, gated))
    gated = exchange(gated)

    dresid, dmixed, *out_parts = back_out(
        first,
        second,
        slot,
        order,
        resid,
        cotangent,
        gain2,
        out_weight,
        mixed_turned,
        kept[2],
        kept[4],
        far_own,
    )
    grads_far = far_grads(far_own, to_core(far_send), dresid)
    grads_y = to_y(grads_far)
    part1, own, sent = back_heads(0, qkv, dmixed, mixed, lse, act, grads_far)
    near1, far1 = sum_core([out_parts[0], own], [out_parts[1], sent])
    part2, own, sent = back_heads(1, qkv, dmixed, mixed, lse, act, near1)
    near_send, near_own = near_pair(kept, ids, ny, part2)
    own, near_own = lax.optimization_barrier((own, near_own))
    near2, far2 = sum_core([own], [sent])
    total1, gated = lax.optimization_barrier((pair_sum(near1, far1, near2), gated))
    first = sum_z(total1)
    tokens_grad = back_in([part1, part2], qkv_weight, tokens, gain1, dresid, total1)
    total2, grads_y = lax.optimization_barrier((pair_sum(near2, far2, tokens_grad), grads_y))
    second = sum_z(total2)
    block_out = combine(slot, resid, gated, total2)
    up_grad, down_grad = near_grads(near_own, to_core(near_send), grads_y, first[0])
    qkv_grad, out_grad, router_grad, gain1_grad, gain2_grad = finish(
        weight_rows, gain_rows, first, second, experts
    )
    return (
        block_out,
        tokens_grad,
        gain1_grad[0],
        qkv_grad,
        out_grad,
        gain2_grad[0],
        router_grad,
        up_grad[None],
        down_grad[None],
    )


def solution(mesh):
    sizes = (mesh.shape["dp"], mesh.shape["expert"])
    return jax.shard_map(
        functools.partial(per_device, sizes),
        mesh=mesh,
        in_specs=(
            P(("dp", "expert"), None),
            P(("dp", "expert"), None),
            P(),
            P(),
            P(),
            P(),
            P(),
            P("expert", None, None),
            P("expert", None, None),
            P(("dp", "expert")),
            P(),
        ),
        out_specs=(
            P(("dp", "expert"), None),
            P(("dp", "expert"), None),
            P(("dp", "expert")),
            P(("dp", "expert"), None),
            P(("dp", "expert"), None),
            P(("dp", "expert")),
            P(("dp", "expert"), None),
            P("expert", None, "dp"),
            P("expert", "dp", None),
        ),
        check_vma=False,
    )
```

```python
import functools

import jax
import jax.numpy as jnp
from jax import lax
from jax.experimental import pallas as pl
from jax.experimental.pallas import tpu as pltpu
from jax.sharding import PartitionSpec as P

HEADS = 12
HDIM = 64
EPS = 1e-05
F32 = jnp.float32
BF = jnp.bfloat16
NT = (((1,), (1,)), ((), ()))
TN = (((0,), (0,)), ((), ()))
MIB = 2**20
VMEM = pl.BlockSpec(memory_space=pltpu.VMEM)
SMEM = pl.BlockSpec(memory_space=pltpu.SMEM)
GROUPS = 2
SCALE = 1
LIMIT = 52
ANY = pl.BlockSpec(memory_space=pltpu.HBM)


def out(shape, dtype):
    return jax.ShapeDtypeStruct(shape, dtype)


def params(mib=LIMIT):
    return pltpu.CompilerParams(vmem_limit_bytes=mib * MIB)


def cost(flops, nbytes):
    return pl.CostEstimate(
        flops=int(flops / SCALE), bytes_accessed=int(nbytes / SCALE), transcendentals=0
    )


def dot(a, b, dims=None):
    if dims is None:
        return jnp.dot(a, b, preferred_element_type=F32)
    return lax.dot_general(a, b, dims, preferred_element_type=F32)


def norm(value, gain):
    center = value - jnp.mean(value, -1, keepdims=True)
    inverse = lax.rsqrt(jnp.mean(center * center, -1, keepdims=True) + EPS)
    normed = center * inverse
    return normed, inverse, normed * gain


def as_row(ref):
    return ref[...].reshape(1, ref.shape[0])


def norm_pull(scaled, normed, inverse):
    return inverse * (
        scaled
        - jnp.mean(scaled, -1, keepdims=True)
        - normed * jnp.mean(scaled * normed, -1, keepdims=True)
    )


def slot_matrix(slot, slots):
    ids = lax.broadcasted_iota(jnp.int32, (slots, slot.shape[1]), 0)
    return jnp.where(ids == slot, 1.0, 0.0).astype(BF)


def plan_body(cap, cap_ref, routes_ref, cot_ref, slot_ref, send_ref):
    experts = cap_ref.shape[0]
    tok, width = cot_ref.shape
    count = experts * cap
    ids = lax.broadcasted_iota(jnp.int32, (experts, tok), 0)
    hot = routes_ref[...] == ids
    limit = jnp.zeros((experts, tok), F32)
    for e in range(experts):
        limit = jnp.where(ids == e, cap_ref[e].astype(F32), limit)
    before = lax.broadcasted_iota(jnp.int32, (tok, tok), 0) < lax.broadcasted_iota(
        jnp.int32, (tok, tok), 1
    )
    position = dot(
        jnp.where(hot, 1.0, 0.0).astype(BF), jnp.where(before, 1.0, 0.0).astype(BF)
    )
    kept = jnp.logical_and(hot, position < limit)
    number = position + (ids * cap).astype(F32) + 1.0
    number += jnp.where(position < cap, 0.0, float(count - cap))
    slot = (jnp.sum(jnp.where(kept, number, 0.0), 0, keepdims=True) - 1.0).astype(jnp.int32)
    slot_ref[...] = slot
    rows = dot(slot_matrix(slot, 2 * count), cot_ref[...]).astype(BF)
    send_ref[:, :width] = rows[:count]
    send_ref[:, width:] = rows[count:]


def plan(routes, capacity, cotangent, cap):
    tok, width = cotangent.shape
    count = capacity.shape[0] * cap
    return pl.pallas_call(
        functools.partial(plan_body, cap),
        in_specs=[SMEM, VMEM, VMEM],
        out_specs=[VMEM] * 2,
        out_shape=[out((1, tok), jnp.int32), out((count, 2 * width), BF)],
        compiler_params=params(),
        cost_estimate=cost(4 * count * tok * width, 8 * count * width),
    )(capacity, routes.reshape(1, tok), cotangent)


def attend_body(
    tok_ref,
    gain1_ref,
    wqkv_ref,
    wout_ref,
    gain2_ref,
    slot_ref,
    act_ref,
    qkv_ref,
    mixed_ref,
    lse_ref,
    resid_ref,
    first_ref,
    second_ref,
):
    tok, width = tok_ref.shape
    inputs = tok_ref[...].astype(F32)
    act = norm(inputs, as_row(gain1_ref))[2].astype(BF)
    act_ref[...] = act
    for j in range(3):
        cols = pl.ds(j * width, width)
        qkv_ref[:, cols] = dot(act, wqkv_ref[:, cols]).astype(BF)
    lane = lax.broadcasted_iota(jnp.int32, (1, 128), 1)
    causal = lax.broadcasted_iota(jnp.int32, (tok, tok), 0) >= lax.broadcasted_iota(
        jnp.int32, (tok, tok), 1
    )
    lse = jnp.zeros((tok, 128), F32)
    for p in range(HEADS // 2):
        query = qkv_ref[:, 128 * p : 128 * p + 128] * jnp.asarray(HDIM**-0.5, BF)
        keys = qkv_ref[:, width + 128 * p : width + 128 * p + 128]
        values = qkv_ref[:, 2 * width + 128 * p : 2 * width + 128 * p + 128]
        parts = []
        for h in range(2):
            mine = (lane < HDIM) if h == 0 else (lane >= HDIM)
            scores = dot(jnp.where(mine, query, jnp.zeros_like(query)), keys, NT)
            scores = jnp.where(causal, scores, -1e30)
            top = jnp.max(scores, -1, keepdims=True)
            expo = jnp.exp(scores - top)
            total = jnp.sum(expo, -1, keepdims=True)
            parts.append(dot(expo.astype(BF), values) * (1.0 / total))
            lse = jnp.where(lane == 2 * p + h, top + jnp.log(total), lse)
        mixed_ref[:, 128 * p : 128 * p + 128] = jnp.where(lane < HDIM, *parts).astype(BF)
    lse_ref[...] = lse
    resid = inputs + dot(mixed_ref[...], wout_ref[...])
    resid_ref[...] = resid
    rows = norm(resid, as_row(gain2_ref))[2].astype(BF)
    count = first_ref.shape[0]
    send = dot(slot_matrix(slot_ref[...], 2 * count), rows).astype(BF)
    first_ref[...] = send[:count]
    second_ref[...] = send[count:]


def attend(tokens, gain1, wqkv, wout, gain2, slot, count):
    tok, width = tokens.shape
    return pl.pallas_call(
        attend_body,
        in_specs=[VMEM] * 6,
        out_specs=[VMEM] * 7,
        out_shape=[
            out((tok, width), BF),
            out((tok, 3 * width), BF),
            out((tok, width), BF),
            out((tok, 128), F32),
            out((tok, width), F32),
            out((count, width), BF),
            out((count, width), BF),
        ],
        compiler_params=params(),
        cost_estimate=cost(12e9, 12e6),
    )(tokens, gain1, wqkv, wout, gain2, slot)


def turn_body(order_ref, act_ref, mixed_ref, act_turned_ref, mixed_turned_ref):
    order = order_matrix(order_ref)
    act_turned_ref[...] = dot(order, act_ref[...], NT).astype(BF)
    mixed_turned_ref[...] = dot(order, mixed_ref[...], NT).astype(BF)


def order_matrix(order_ref):
    width = order_ref.shape[1]
    ids = lax.broadcasted_iota(jnp.int32, (width, width), 0)
    return jnp.where(ids == order_ref[...], 1.0, 0.0).astype(BF)


def turn(order, act, mixed):
    tok, width = act.shape
    return pl.pallas_call(
        turn_body,
        in_specs=[VMEM] * 3,
        out_specs=[VMEM] * 2,
        out_shape=[out((width, tok), BF)] * 2,
        compiler_params=params(),
        cost_estimate=cost(4 * tok * width * width, 8 * tok * width),
    )(order, act, mixed)


def expert_body(
    steps,
    ids_ref,
    rows_ref,
    cot_ref,
    router_ref,
    up_ref,
    down_ref,
    put,
    hid_ref,
    du_ref,
    rows_turned_ref,
    dy_turned_ref,
    dscore_ref,
    dy_ref,
    sum_ref,
    grad_ref,
    gate_ref,
):
    step = pl.program_id(0)

    @pl.when(step == 0)
    def _():
        score = jnp.sum(rows_ref[...].astype(F32) * router_ref[...], -1, keepdims=True)
        gate = jax.nn.sigmoid(score)
        gate_ref[...] = gate
        dy = (cot_ref[...].astype(F32) * gate).astype(BF)
        dy_ref[...] = dy
        rows_turned_ref[...] = jnp.transpose(rows_ref[...])
        dy_turned_ref[...] = jnp.transpose(dy)

    upper = dot(rows_ref[...], up_ref[...])
    hidden_grad = dot(dy_ref[...], down_ref[...], NT)
    cdf = 0.5 + 0.5 * lax.erf(upper * 0.7071067811865476)
    density = jnp.exp(-0.5 * upper * upper) * 0.3989422804014327
    hidden = (upper * cdf).astype(BF)
    upper_grad = (hidden_grad * (cdf + upper * density)).astype(BF)
    hid_ref[...] = hidden
    du_ref[...] = upper_grad
    part = dot(hidden, down_ref[...])
    part_grad = dot(upper_grad, up_ref[...], NT)

    @pl.when(step == 0)
    def _():
        sum_ref[...] = part
        grad_ref[...] = part_grad

    @pl.when(step > 0)
    def _():
        sum_ref[...] += part
        grad_ref[...] += part_grad

    @pl.when(step == steps - 1)
    def _():
        gate = gate_ref[...]
        gated = sum_ref[...] * gate
        dscore = jnp.sum(cot_ref[...].astype(F32) * gated, -1, keepdims=True) * (1.0 - gate)
        put(grad_ref[...] + dscore * router_ref[...], gated)
        lane = lax.broadcasted_iota(jnp.int32, dscore_ref.shape, 1)
        dscore_ref[...] = jnp.where(lane == ids_ref[2] + 1, dscore, 0.0).astype(BF)


def batch_body(first, steps, *refs):
    *ins, back_ref, gated_ref = refs[: (8 if first else 14)]

    def put(back, gated):
        back_ref[...] = back.astype(BF)
        gated_ref[...] = gated.astype(BF)

    expert_body(steps, *ins[:6], put, *refs[8 if first else 14 :])


def expert(ids, rows, cots, router, up, down, kept):
    i = 0 if kept is None else 1
    width, hidden = up.shape
    tile = 768
    steps = hidden // tile
    count = rows.shape[0]
    whole = lambda *s: pl.BlockSpec(s, lambda f: (0,) * len(s))
    side = pl.BlockSpec((count, width), lambda f: (0, i))
    tiles = pl.BlockSpec((count, tile), lambda f: (i, f))
    turned = pl.BlockSpec((width, count), lambda f: (0, i))
    return pl.pallas_call(
        functools.partial(batch_body, kept is None, steps),
        grid=(steps,),
        in_specs=[
            SMEM,
            whole(count, width),
            side,
            whole(1, width),
            pl.BlockSpec((width, tile), lambda f: (0, f)),
            pl.BlockSpec((tile, width), lambda f: (f, 0)),
        ]
        + [ANY] * (6 * i),
        out_specs=[
            whole(count, width),
            side,
            tiles,
            tiles,
            turned,
            turned,
            pl.BlockSpec((count, 128), lambda f: (i, 0)),
        ],
        out_shape=[
            out((count, width), BF),
            out((count, 2 * width), BF),
            out((2 * count, hidden), BF),
            out((2 * count, hidden), BF),
            out((width, 2 * count), BF),
            out((width, 2 * count), BF),
            out((2 * count, 128), BF),
        ],
        scratch_shapes=[
            pltpu.VMEM((count, width), BF),
            pltpu.VMEM((count, width), F32),
            pltpu.VMEM((count, width), F32),
            pltpu.VMEM((count, 1), F32),
        ],
        input_output_aliases={6 + j: 1 + j for j in range(6 * i)},
        compiler_params=params(),
        cost_estimate=cost(8 * count * width * hidden, 10 * width * hidden),
    )(ids, rows, cots, router, up, down, *(kept or ()))


def expert_grads_body(ny, ids_ref, turned_ref, du_ref, hid_ref, dy_ref, _, *refs):
    step = pl.program_id(0)
    up = dot(turned_ref[...], du_ref[...]).astype(BF)
    down = dot(dy_ref[...], hid_ref[...]).astype(BF)
    ends = (0, ny - 1, ny, 2 * ny - 1, 2 * ny)
    for ref, start, end in zip(refs, ends, ends[1:]):

        @pl.when(jnp.logical_and(step >= start, step < end))
        def _(ref=ref):
            ref[0, 0] = up
            ref[0, 1] = down


def expert_grads(kept, ids, ny, after):
    hid, du, rows, dy, _ = kept
    count, hidden = hid.shape
    width = rows.shape[0]
    part = hidden // (2 * ny)

    def chunk(s, ids):
        core = jnp.where(s < ny, 1 - ids[1], ids[1])
        away = jnp.where(s < ny, s, s - ny) + 1
        return jnp.bitwise_xor(jnp.where(away == ny, 0, away), ids[0]) * 2 + core

    whole = lambda *shape: pl.BlockSpec(shape, lambda s, ids: (0, 0))
    cols = pl.BlockSpec((count, part), lambda s, ids: (0, chunk(s, ids)))

    def block(start, number):
        return pl.BlockSpec(
            (1, 2, width, part), lambda s, ids: (jnp.clip(s - start, 0, number - 1), 0, 0, 0)
        )

    far, near = out((ny - 1, 2, width, part), BF), out((1, 2, width, part), BF)
    return pl.pallas_call(
        functools.partial(expert_grads_body, ny),
        grid_spec=pltpu.PrefetchScalarGridSpec(
            num_scalar_prefetch=1,
            grid=(2 * ny,),
            in_specs=[whole(width, count), cols, cols, whole(width, count), ANY],
            out_specs=[
                block(0, ny - 1),
                block(ny - 1, 1),
                block(ny, ny - 1),
                block(2 * ny - 1, 1),
            ],
        ),
        out_shape=[far, near, far, near],
        compiler_params=params(),
        cost_estimate=cost(1e6, 1e5),
    )(ids, rows, du, hid, dy, after)


def far_grads_body(own_ref, received_ref, _, out_ref):
    out_ref[...] = (own_ref[...].astype(F32) + received_ref[...].astype(F32)).astype(BF)


def far_grads(own, received, after):
    number, _, width, part = own.shape
    tall = width // 2
    block = pl.BlockSpec((1, 2, tall, part), lambda j, r: (j, 0, r, 0))
    return pl.pallas_call(
        far_grads_body,
        grid=(number, 2),
        in_specs=[block, block, ANY],
        out_specs=block,
        out_shape=out(own.shape, BF),
        compiler_params=params(),
        cost_estimate=cost(1e6, 1e5),
    )(own, received, after)


def near_grads_body(own_ref, received_ref, *refs):
    parts, (_, up_ref, down_ref) = refs[:-3], refs[-3:]
    total = own_ref[0].astype(F32) + received_ref[0].astype(F32)
    for ref in parts:
        total = total + ref[...].astype(F32)
    up_ref[...] = total[0]
    down_ref[...] = jnp.transpose(total[1])


def near_grads(own, received, parts, after):
    _, _, width, part = own.shape
    tall = 384
    first = pl.BlockSpec((1, 2, tall, part), lambda j: (0, 0, j, 0))
    return pl.pallas_call(
        near_grads_body,
        grid=(width // tall,),
        in_specs=[first, first]
        + [pl.BlockSpec((2, tall, part), lambda j: (0, j, 0))] * len(parts)
        + [ANY],
        out_specs=[
            pl.BlockSpec((tall, part), lambda j: (j, 0)),
            pl.BlockSpec((part, tall), lambda j: (0, j)),
        ],
        out_shape=[out((width, part), F32), out((part, width), F32)],
        compiler_params=params(),
        cost_estimate=cost(own.size, 3 * own.size),
    )(own, received, *parts, after)


def gather_rows(slot_ref, first, second):
    count = first.shape[0]
    select = slot_matrix(slot_ref[...], 2 * count)
    return dot(select[:count], first, TN) + dot(select[count:], second, TN)


def combine_body(slot_ref, resid_ref, rows_ref, _, out_ref):
    width = resid_ref.shape[1]
    rows = gather_rows(slot_ref, rows_ref[:, :width], rows_ref[:, width:])
    out_ref[...] = (resid_ref[...] + rows).astype(BF)


def combine(slot, resid, rows, after):
    return pl.pallas_call(
        combine_body,
        in_specs=[VMEM] * 3 + [ANY],
        out_specs=VMEM,
        out_shape=out(resid.shape, BF),
        compiler_params=params(),
        cost_estimate=cost(1e6, 1e5),
    )(slot, resid, rows, after)


def back_out_body(
    first_ref,
    second_ref,
    slot_ref,
    order_ref,
    resid_ref,
    cot_ref,
    gain_ref,
    wout_ref,
    mixed_ref,
    turned_ref,
    score_ref,
    _,
    dresid_ref,
    dmixed_ref,
    own_ref,
    send_ref,
    send_far_ref,
):
    width = first_ref.shape[1]
    grad = gather_rows(slot_ref, first_ref[...], second_ref[...])
    gain = as_row(gain_ref)
    normed, inverse, _ = norm(resid_ref[...], gain)
    gain_grad = jnp.sum(grad * normed, 0, keepdims=True)
    dresid = cot_ref[...].astype(F32) + norm_pull(grad * gain, normed, inverse)
    dresid_ref[...] = dresid
    low = dresid.astype(BF)
    dmixed_ref[...] = dot(low, wout_ref[...], NT).astype(BF)
    lane = lax.broadcasted_iota(jnp.int32, (width, 128), 1)
    column = jnp.transpose(jnp.broadcast_to(gain_grad, (128, width)))
    router_grad = dot(turned_ref[...], score_ref[...])
    extra = jnp.where(lane == 0, column, router_grad).astype(BF)
    extra = dot(order_matrix(order_ref), extra).astype(BF)
    rows = width // 4
    places = [slice(0, 2 * rows), slice(2 * rows, 3 * rows), slice(3 * rows, width)]
    for ref, part in zip((own_ref, send_ref, send_far_ref), places):
        ref[:, :width] = dot(mixed_ref[part], low).astype(BF)
        ref[:, width:] = extra[part]


def back_out(first, second, slot, order, resid, cot, gain, wout, mixed, turned, score, after):
    tok, width = cot.shape
    return pl.pallas_call(
        back_out_body,
        in_specs=[VMEM] * 11 + [ANY],
        out_specs=[VMEM] * 5,
        out_shape=[
            out((tok, width), F32),
            out((tok, width), BF),
            out((width // 2, width + 128), BF),
            out((width // 4, width + 128), BF),
            out((width // 4, width + 128), BF),
        ],
        compiler_params=params(),
        cost_estimate=cost(30e9, 8e6),
    )(first, second, slot, order, resid, cot, gain, wout, mixed, turned, score, after)


def back_heads_body(
    first,
    query_ref,
    key_ref,
    value_ref,
    dmixed_ref,
    mixed_ref,
    lse_ref,
    act_ref,
    _,
    dqkv_ref,
    own_ref,
    send_ref,
    send_far_ref,
):
    tok, width = query_ref.shape
    pairs = width // 128
    lane = lax.broadcasted_iota(jnp.int32, (1, 128), 1)
    causal = lax.broadcasted_iota(jnp.int32, (tok, tok), 1) >= lax.broadcasted_iota(
        jnp.int32, (tok, tok), 0
    )
    lse = jnp.transpose(lse_ref[...])
    shift = jnp.zeros((tok, 128), F32)
    for p in range(pairs):
        cols = slice(128 * p, 128 * p + 128)
        product = dmixed_ref[:, cols].astype(F32) * mixed_ref[:, cols].astype(F32)
        for h in range(2):
            mine = (lane < HDIM) if h == 0 else (lane >= HDIM)
            total = jnp.sum(jnp.where(mine, product, 0.0), -1, keepdims=True)
            shift = jnp.where(lane == 2 * p + h, total, shift)
    shift = jnp.transpose(shift)
    for p in range(pairs):
        cols = slice(128 * p, 128 * p + 128)
        query = query_ref[:, cols] * jnp.asarray(HDIM**-0.5, BF)
        keys, values, dmixed = key_ref[:, cols], value_ref[:, cols], dmixed_ref[:, cols]
        dquery, dkeys, dvalues = [], [], []
        for h in range(2):
            mine = (lane < HDIM) if h == 0 else (lane >= HDIM)
            own_keys = jnp.where(mine, keys, jnp.zeros_like(keys))
            own_values = jnp.where(mine, values, jnp.zeros_like(values))
            i = 2 * p + h
            scores = dot(own_keys, query, NT)
            probs = jnp.where(causal, jnp.exp(scores - lse[first + i : first + i + 1]), 0.0)
            dprobs = dot(own_values, dmixed, NT)
            dscores = (probs * (dprobs - shift[i : i + 1])).astype(BF)
            dvalues.append(dot(probs.astype(BF), dmixed))
            dkeys.append(dot(dscores, query))
            dquery.append(dot(dscores, keys, TN))
        dquery = jnp.where(lane < HDIM, *dquery) * HDIM**-0.5
        parts = (dquery, jnp.where(lane < HDIM, *dkeys), jnp.where(lane < HDIM, *dvalues))
        for j, part in enumerate(parts):
            start = j * width + 128 * p
            dqkv_ref[:, start : start + 128] = part.astype(BF)
    rows = act_ref.shape[0] // 2
    own_ref[...] = dot(act_ref[:rows], dqkv_ref[...]).astype(BF)
    send = dot(act_ref[rows:], dqkv_ref[...]).astype(BF)
    send_ref[...] = send[: rows // 2]
    send_far_ref[...] = send[rows // 2 :]


def back_heads(group, qkv, dmixed, mixed, lse, act, after):
    width, tok = act.shape
    cols = width // GROUPS
    block = lambda j: pl.BlockSpec((tok, cols), lambda i: (0, j))
    whole = lambda *s: pl.BlockSpec(s, lambda i: (0,) * len(s))
    half = (width // 2, 3 * cols)
    quarter = (width // 4, 3 * cols)
    return pl.pallas_call(
        functools.partial(back_heads_body, group * HEADS // GROUPS),
        grid=(1,),
        in_specs=[
            block(group),
            block(GROUPS + group),
            block(2 * GROUPS + group),
            block(group),
            block(group),
            whole(tok, 128),
            whole(width, tok),
            ANY,
        ],
        out_specs=[whole(tok, 3 * cols), whole(*half), whole(*quarter), whole(*quarter)],
        out_shape=[out((tok, 3 * cols), BF), out(half, BF), out(quarter, BF), out(quarter, BF)],
        compiler_params=params(),
        cost_estimate=cost(9e9 if group == 0 else 1e6, 1e5),
    )(qkv, qkv, qkv, dmixed, mixed, lse, act, after)


def back_group(dqkv_ref, weight_refs):
    cols = dqkv_ref.shape[1] // 3
    return sum(
        dot(dqkv_ref[:, j * cols : (j + 1) * cols], ref[...], NT)
        for j, ref in enumerate(weight_refs)
    )


def back_part_body(number, dqkv_ref, first_ref, second_ref, third_ref, *refs):
    *refs, out_ref, near_ref, far_ref = refs
    out_ref[...] = back_group(dqkv_ref, (first_ref, second_ref, third_ref))
    core_sum_body(number, *refs, near_ref, far_ref)


def back_in_body(
    dqkv_ref,
    first_ref,
    second_ref,
    third_ref,
    part_ref,
    tok_ref,
    gain_ref,
    dresid_ref,
    out_ref,
):
    grad = part_ref[...] + back_group(dqkv_ref, (first_ref, second_ref, third_ref))
    gain = as_row(gain_ref)
    normed, inverse, _ = norm(tok_ref[...].astype(F32), gain)
    out_ref[...] = dresid_ref[...] + norm_pull(grad * gain, normed, inverse)


def weight_columns(group, width):
    cols = width // GROUPS
    return [
        pl.BlockSpec((width, cols), lambda i, j=j: (0, j * GROUPS + group)) for j in range(3)
    ]


def back_part(group, dqkv, wqkv, own, received):
    tok = dqkv.shape[0]
    width = wqkv.shape[0]
    whole = lambda *s: pl.BlockSpec(s, lambda i: (0,) * len(s))
    sums = [*own, *[part for parts in received for part in parts]]
    total = (width // 4, sum(part.shape[1] for part in own))
    return pl.pallas_call(
        functools.partial(back_part_body, len(own)),
        grid=(1,),
        in_specs=[whole(*dqkv.shape)]
        + weight_columns(group, width)
        + [whole(*part.shape) for part in sums],
        out_specs=[whole(tok, width), whole(*total), whole(*total)],
        out_shape=[out((tok, width), F32), out(total, BF), out(total, BF)],
        compiler_params=params(),
        cost_estimate=cost(3e9, 5e6),
    )(dqkv, wqkv, wqkv, wqkv, *sums)


def back_in(group, dqkv, wqkv, part, tokens, gain, dresid):
    tok = dqkv.shape[0]
    width = wqkv.shape[0]
    whole = lambda *s: pl.BlockSpec(s, lambda i: (0,) * len(s))
    return pl.pallas_call(
        back_in_body,
        grid=(1,),
        in_specs=[whole(*dqkv.shape)]
        + weight_columns(group, width)
        + [whole(*a.shape) for a in (part, tokens, gain, dresid)],
        out_specs=whole(tok, width),
        out_shape=out((tok, width), F32),
        compiler_params=params(),
        cost_estimate=cost(1e6, 1e5),
    )(dqkv, wqkv, wqkv, wqkv, part, tokens, gain, dresid)


def core_sum_body(number, *refs):
    own_refs, refs = refs[:number], refs[number:]
    near_ref, far_ref = refs[2 * number : 2 * number + 2]
    rows = near_ref.shape[0]
    start = 0
    for i, own_ref in enumerate(own_refs):
        place = slice(start, start + own_ref.shape[1])
        start = place.stop
        for k, ref in enumerate((near_ref, far_ref)):
            own = own_ref[k * rows : (k + 1) * rows].astype(F32)
            ref[:, place] = (own + refs[2 * i + k][...].astype(F32)).astype(BF)


def core_sum(own, received, after):
    rows = own[0].shape[0] // 2
    cols = sum(part.shape[1] for part in own)

    def body(*refs):
        core_sum_body(len(own), *refs[: 3 * len(own)], *refs[3 * len(own) + 1 :])

    return pl.pallas_call(
        body,
        in_specs=[VMEM] * (3 * len(own)) + [ANY],
        out_specs=[VMEM] * 2,
        out_shape=[out((rows, cols), BF)] * 2,
        compiler_params=params(),
        cost_estimate=cost(1e6, 1e5),
    )(*own, *[part for parts in received for part in parts], after)


def pair_sum_body(first_ref, second_ref, _, out_ref):
    out_ref[...] = (first_ref[...].astype(F32) + second_ref[...].astype(F32)).astype(BF)


def pair_sum(first, second, after):
    return pl.pallas_call(
        pair_sum_body,
        in_specs=[VMEM] * 2 + [ANY],
        out_specs=VMEM,
        out_shape=out(first.shape, BF),
        compiler_params=params(),
        cost_estimate=cost(1e6, 1e5),
    )(first, second, after)


def z_sum_body(blocks_ref, _, near_ref, *far_refs):
    near_ref[...] = jnp.sum(blocks_ref[:, 0].astype(F32), 0)
    for j, ref in enumerate(far_refs):
        ref[...] = jnp.sum(blocks_ref[:, j + 1].astype(F32), 0).astype(BF)


def z_sum(blocks, after):
    _, ny, rows, cols = blocks.shape
    return pl.pallas_call(
        z_sum_body,
        in_specs=[VMEM, ANY],
        out_specs=[VMEM] * ny,
        out_shape=[out((rows, cols), F32)] + [out((rows, cols), BF)] * (ny - 1),
        compiler_params=params(),
        cost_estimate=cost(blocks.size, blocks.size),
    )(blocks, after)


def finish_body(ny, weight_ref, gain_ref, *refs):
    part_refs, refs = refs[: 2 * ny], refs[2 * ny :]
    grad_ref, out_ref, router_ref, gain1_ref, gain2_ref = refs
    rows, width = out_ref.shape
    cols = width // GROUPS
    first, second = (
        sum(ref[...].astype(F32) for ref in part_refs[i : i + ny]) for i in (0, ny)
    )
    out_ref[...] = first[:, :width]
    extra = first[:, width : width + 128]
    router_ref[...] = extra[:, 1 : 1 + router_ref.shape[1]]
    groups = [first[:, width + 128 :], second]
    gain_grad = 0.0
    for g, total in enumerate(groups):
        for j in range(3):
            piece = total[:, j * cols : (j + 1) * cols]
            place = slice((j * GROUPS + g) * cols, (j * GROUPS + g + 1) * cols)
            grad_ref[:, place] = piece
            weight = weight_ref[:, place].astype(F32)
            gain_grad += jnp.sum(piece * weight, -1, keepdims=True)
    lane = lax.broadcasted_iota(jnp.int32, (rows, 128), 1)
    both = jnp.where(lane == 0, extra, gain_grad / gain_ref[...])
    turned = jnp.transpose(both)
    gain2_ref[...] = turned[:1]
    gain1_ref[...] = turned[1:2]


def finish(weight, gain, first, second, experts):
    rows, width = weight.shape
    return pl.pallas_call(
        functools.partial(finish_body, len(first)),
        in_specs=[VMEM] * (2 + len(first) + len(second)),
        out_specs=[VMEM] * 5,
        out_shape=[
            out((rows, width), F32),
            out((rows, width // 3), F32),
            out((rows, experts), F32),
            out((1, rows), F32),
            out((1, rows), F32),
        ],
        compiler_params=params(),
        cost_estimate=cost(first[0].size, 4 * first[0].size),
    )(weight, gain, *first, *second)


def per_device(
    sizes,
    tokens,
    cotangent,
    norm1_gain,
    qkv_weight,
    out_weight,
    norm2_gain,
    router_weight,
    up_weight,
    down_weight,
    routes,
    capacity,
):
    n_dp, n_ex = sizes
    ny = n_dp // 2
    tok, width = tokens.shape
    experts = router_weight.shape[1]
    cap = 3 * tok // (4 * experts)
    dp = lax.axis_index("dp")
    ex = lax.axis_index("expert")
    ids = jnp.stack([dp // 2, dp % 2, ex]).astype(jnp.int32)
    gain1, gain2 = norm1_gain, norm2_gain
    router = lax.dynamic_slice(router_weight, (0, ex), (width, 1)).reshape(1, width)
    up, down = up_weight[0], down_weight[0]
    rows_dev = width // (n_dp * n_ex)
    start = (dp * n_ex + ex) * rows_dev
    weight_rows = lax.dynamic_slice(qkv_weight, (start, 0), (rows_dev, 3 * width))
    gain_rows = lax.dynamic_slice(norm1_gain, (start,), (rows_dev,)).reshape(rows_dev, 1)
    nz = n_ex // 2
    row = jnp.arange(width, dtype=jnp.int32)
    chunk = row // rows_dev
    y, core, z, x = chunk // (2 * n_ex), chunk // n_ex % 2, chunk // 2 % nz, chunk % 2
    order = ((core ^ (dp % 2)) * 2 + (x ^ (ex % 2))) * nz + z
    order = ((order * ny + (y ^ (dp // 2))) * rows_dev + row % rows_dev).reshape(1, width)

    z_groups = [list(range(0, n_ex, 2)), list(range(1, n_ex, 2))]

    def exchange(value):
        return lax.all_to_all(value, "expert", split_axis=0, concat_axis=0, tiled=True)

    def exchange_z(value):
        return lax.all_to_all(
            value, "expert", split_axis=0, concat_axis=0, tiled=True, axis_index_groups=z_groups
        )

    def to_core(value):
        return lax.ppermute(value, "dp", [(i, i ^ 1) for i in range(n_dp)])

    def to_y(values):
        return [
            lax.ppermute(values[j - 1], "dp", [(i, i ^ (2 * j)) for i in range(n_dp)])
            for j in range(1, ny)
        ]

    def to_core_all(values):
        return [to_core(value) for value in values]

    def to_x(value):
        return lax.ppermute(value, "expert", [(i, i ^ 1) for i in range(n_ex)])

    def sum_z(blocks, after):
        near, *far = z_sum(blocks.reshape(nz, ny, rows_dev, blocks.shape[1]), after)
        return [near] + to_y(far)

    slot, cots = plan(routes, capacity, cotangent, cap)
    cots = exchange(cots)
    act, qkv, mixed, lse, resid, first, second = attend(
        tokens, gain1, qkv_weight, out_weight, gain2, slot, experts * cap
    )
    first, cots = lax.optimization_barrier((first, cots))
    first = exchange(first)
    act, mixed_turned = turn(order, act, mixed)
    first, order, weight_rows, gain_rows, second, act, mixed_turned, ids = lax.optimization_barrier(
        (first, order, weight_rows, gain_rows, second, act, mixed_turned, ids)
    )
    second = exchange(second)
    first, *kept = expert(ids, first, cots, router, up, down, None)
    first = exchange(first)
    second, gated, *kept = expert(ids, second, cots, router, up, down, kept)
    second = exchange(second)

    far_send, near_send, far_own, near_own = expert_grads(kept, ids, ny, first)
    second, gated = lax.optimization_barrier((second, gated))
    gated = exchange(gated)

    dresid, dmixed, out_own, *out_sent = back_out(
        first,
        second,
        slot,
        order,
        resid,
        cotangent,
        gain2,
        out_weight,
        mixed_turned,
        kept[2],
        kept[4],
        near_own,
    )
    grads_far = far_grads(far_own, to_core(far_send), dresid)
    grads_y = to_y(grads_far)
    part1, own1, *sent1 = back_heads(0, qkv, dmixed, mixed, lse, act, grads_far)
    received = [to_core_all(out_sent), to_core_all(sent1)]
    tokens_part, near1, far1 = back_part(0, part1, qkv_weight, [out_own, own1], received)
    far1 = to_x(far1)
    part2, own2, *sent2 = back_heads(1, qkv, dmixed, mixed, lse, act, near1)
    received = [to_core_all(sent2)]
    tokens_grad = back_in(1, part2, qkv_weight, tokens_part, tokens, gain1, dresid)
    near2, far2 = core_sum([own2], received, tokens_grad)
    far2 = to_x(far2)
    block_out = combine(slot, resid, gated, near2)
    total1 = pair_sum(near1, far1, block_out)
    first = sum_z(exchange_z(total1), total1)
    total2, grads_y = lax.optimization_barrier((pair_sum(near2, far2, total1), grads_y))
    second = exchange_z(total2)
    up_grad, down_grad = near_grads(near_own, to_core(near_send), grads_y, first[0])
    second = sum_z(second, up_grad)
    qkv_grad, out_grad, router_grad, gain1_grad, gain2_grad = finish(
        weight_rows, gain_rows, first, second, experts
    )
    return (
        block_out,
        tokens_grad,
        gain1_grad[0],
        qkv_grad,
        out_grad,
        gain2_grad[0],
        router_grad,
        up_grad[None],
        down_grad[None],
    )


def solution(mesh):
    sizes = (mesh.shape["dp"], mesh.shape["expert"])
    return jax.shard_map(
        functools.partial(per_device, sizes),
        mesh=mesh,
        in_specs=(
            P(("dp", "expert"), None),
            P(("dp", "expert"), None),
            P(),
            P(),
            P(),
            P(),
            P(),
            P("expert", None, None),
            P("expert", None, None),
            P(("dp", "expert")),
            P(),
        ),
        out_specs=(
            P(("dp", "expert"), None),
            P(("dp", "expert"), None),
            P(("dp", "expert")),
            P(("dp", "expert"), None),
            P(("dp", "expert"), None),
            P(("dp", "expert")),
            P(("dp", "expert"), None),
            P("expert", None, "dp"),
            P("expert", "dp", None),
        ),
        check_vma=False,
    )
```

```python
import functools

import jax
import jax.numpy as jnp
from jax import lax
from jax.experimental import pallas as pl
from jax.experimental.pallas import tpu as pltpu
from jax.sharding import PartitionSpec as P

HEADS = 12
HDIM = 64
EPS = 1e-05
F32 = jnp.float32
BF = jnp.bfloat16
NT = (((1,), (1,)), ((), ()))
TN = (((0,), (0,)), ((), ()))
MIB = 2**20
VMEM = pl.BlockSpec(memory_space=pltpu.VMEM)
SMEM = pl.BlockSpec(memory_space=pltpu.SMEM)
GROUPS = 2
SCALE = 1
LIMIT = 52
ANY = pl.BlockSpec(memory_space=pltpu.HBM)


def out(shape, dtype):
    return jax.ShapeDtypeStruct(shape, dtype)


def params(mib=LIMIT):
    return pltpu.CompilerParams(vmem_limit_bytes=mib * MIB)


def cost(flops, nbytes):
    return pl.CostEstimate(
        flops=int(flops / SCALE), bytes_accessed=int(nbytes / SCALE), transcendentals=0
    )


def dot(a, b, dims=None):
    if dims is None:
        return jnp.dot(a, b, preferred_element_type=F32)
    return lax.dot_general(a, b, dims, preferred_element_type=F32)


def norm(value, gain):
    center = value - jnp.mean(value, -1, keepdims=True)
    inverse = lax.rsqrt(jnp.mean(center * center, -1, keepdims=True) + EPS)
    normed = center * inverse
    return normed, inverse, normed * gain


def as_row(ref):
    return ref[...].reshape(1, ref.shape[0])


def norm_pull(scaled, normed, inverse):
    return inverse * (
        scaled
        - jnp.mean(scaled, -1, keepdims=True)
        - normed * jnp.mean(scaled * normed, -1, keepdims=True)
    )


def slot_matrix(slot, slots):
    ids = lax.broadcasted_iota(jnp.int32, (slots, slot.shape[1]), 0)
    return jnp.where(ids == slot, 1.0, 0.0).astype(BF)


def plan_body(cap, cap_ref, routes_ref, cot_ref, slot_ref, send_ref):
    experts = cap_ref.shape[0]
    tok, width = cot_ref.shape
    count = experts * cap
    ids = lax.broadcasted_iota(jnp.int32, (experts, tok), 0)
    hot = routes_ref[...] == ids
    limit = jnp.zeros((experts, tok), F32)
    for e in range(experts):
        limit = jnp.where(ids == e, cap_ref[e].astype(F32), limit)
    before = lax.broadcasted_iota(jnp.int32, (tok, tok), 0) < lax.broadcasted_iota(
        jnp.int32, (tok, tok), 1
    )
    position = dot(
        jnp.where(hot, 1.0, 0.0).astype(BF), jnp.where(before, 1.0, 0.0).astype(BF)
    )
    kept = jnp.logical_and(hot, position < limit)
    number = position + (ids * cap).astype(F32) + 1.0
    number += jnp.where(position < cap, 0.0, float(count - cap))
    slot = (jnp.sum(jnp.where(kept, number, 0.0), 0, keepdims=True) - 1.0).astype(jnp.int32)
    slot_ref[...] = slot
    rows = dot(slot_matrix(slot, 2 * count), cot_ref[...]).astype(BF)
    send_ref[:, :width] = rows[:count]
    send_ref[:, width:] = rows[count:]


def plan(routes, capacity, cotangent, cap):
    tok, width = cotangent.shape
    count = capacity.shape[0] * cap
    return pl.pallas_call(
        functools.partial(plan_body, cap),
        in_specs=[SMEM, VMEM, VMEM],
        out_specs=[VMEM] * 2,
        out_shape=[out((1, tok), jnp.int32), out((count, 2 * width), BF)],
        compiler_params=params(63),
        cost_estimate=cost(4 * count * tok * width, 8 * count * width),
    )(capacity, routes.reshape(1, tok), cotangent)


def attend_body(
    tok_ref,
    gain1_ref,
    wqkv_ref,
    wout_ref,
    gain2_ref,
    slot_ref,
    act_ref,
    qkv_ref,
    mixed_ref,
    lse_ref,
    resid_ref,
    first_ref,
    second_ref,
):
    tok, width = tok_ref.shape
    inputs = tok_ref[...].astype(F32)
    act = norm(inputs, as_row(gain1_ref))[2].astype(BF)
    act_ref[...] = act
    for j in range(3):
        cols = pl.ds(j * width, width)
        qkv_ref[:, cols] = dot(act, wqkv_ref[:, cols]).astype(BF)
    lane = lax.broadcasted_iota(jnp.int32, (1, 128), 1)
    causal = lax.broadcasted_iota(jnp.int32, (tok, tok), 0) >= lax.broadcasted_iota(
        jnp.int32, (tok, tok), 1
    )
    lse = jnp.zeros((tok, 128), F32)
    for p in range(HEADS // 2):
        query = qkv_ref[:, 128 * p : 128 * p + 128] * jnp.asarray(HDIM**-0.5, BF)
        keys = qkv_ref[:, width + 128 * p : width + 128 * p + 128]
        values = qkv_ref[:, 2 * width + 128 * p : 2 * width + 128 * p + 128]
        parts = []
        for h in range(2):
            mine = (lane < HDIM) if h == 0 else (lane >= HDIM)
            scores = dot(jnp.where(mine, query, jnp.zeros_like(query)), keys, NT)
            scores = jnp.where(causal, scores, -1e30)
            top = jnp.max(scores, -1, keepdims=True)
            expo = jnp.exp(scores - top)
            total = jnp.sum(expo, -1, keepdims=True)
            parts.append(dot(expo.astype(BF), values) * (1.0 / total))
            lse = jnp.where(lane == 2 * p + h, top + jnp.log(total), lse)
        mixed_ref[:, 128 * p : 128 * p + 128] = jnp.where(lane < HDIM, *parts).astype(BF)
    lse_ref[...] = lse
    resid = inputs + dot(mixed_ref[...], wout_ref[...])
    resid_ref[...] = resid
    rows = norm(resid, as_row(gain2_ref))[2].astype(BF)
    count = first_ref.shape[0]
    send = dot(slot_matrix(slot_ref[...], 2 * count), rows).astype(BF)
    first_ref[...] = send[:count]
    second_ref[...] = send[count:]


def attend(tokens, gain1, wqkv, wout, gain2, slot, count):
    tok, width = tokens.shape
    return pl.pallas_call(
        attend_body,
        in_specs=[VMEM] * 6,
        out_specs=[VMEM] * 7,
        out_shape=[
            out((tok, width), BF),
            out((tok, 3 * width), BF),
            out((tok, width), BF),
            out((tok, 128), F32),
            out((tok, width), F32),
            out((count, width), BF),
            out((count, width), BF),
        ],
        compiler_params=params(),
        cost_estimate=cost(12e9, 12e6),
    )(tokens, gain1, wqkv, wout, gain2, slot)


def turn_body(order_ref, act_ref, mixed_ref, act_turned_ref, mixed_turned_ref):
    order = order_matrix(order_ref)
    act_turned_ref[...] = dot(order, act_ref[...], NT).astype(BF)
    mixed_turned_ref[...] = dot(order, mixed_ref[...], NT).astype(BF)


def order_matrix(order_ref):
    width = order_ref.shape[1]
    ids = lax.broadcasted_iota(jnp.int32, (width, width), 0)
    return jnp.where(ids == order_ref[...], 1.0, 0.0).astype(BF)


def turn(order, act, mixed):
    tok, width = act.shape
    return pl.pallas_call(
        turn_body,
        in_specs=[VMEM] * 3,
        out_specs=[VMEM] * 2,
        out_shape=[out((width, tok), BF)] * 2,
        compiler_params=params(),
        cost_estimate=cost(4 * tok * width * width, 8 * tok * width),
    )(order, act, mixed)


def expert_body(
    steps,
    ids_ref,
    rows_ref,
    cot_ref,
    router_ref,
    up_ref,
    down_ref,
    put,
    hid_ref,
    du_ref,
    rows_turned_ref,
    dy_turned_ref,
    dscore_ref,
    dy_ref,
    sum_ref,
    grad_ref,
    gate_ref,
):
    step = pl.program_id(0)

    @pl.when(step == 0)
    def _():
        score = jnp.sum(rows_ref[...].astype(F32) * router_ref[...], -1, keepdims=True)
        gate = jax.nn.sigmoid(score)
        gate_ref[...] = gate
        dy = (cot_ref[...].astype(F32) * gate).astype(BF)
        dy_ref[...] = dy
        rows_turned_ref[...] = jnp.transpose(rows_ref[...])
        dy_turned_ref[...] = jnp.transpose(dy)

    upper = dot(rows_ref[...], up_ref[...])
    hidden_grad = dot(dy_ref[...], down_ref[...], NT)
    cdf = 0.5 + 0.5 * lax.erf(upper * 0.7071067811865476)
    density = jnp.exp(-0.5 * upper * upper) * 0.3989422804014327
    hidden = (upper * cdf).astype(BF)
    upper_grad = (hidden_grad * (cdf + upper * density)).astype(BF)
    hid_ref[...] = hidden
    du_ref[...] = upper_grad
    part = dot(hidden, down_ref[...])
    part_grad = dot(upper_grad, up_ref[...], NT)

    @pl.when(step == 0)
    def _():
        sum_ref[...] = part
        grad_ref[...] = part_grad

    @pl.when(step > 0)
    def _():
        sum_ref[...] += part
        grad_ref[...] += part_grad

    @pl.when(step == steps - 1)
    def _():
        gate = gate_ref[...]
        gated = sum_ref[...] * gate
        dscore = jnp.sum(cot_ref[...].astype(F32) * gated, -1, keepdims=True) * (1.0 - gate)
        put(grad_ref[...] + dscore * router_ref[...], gated)
        lane = lax.broadcasted_iota(jnp.int32, dscore_ref.shape, 1)
        dscore_ref[...] = jnp.where(lane == ids_ref[2] + 1, dscore, 0.0).astype(BF)


def batch_body(first, steps, *refs):
    *ins, back_ref, gated_ref = refs[: (8 if first else 14)]

    def put(back, gated):
        back_ref[...] = back.astype(BF)
        gated_ref[...] = gated.astype(BF)

    expert_body(steps, *ins[:6], put, *refs[8 if first else 14 :])


def expert(ids, rows, cots, router, up, down, kept):
    i = 0 if kept is None else 1
    width, hidden = up.shape
    tile = 768
    steps = hidden // tile
    count = rows.shape[0]
    whole = lambda *s: pl.BlockSpec(s, lambda f: (0,) * len(s))
    side = pl.BlockSpec((count, width), lambda f: (0, i))
    tiles = pl.BlockSpec((count, tile), lambda f: (i, f))
    turned = pl.BlockSpec((width, count), lambda f: (0, i))
    return pl.pallas_call(
        functools.partial(batch_body, kept is None, steps),
        grid=(steps,),
        in_specs=[
            SMEM,
            whole(count, width),
            side,
            whole(1, width),
            pl.BlockSpec((width, tile), lambda f: (0, f)),
            pl.BlockSpec((tile, width), lambda f: (f, 0)),
        ]
        + [ANY] * (6 * i),
        out_specs=[
            whole(count, width),
            side,
            tiles,
            tiles,
            turned,
            turned,
            pl.BlockSpec((count, 128), lambda f: (i, 0)),
        ],
        out_shape=[
            out((count, width), BF),
            out((count, 2 * width), BF),
            out((2 * count, hidden), BF),
            out((2 * count, hidden), BF),
            out((width, 2 * count), BF),
            out((width, 2 * count), BF),
            out((2 * count, 128), BF),
        ],
        scratch_shapes=[
            pltpu.VMEM((count, width), BF),
            pltpu.VMEM((count, width), F32),
            pltpu.VMEM((count, width), F32),
            pltpu.VMEM((count, 1), F32),
        ],
        input_output_aliases={6 + j: 1 + j for j in range(6 * i)},
        compiler_params=params(),
        cost_estimate=cost(8 * count * width * hidden, 10 * width * hidden),
    )(ids, rows, cots, router, up, down, *(kept or ()))


def expert_grads_body(ny, ids_ref, turned_ref, du_ref, hid_ref, dy_ref, _, *refs):
    step = pl.program_id(0)
    up = dot(turned_ref[...], du_ref[...]).astype(BF)
    down = dot(dy_ref[...], hid_ref[...]).astype(BF)
    ends = (0, ny - 1, ny, 2 * ny - 1, 2 * ny)
    for ref, start, end in zip(refs, ends, ends[1:]):

        @pl.when(jnp.logical_and(step >= start, step < end))
        def _(ref=ref):
            ref[0, 0] = up
            ref[0, 1] = down


def expert_grads(kept, ids, ny, after):
    hid, du, rows, dy, _ = kept
    count, hidden = hid.shape
    width = rows.shape[0]
    part = hidden // (2 * ny)

    def chunk(s, ids):
        core = jnp.where(s < ny, 1 - ids[1], ids[1])
        away = jnp.where(s < ny, s, s - ny) + 1
        return jnp.bitwise_xor(jnp.where(away == ny, 0, away), ids[0]) * 2 + core

    whole = lambda *shape: pl.BlockSpec(shape, lambda s, ids: (0, 0))
    cols = pl.BlockSpec((count, part), lambda s, ids: (0, chunk(s, ids)))

    def block(start, number):
        return pl.BlockSpec(
            (1, 2, width, part), lambda s, ids: (jnp.clip(s - start, 0, number - 1), 0, 0, 0)
        )

    far, near = out((ny - 1, 2, width, part), BF), out((1, 2, width, part), BF)
    return pl.pallas_call(
        functools.partial(expert_grads_body, ny),
        grid_spec=pltpu.PrefetchScalarGridSpec(
            num_scalar_prefetch=1,
            grid=(2 * ny,),
            in_specs=[whole(width, count), cols, cols, whole(width, count), ANY],
            out_specs=[
                block(0, ny - 1),
                block(ny - 1, 1),
                block(ny, ny - 1),
                block(2 * ny - 1, 1),
            ],
        ),
        out_shape=[far, near, far, near],
        compiler_params=params(),
        cost_estimate=cost(1e6, 1e5),
    )(ids, rows, du, hid, dy, after)


def far_grads_body(own_ref, received_ref, _, out_ref):
    out_ref[...] = (own_ref[...].astype(F32) + received_ref[...].astype(F32)).astype(BF)


def far_grads(own, received, after):
    number, _, width, part = own.shape
    tall = width // 2
    block = pl.BlockSpec((1, 2, tall, part), lambda j, r: (j, 0, r, 0))
    return pl.pallas_call(
        far_grads_body,
        grid=(number, 2),
        in_specs=[block, block, ANY],
        out_specs=block,
        out_shape=out(own.shape, BF),
        compiler_params=params(),
        cost_estimate=cost(1e6, 1e5),
    )(own, received, after)


def near_grads_body(own_ref, received_ref, *refs):
    parts, (_, up_ref, down_ref) = refs[:-3], refs[-3:]
    total = own_ref[0].astype(F32) + received_ref[0].astype(F32)
    for ref in parts:
        total = total + ref[...].astype(F32)
    up_ref[...] = total[0]
    down_ref[...] = jnp.transpose(total[1])


def near_grads(own, received, parts, after):
    _, _, width, part = own.shape
    tall = 384
    first = pl.BlockSpec((1, 2, tall, part), lambda j: (0, 0, j, 0))
    return pl.pallas_call(
        near_grads_body,
        grid=(width // tall,),
        in_specs=[first, first]
        + [pl.BlockSpec((2, tall, part), lambda j: (0, j, 0))] * len(parts)
        + [ANY],
        out_specs=[
            pl.BlockSpec((tall, part), lambda j: (j, 0)),
            pl.BlockSpec((part, tall), lambda j: (0, j)),
        ],
        out_shape=[out((width, part), F32), out((part, width), F32)],
        compiler_params=params(),
        cost_estimate=cost(own.size, 3 * own.size),
    )(own, received, *parts, after)


def gather_rows(slot_ref, first, second):
    count = first.shape[0]
    select = slot_matrix(slot_ref[...], 2 * count)
    return dot(select[:count], first, TN) + dot(select[count:], second, TN)


def combine_body(slot_ref, resid_ref, rows_ref, _, out_ref):
    width = resid_ref.shape[1]
    rows = gather_rows(slot_ref, rows_ref[:, :width], rows_ref[:, width:])
    out_ref[...] = (resid_ref[...] + rows).astype(BF)


def combine(slot, resid, rows, after):
    return pl.pallas_call(
        combine_body,
        in_specs=[VMEM] * 3 + [ANY],
        out_specs=VMEM,
        out_shape=out(resid.shape, BF),
        compiler_params=params(),
        cost_estimate=cost(1e6, 1e5),
    )(slot, resid, rows, after)


def back_out_body(
    first_ref,
    second_ref,
    slot_ref,
    order_ref,
    resid_ref,
    cot_ref,
    gain_ref,
    wout_ref,
    mixed_ref,
    turned_ref,
    score_ref,
    _,
    dresid_ref,
    dmixed_ref,
    own_ref,
    send_ref,
    send_far_ref,
):
    width = first_ref.shape[1]
    grad = gather_rows(slot_ref, first_ref[...], second_ref[...])
    gain = as_row(gain_ref)
    normed, inverse, _ = norm(resid_ref[...], gain)
    gain_grad = jnp.sum(grad * normed, 0, keepdims=True)
    dresid = cot_ref[...].astype(F32) + norm_pull(grad * gain, normed, inverse)
    dresid_ref[...] = dresid
    low = dresid.astype(BF)
    dmixed_ref[...] = dot(low, wout_ref[...], NT).astype(BF)
    lane = lax.broadcasted_iota(jnp.int32, (width, 128), 1)
    column = jnp.transpose(jnp.broadcast_to(gain_grad, (128, width)))
    router_grad = dot(turned_ref[...], score_ref[...])
    extra = jnp.where(lane == 0, column, router_grad).astype(BF)
    extra = dot(order_matrix(order_ref), extra).astype(BF)
    rows = width // 4
    places = [slice(0, 2 * rows), slice(2 * rows, 3 * rows), slice(3 * rows, width)]
    for ref, part in zip((own_ref, send_ref, send_far_ref), places):
        ref[:, :width] = dot(mixed_ref[part], low).astype(BF)
        ref[:, width:] = extra[part]


def back_out(first, second, slot, order, resid, cot, gain, wout, mixed, turned, score, after):
    tok, width = cot.shape
    return pl.pallas_call(
        back_out_body,
        in_specs=[VMEM] * 11 + [ANY],
        out_specs=[VMEM] * 5,
        out_shape=[
            out((tok, width), F32),
            out((tok, width), BF),
            out((width // 2, width + 128), BF),
            out((width // 4, width + 128), BF),
            out((width // 4, width + 128), BF),
        ],
        compiler_params=params(),
        cost_estimate=cost(30e9, 8e6),
    )(first, second, slot, order, resid, cot, gain, wout, mixed, turned, score, after)


def back_heads_body(
    first,
    query_ref,
    key_ref,
    value_ref,
    dmixed_ref,
    mixed_ref,
    lse_ref,
    act_ref,
    _,
    dqkv_ref,
    own_ref,
    send_ref,
    send_far_ref,
):
    tok, width = query_ref.shape
    pairs = width // 128
    lane = lax.broadcasted_iota(jnp.int32, (1, 128), 1)
    causal = lax.broadcasted_iota(jnp.int32, (tok, tok), 1) >= lax.broadcasted_iota(
        jnp.int32, (tok, tok), 0
    )
    lse = jnp.transpose(lse_ref[...])
    shift = jnp.zeros((tok, 128), F32)
    for p in range(pairs):
        cols = slice(128 * p, 128 * p + 128)
        product = dmixed_ref[:, cols].astype(F32) * mixed_ref[:, cols].astype(F32)
        for h in range(2):
            mine = (lane < HDIM) if h == 0 else (lane >= HDIM)
            total = jnp.sum(jnp.where(mine, product, 0.0), -1, keepdims=True)
            shift = jnp.where(lane == 2 * p + h, total, shift)
    shift = jnp.transpose(shift)
    for p in range(pairs):
        cols = slice(128 * p, 128 * p + 128)
        query = query_ref[:, cols] * jnp.asarray(HDIM**-0.5, BF)
        keys, values, dmixed = key_ref[:, cols], value_ref[:, cols], dmixed_ref[:, cols]
        dquery, dkeys, dvalues = [], [], []
        for h in range(2):
            mine = (lane < HDIM) if h == 0 else (lane >= HDIM)
            own_keys = jnp.where(mine, keys, jnp.zeros_like(keys))
            own_values = jnp.where(mine, values, jnp.zeros_like(values))
            i = 2 * p + h
            scores = dot(own_keys, query, NT)
            probs = jnp.where(causal, jnp.exp(scores - lse[first + i : first + i + 1]), 0.0)
            dprobs = dot(own_values, dmixed, NT)
            dscores = (probs * (dprobs - shift[i : i + 1])).astype(BF)
            dvalues.append(dot(probs.astype(BF), dmixed))
            dkeys.append(dot(dscores, query))
            dquery.append(dot(dscores, keys, TN))
        dquery = jnp.where(lane < HDIM, *dquery) * HDIM**-0.5
        parts = (dquery, jnp.where(lane < HDIM, *dkeys), jnp.where(lane < HDIM, *dvalues))
        for j, part in enumerate(parts):
            start = j * width + 128 * p
            dqkv_ref[:, start : start + 128] = part.astype(BF)
    rows = act_ref.shape[0] // 2
    own_ref[...] = dot(act_ref[:rows], dqkv_ref[...]).astype(BF)
    send = dot(act_ref[rows:], dqkv_ref[...]).astype(BF)
    send_ref[...] = send[: rows // 2]
    send_far_ref[...] = send[rows // 2 :]


def back_heads(group, qkv, dmixed, mixed, lse, act, after):
    width, tok = act.shape
    cols = width // GROUPS
    block = lambda j: pl.BlockSpec((tok, cols), lambda i: (0, j))
    whole = lambda *s: pl.BlockSpec(s, lambda i: (0,) * len(s))
    half = (width // 2, 3 * cols)
    quarter = (width // 4, 3 * cols)
    return pl.pallas_call(
        functools.partial(back_heads_body, group * HEADS // GROUPS),
        grid=(1,),
        in_specs=[
            block(group),
            block(GROUPS + group),
            block(2 * GROUPS + group),
            block(group),
            block(group),
            whole(tok, 128),
            whole(width, tok),
            ANY,
        ],
        out_specs=[whole(tok, 3 * cols), whole(*half), whole(*quarter), whole(*quarter)],
        out_shape=[out((tok, 3 * cols), BF), out(half, BF), out(quarter, BF), out(quarter, BF)],
        compiler_params=params(),
        cost_estimate=cost(1e6, 1e5),
    )(qkv, qkv, qkv, dmixed, mixed, lse, act, after)


def back_in_body(*refs):
    number = 3 * GROUPS
    part_refs, weight_refs = refs[:GROUPS], refs[GROUPS : GROUPS + number]
    tok_ref, gain_ref, dresid_ref, _, out_ref = refs[GROUPS + number :]
    cols = part_refs[0].shape[1] // 3
    grad = sum(
        dot(part_refs[k // 3][:, k % 3 * cols : (k % 3 + 1) * cols], ref[...], NT)
        for k, ref in enumerate(weight_refs)
    )
    gain = as_row(gain_ref)
    normed, inverse, _ = norm(tok_ref[...].astype(F32), gain)
    out_ref[...] = dresid_ref[...] + norm_pull(grad * gain, normed, inverse)


def back_in(dqkv, wqkv, tokens, gain, dresid, after):
    tok, width = tokens.shape
    cols = width // GROUPS
    whole = lambda *s: pl.BlockSpec(s, lambda i: (0,) * len(s))
    weights = [
        pl.BlockSpec((width, cols), lambda i, j=j, g=g: (0, j * GROUPS + g))
        for g in range(GROUPS)
        for j in range(3)
    ]
    return pl.pallas_call(
        back_in_body,
        grid=(1,),
        in_specs=[whole(*part.shape) for part in dqkv]
        + weights
        + [whole(*a.shape) for a in (tokens, gain, dresid)]
        + [ANY],
        out_specs=whole(tok, width),
        out_shape=out((tok, width), F32),
        compiler_params=params(63),
        cost_estimate=cost(1e6, 1e5),
    )(*dqkv, *[wqkv] * len(weights), tokens, gain, dresid, after)


def core_sum_body(number, *refs):
    own_refs, refs = refs[:number], refs[number:]
    near_ref, far_ref = refs[2 * number : 2 * number + 2]
    rows = near_ref.shape[0]
    start = 0
    for i, own_ref in enumerate(own_refs):
        place = slice(start, start + own_ref.shape[1])
        start = place.stop
        for k, ref in enumerate((near_ref, far_ref)):
            own = own_ref[k * rows : (k + 1) * rows].astype(F32)
            ref[:, place] = (own + refs[2 * i + k][...].astype(F32)).astype(BF)


def core_sum(own, received, after):
    rows = own[0].shape[0] // 2
    cols = sum(part.shape[1] for part in own)

    def body(*refs):
        core_sum_body(len(own), *refs[: 3 * len(own)], *refs[3 * len(own) + 1 :])

    return pl.pallas_call(
        body,
        in_specs=[VMEM] * (3 * len(own)) + [ANY],
        out_specs=[VMEM] * 2,
        out_shape=[out((rows, cols), BF)] * 2,
        compiler_params=params(),
        cost_estimate=cost(1e6, 1e5),
    )(*own, *[part for parts in received for part in parts], after)


def pair_sum_body(first_ref, second_ref, _, out_ref):
    out_ref[...] = (first_ref[...].astype(F32) + second_ref[...].astype(F32)).astype(BF)


def pair_sum(first, second, after):
    return pl.pallas_call(
        pair_sum_body,
        in_specs=[VMEM] * 2 + [ANY],
        out_specs=VMEM,
        out_shape=out(first.shape, BF),
        compiler_params=params(),
        cost_estimate=cost(1e6, 1e5),
    )(first, second, after)


def split_sum_body(index_ref, first_ref, second_ref, _, *out_refs):
    for d, ref in enumerate(out_refs):
        place = jnp.bitwise_xor(index_ref[3], d)
        total = first_ref[place].astype(F32) + second_ref[place].astype(F32)
        ref[...] = total.astype(BF)


def split_sum(ids, first, second, after, nz):
    rows, cols = first.shape
    shape = (nz, rows // nz, cols)
    return pl.pallas_call(
        split_sum_body,
        in_specs=[SMEM, VMEM, VMEM, ANY],
        out_specs=[VMEM] * nz,
        out_shape=[out(shape[1:], BF)] * nz,
        compiler_params=params(),
        cost_estimate=cost(1e6, 1e5),
    )(ids, first.reshape(shape), second.reshape(shape), after)


def z_parts_body(ny, number, *refs):
    part_refs, (_, *out_refs) = refs[:number], refs[number:]
    total = sum(ref[...].astype(F32) for ref in part_refs)
    rows = total.shape[0] // ny
    for j, ref in enumerate(out_refs):
        ref[...] = total[j * rows : (j + 1) * rows].astype(ref.dtype)


def z_parts(parts, ny, after):
    rows, cols = parts[0].shape
    shape = (rows // ny, cols)
    return pl.pallas_call(
        functools.partial(z_parts_body, ny, len(parts)),
        in_specs=[VMEM] * len(parts) + [ANY],
        out_specs=[VMEM] * ny,
        out_shape=[out(shape, F32)] + [out(shape, BF)] * (ny - 1),
        compiler_params=params(),
        cost_estimate=cost(1e6, 1e5),
    )(*parts, after)


def z_sum_body(blocks_ref, _, near_ref, *far_refs):
    near_ref[...] = jnp.sum(blocks_ref[:, 0].astype(F32), 0)
    for j, ref in enumerate(far_refs):
        ref[...] = jnp.sum(blocks_ref[:, j + 1].astype(F32), 0).astype(BF)


def z_sum(blocks, after):
    _, ny, rows, cols = blocks.shape
    return pl.pallas_call(
        z_sum_body,
        in_specs=[VMEM, ANY],
        out_specs=[VMEM] * ny,
        out_shape=[out((rows, cols), F32)] + [out((rows, cols), BF)] * (ny - 1),
        compiler_params=params(),
        cost_estimate=cost(blocks.size, blocks.size),
    )(blocks, after)


def finish_body(ny, weight_ref, gain_ref, *refs):
    part_refs, refs = refs[: 2 * ny], refs[2 * ny + 1 :]
    grad_ref, out_ref, router_ref, gain1_ref, gain2_ref = refs
    rows, width = out_ref.shape
    cols = width // GROUPS
    first, second = (
        sum(ref[...].astype(F32) for ref in part_refs[i : i + ny]) for i in (0, ny)
    )
    out_ref[...] = first[:, :width]
    extra = first[:, width : width + 128]
    experts = router_ref.shape[0]
    groups = [first[:, width + 128 :], second]
    gain_grad = 0.0
    for g, total in enumerate(groups):
        for j in range(3):
            piece = total[:, j * cols : (j + 1) * cols]
            place = slice((j * GROUPS + g) * cols, (j * GROUPS + g + 1) * cols)
            grad_ref[:, place] = piece
            weight = weight_ref[:, place].astype(F32)
            gain_grad += jnp.sum(piece * weight, -1, keepdims=True)
    lane = lax.broadcasted_iota(jnp.int32, (rows, 128), 1)
    turned = jnp.transpose(jnp.where(lane == experts + 1, gain_grad / gain_ref[...], extra))
    gain2_ref[...] = turned[:1]
    router_ref[...] = turned[1 : experts + 1]
    gain1_ref[...] = turned[experts + 1 : experts + 2]


def finish(weight, gain, first, second, experts, after):
    rows, width = weight.shape
    return pl.pallas_call(
        functools.partial(finish_body, len(first)),
        in_specs=[VMEM] * (2 + len(first) + len(second)) + [ANY],
        out_specs=[VMEM] * 5,
        out_shape=[
            out((rows, width), F32),
            out((rows, width // 3), F32),
            out((experts, rows), F32),
            out((1, rows), F32),
            out((1, rows), F32),
        ],
        compiler_params=params(),
        cost_estimate=cost(first[0].size, 4 * first[0].size),
    )(weight, gain, *first, *second, after)


def per_device(
    sizes,
    tokens,
    cotangent,
    norm1_gain,
    qkv_weight,
    out_weight,
    norm2_gain,
    router_weight,
    up_weight,
    down_weight,
    routes,
    capacity,
):
    n_dp, n_ex = sizes
    ny = n_dp // 2
    tok, width = tokens.shape
    experts = router_weight.shape[1]
    cap = 3 * tok // (4 * experts)
    dp = lax.axis_index("dp")
    ex = lax.axis_index("expert")
    ids = jnp.stack([dp // 2, dp % 2, ex, ex // 2]).astype(jnp.int32)
    gain1, gain2 = norm1_gain, norm2_gain
    router = lax.dynamic_slice(router_weight, (0, ex), (width, 1)).reshape(1, width)
    up, down = up_weight[0], down_weight[0]
    rows_dev = width // (n_dp * n_ex)
    start = (dp * n_ex + ex) * rows_dev
    weight_rows = lax.dynamic_slice(qkv_weight, (start, 0), (rows_dev, 3 * width))
    gain_rows = lax.dynamic_slice(norm1_gain, (start,), (rows_dev,)).reshape(rows_dev, 1)
    nz = n_ex // 2
    row = jnp.arange(width, dtype=jnp.int32)
    chunk = row // rows_dev
    y, core, z, x = chunk // (2 * n_ex), chunk // n_ex % 2, chunk // 2 % nz, chunk % 2
    order = ((core ^ (dp % 2)) * 2 + (x ^ (ex % 2))) * nz + z
    order = ((order * ny + (y ^ (dp // 2))) * rows_dev + row % rows_dev).reshape(1, width)

    z_groups = [list(range(0, n_ex, 2)), list(range(1, n_ex, 2))]

    def exchange(value):
        return lax.all_to_all(value, "expert", split_axis=0, concat_axis=0, tiled=True)

    def exchange_z(value):
        return lax.all_to_all(
            value, "expert", split_axis=0, concat_axis=0, tiled=True, axis_index_groups=z_groups
        )

    def to_core(value):
        return lax.ppermute(value, "dp", [(i, i ^ 1) for i in range(n_dp)])

    def to_y(values):
        return [
            lax.ppermute(values[j - 1], "dp", [(i, i ^ (2 * j)) for i in range(n_dp)])
            for j in range(1, ny)
        ]

    def to_core_all(values):
        return [to_core(value) for value in values]

    def to_x(value):
        return lax.ppermute(value, "expert", [(i, i ^ 1) for i in range(n_ex)])

    def sum_z(blocks, after):
        near, *far = z_sum(blocks.reshape(nz, ny, rows_dev, blocks.shape[1]), after)
        return [near] + to_y(far)

    slot, cots = plan(routes, capacity, cotangent, cap)
    cots = exchange(cots)
    act, qkv, mixed, lse, resid, first, second = attend(
        tokens, gain1, qkv_weight, out_weight, gain2, slot, experts * cap
    )
    first, cots = lax.optimization_barrier((first, cots))
    first = exchange(first)
    act, mixed_turned = turn(order, act, mixed)
    first, order, weight_rows, gain_rows, second, act, mixed_turned, ids = lax.optimization_barrier(
        (first, order, weight_rows, gain_rows, second, act, mixed_turned, ids)
    )
    second = exchange(second)
    first, *kept = expert(ids, first, cots, router, up, down, None)
    first = exchange(first)
    second, gated, *kept = expert(ids, second, cots, router, up, down, kept)
    second = exchange(second)

    far_send, near_send, far_own, near_own = expert_grads(kept, ids, ny, first)
    second, gated = lax.optimization_barrier((second, gated))
    gated = exchange(gated)

    dresid, dmixed, out_own, *out_sent = back_out(
        first,
        second,
        slot,
        order,
        resid,
        cotangent,
        gain2,
        out_weight,
        mixed_turned,
        kept[2],
        kept[4],
        near_own,
    )
    part1, own1, *sent1 = back_heads(0, qkv, dmixed, mixed, lse, act, dmixed)
    grads_far = far_grads(far_own, to_core(far_send), part1)
    grads_y = to_y(grads_far)
    received = [to_core_all(out_sent), to_core_all(sent1)]
    near1, far1 = core_sum([out_own, own1], received, grads_far)
    far1 = to_x(far1)
    part2, own2, *sent2 = back_heads(1, qkv, dmixed, mixed, lse, act, near1)
    received = [to_core_all(sent2)]
    block_out = combine(slot, resid, gated, part2)
    near2, far2 = core_sum([own2], received, block_out)
    far2 = to_x(far2)
    total1 = pair_sum(near1, far1, near2)
    blocks1 = exchange_z(total1)
    tokens_grad = back_in([part1, part2], qkv_weight, tokens, gain1, dresid, total1)
    own, *sent = split_sum(ids, near2, far2, tokens_grad, nz)
    parts = [own] + [
        lax.ppermute(value, "expert", [(i, i ^ (2 * d + 2)) for i in range(n_ex)])
        for d, value in enumerate(sent)
    ]
    near, *far = z_parts(parts, ny, tokens_grad)
    second = [near] + to_y(far)
    first = sum_z(blocks1, near)
    up_grad, down_grad = near_grads(near_own, to_core(near_send), grads_y, first[0])
    qkv_grad, out_grad, router_grad, gain1_grad, gain2_grad = finish(
        weight_rows, gain_rows, first, second, experts, up_grad
    )
    return (
        block_out,
        tokens_grad,
        gain1_grad[0],
        qkv_grad,
        out_grad,
        gain2_grad[0],
        router_grad.T,
        up_grad[None],
        down_grad[None],
    )


def solution(mesh):
    sizes = (mesh.shape["dp"], mesh.shape["expert"])
    return jax.shard_map(
        functools.partial(per_device, sizes),
        mesh=mesh,
        in_specs=(
            P(("dp", "expert"), None),
            P(("dp", "expert"), None),
            P(),
            P(),
            P(),
            P(),
            P(),
            P("expert", None, None),
            P("expert", None, None),
            P(("dp", "expert")),
            P(),
        ),
        out_specs=(
            P(("dp", "expert"), None),
            P(("dp", "expert"), None),
            P(("dp", "expert")),
            P(("dp", "expert"), None),
            P(("dp", "expert"), None),
            P(("dp", "expert")),
            P(("dp", "expert"), None),
            P("expert", None, "dp"),
            P("expert", "dp", None),
        ),
        check_vma=False,
    )
```

```python
import functools

import jax
import jax.numpy as jnp
from jax import lax
from jax.experimental import pallas as pl
from jax.experimental.pallas import tpu as pltpu
from jax.sharding import PartitionSpec as P

HEADS = 12
HDIM = 64
EPS = 1e-05
F32 = jnp.float32
BF = jnp.bfloat16
NT = (((1,), (1,)), ((), ()))
TN = (((0,), (0,)), ((), ()))
MIB = 2**20
VMEM = pl.BlockSpec(memory_space=pltpu.VMEM)
SMEM = pl.BlockSpec(memory_space=pltpu.SMEM)
GROUPS = 2
SCALE = 1
LIMIT = 52
ANY = pl.BlockSpec(memory_space=pltpu.HBM)


def out(shape, dtype):
    return jax.ShapeDtypeStruct(shape, dtype)


def params(mib=LIMIT):
    return pltpu.CompilerParams(vmem_limit_bytes=mib * MIB)


def cost(flops, nbytes):
    return pl.CostEstimate(
        flops=int(flops / SCALE), bytes_accessed=int(nbytes / SCALE), transcendentals=0
    )


def dot(a, b, dims=None):
    if dims is None:
        return jnp.dot(a, b, preferred_element_type=F32)
    return lax.dot_general(a, b, dims, preferred_element_type=F32)


def norm(value, gain):
    center = value - jnp.mean(value, -1, keepdims=True)
    inverse = lax.rsqrt(jnp.mean(center * center, -1, keepdims=True) + EPS)
    normed = center * inverse
    return normed, inverse, normed * gain


def as_row(ref):
    return ref[...].reshape(1, ref.shape[0])


def norm_pull(scaled, normed, inverse):
    return inverse * (
        scaled
        - jnp.mean(scaled, -1, keepdims=True)
        - normed * jnp.mean(scaled * normed, -1, keepdims=True)
    )


def slot_matrix(slot, slots):
    ids = lax.broadcasted_iota(jnp.int32, (slots, slot.shape[1]), 0)
    return jnp.where(ids == slot, 1.0, 0.0).astype(BF)


def plan_body(cap, cap_ref, routes_ref, cot_ref, slot_ref, send_ref):
    experts = cap_ref.shape[0]
    tok, width = cot_ref.shape
    count = experts * cap
    ids = lax.broadcasted_iota(jnp.int32, (experts, tok), 0)
    hot = routes_ref[...] == ids
    limit = jnp.zeros((experts, tok), F32)
    for e in range(experts):
        limit = jnp.where(ids == e, cap_ref[e].astype(F32), limit)
    before = lax.broadcasted_iota(jnp.int32, (tok, tok), 0) < lax.broadcasted_iota(
        jnp.int32, (tok, tok), 1
    )
    position = dot(
        jnp.where(hot, 1.0, 0.0).astype(BF), jnp.where(before, 1.0, 0.0).astype(BF)
    )
    kept = jnp.logical_and(hot, position < limit)
    number = position + (ids * cap).astype(F32) + 1.0
    number += jnp.where(position < cap, 0.0, float(count - cap))
    slot = (jnp.sum(jnp.where(kept, number, 0.0), 0, keepdims=True) - 1.0).astype(jnp.int32)
    slot_ref[...] = slot
    rows = dot(slot_matrix(slot, 2 * count), cot_ref[...]).astype(BF)
    send_ref[:, :width] = rows[:count]
    send_ref[:, width:] = rows[count:]


def plan(routes, capacity, cotangent, cap):
    tok, width = cotangent.shape
    count = capacity.shape[0] * cap
    return pl.pallas_call(
        functools.partial(plan_body, cap),
        in_specs=[SMEM, VMEM, VMEM],
        out_specs=[VMEM] * 2,
        out_shape=[out((1, tok), jnp.int32), out((count, 2 * width), BF)],
        compiler_params=params(63),
        cost_estimate=cost(4 * count * tok * width, 8 * count * width),
    )(capacity, routes.reshape(1, tok), cotangent)


def attend_body(
    tok_ref,
    gain1_ref,
    wqkv_ref,
    wout_ref,
    gain2_ref,
    slot_ref,
    act_ref,
    qkv_ref,
    mixed_ref,
    lse_ref,
    resid_ref,
    first_ref,
    second_ref,
):
    tok, width = tok_ref.shape
    inputs = tok_ref[...].astype(F32)
    act = norm(inputs, as_row(gain1_ref))[2].astype(BF)
    act_ref[...] = act
    for j in range(3):
        cols = pl.ds(j * width, width)
        qkv_ref[:, cols] = dot(act, wqkv_ref[:, cols]).astype(BF)
    lane = lax.broadcasted_iota(jnp.int32, (1, 128), 1)
    causal = lax.broadcasted_iota(jnp.int32, (tok, tok), 0) >= lax.broadcasted_iota(
        jnp.int32, (tok, tok), 1
    )
    lse = jnp.zeros((tok, 128), F32)
    for p in range(HEADS // 2):
        query = qkv_ref[:, 128 * p : 128 * p + 128] * jnp.asarray(HDIM**-0.5, BF)
        keys = qkv_ref[:, width + 128 * p : width + 128 * p + 128]
        values = qkv_ref[:, 2 * width + 128 * p : 2 * width + 128 * p + 128]
        parts = []
        for h in range(2):
            mine = (lane < HDIM) if h == 0 else (lane >= HDIM)
            scores = dot(jnp.where(mine, query, jnp.zeros_like(query)), keys, NT)
            scores = jnp.where(causal, scores, -1e30)
            top = jnp.max(scores, -1, keepdims=True)
            expo = jnp.exp(scores - top)
            total = jnp.sum(expo, -1, keepdims=True)
            parts.append(dot(expo.astype(BF), values) * (1.0 / total))
            lse = jnp.where(lane == 2 * p + h, top + jnp.log(total), lse)
        mixed_ref[:, 128 * p : 128 * p + 128] = jnp.where(lane < HDIM, *parts).astype(BF)
    lse_ref[...] = lse
    resid = inputs + dot(mixed_ref[...], wout_ref[...])
    resid_ref[...] = resid
    rows = norm(resid, as_row(gain2_ref))[2].astype(BF)
    count = first_ref.shape[0]
    send = dot(slot_matrix(slot_ref[...], 2 * count), rows).astype(BF)
    first_ref[...] = send[:count]
    second_ref[...] = send[count:]


def attend(tokens, gain1, wqkv, wout, gain2, slot, count):
    tok, width = tokens.shape
    return pl.pallas_call(
        attend_body,
        in_specs=[VMEM] * 6,
        out_specs=[VMEM] * 7,
        out_shape=[
            out((tok, width), BF),
            out((tok, 3 * width), BF),
            out((tok, width), BF),
            out((tok, 128), F32),
            out((tok, width), F32),
            out((count, width), BF),
            out((count, width), BF),
        ],
        compiler_params=params(63),
        cost_estimate=cost(12e9, 12e6),
    )(tokens, gain1, wqkv, wout, gain2, slot)


def turn_body(order_ref, act_ref, mixed_ref, act_turned_ref, mixed_turned_ref):
    order = order_matrix(order_ref)
    act_turned_ref[...] = dot(order, act_ref[...], NT).astype(BF)
    mixed_turned_ref[...] = dot(order, mixed_ref[...], NT).astype(BF)


def order_matrix(order_ref):
    width = order_ref.shape[1]
    ids = lax.broadcasted_iota(jnp.int32, (width, width), 0)
    return jnp.where(ids == order_ref[...], 1.0, 0.0).astype(BF)


def turn(order, act, mixed):
    tok, width = act.shape
    return pl.pallas_call(
        turn_body,
        in_specs=[VMEM] * 3,
        out_specs=[VMEM] * 2,
        out_shape=[out((width, tok), BF)] * 2,
        compiler_params=params(63),
        cost_estimate=cost(4 * tok * width * width, 8 * tok * width),
    )(order, act, mixed)


def expert_body(
    steps,
    ids_ref,
    rows_ref,
    cot_ref,
    router_ref,
    up_ref,
    down_ref,
    put,
    hid_ref,
    du_ref,
    rows_turned_ref,
    dy_turned_ref,
    dscore_ref,
    dy_ref,
    sum_ref,
    grad_ref,
    gate_ref,
):
    step = pl.program_id(0)

    @pl.when(step == 0)
    def _():
        score = jnp.sum(rows_ref[...].astype(F32) * router_ref[...], -1, keepdims=True)
        gate = jax.nn.sigmoid(score)
        gate_ref[...] = gate
        dy = (cot_ref[...].astype(F32) * gate).astype(BF)
        dy_ref[...] = dy
        rows_turned_ref[...] = jnp.transpose(rows_ref[...])
        dy_turned_ref[...] = jnp.transpose(dy)

    upper = dot(rows_ref[...], up_ref[...])
    hidden_grad = dot(dy_ref[...], down_ref[...], NT)
    cdf = 0.5 + 0.5 * lax.erf(upper * 0.7071067811865476)
    density = jnp.exp(-0.5 * upper * upper) * 0.3989422804014327
    hidden = (upper * cdf).astype(BF)
    upper_grad = (hidden_grad * (cdf + upper * density)).astype(BF)
    hid_ref[...] = hidden
    du_ref[...] = upper_grad
    part = dot(hidden, down_ref[...])
    part_grad = dot(upper_grad, up_ref[...], NT)

    @pl.when(step == 0)
    def _():
        sum_ref[...] = part
        grad_ref[...] = part_grad

    @pl.when(step > 0)
    def _():
        sum_ref[...] += part
        grad_ref[...] += part_grad

    @pl.when(step == steps - 1)
    def _():
        gate = gate_ref[...]
        gated = sum_ref[...] * gate
        dscore = jnp.sum(cot_ref[...].astype(F32) * gated, -1, keepdims=True) * (1.0 - gate)
        put(grad_ref[...] + dscore * router_ref[...], gated)
        lane = lax.broadcasted_iota(jnp.int32, dscore_ref.shape, 1)
        dscore_ref[...] = jnp.where(lane == ids_ref[2] + 1, dscore, 0.0).astype(BF)


def batch_body(first, steps, *refs):
    *ins, back_ref, gated_ref = refs[: (8 if first else 14)]

    def put(back, gated):
        back_ref[...] = back.astype(BF)
        gated_ref[...] = gated.astype(BF)

    expert_body(steps, *ins[:6], put, *refs[8 if first else 14 :])


def expert(ids, rows, cots, router, up, down, kept):
    i = 0 if kept is None else 1
    width, hidden = up.shape
    tile = 768
    steps = hidden // tile
    count = rows.shape[0]
    whole = lambda *s: pl.BlockSpec(s, lambda f: (0,) * len(s))
    side = pl.BlockSpec((count, width), lambda f: (0, i))
    tiles = pl.BlockSpec((count, tile), lambda f: (i, f))
    turned = pl.BlockSpec((width, count), lambda f: (0, i))
    return pl.pallas_call(
        functools.partial(batch_body, kept is None, steps),
        grid=(steps,),
        in_specs=[
            SMEM,
            whole(count, width),
            side,
            whole(1, width),
            pl.BlockSpec((width, tile), lambda f: (0, f)),
            pl.BlockSpec((tile, width), lambda f: (f, 0)),
        ]
        + [ANY] * (6 * i),
        out_specs=[
            whole(count, width),
            side,
            tiles,
            tiles,
            turned,
            turned,
            pl.BlockSpec((count, 128), lambda f: (i, 0)),
        ],
        out_shape=[
            out((count, width), BF),
            out((count, 2 * width), BF),
            out((2 * count, hidden), BF),
            out((2 * count, hidden), BF),
            out((width, 2 * count), BF),
            out((width, 2 * count), BF),
            out((2 * count, 128), BF),
        ],
        scratch_shapes=[
            pltpu.VMEM((count, width), BF),
            pltpu.VMEM((count, width), F32),
            pltpu.VMEM((count, width), F32),
            pltpu.VMEM((count, 1), F32),
        ],
        input_output_aliases={6 + j: 1 + j for j in range(6 * i)},
        compiler_params=params(63),
        cost_estimate=cost(8 * count * width * hidden, 10 * width * hidden),
    )(ids, rows, cots, router, up, down, *(kept or ()))


def expert_grads_body(ny, ids_ref, turned_ref, du_ref, hid_ref, dy_ref, _, *refs):
    step = pl.program_id(0)
    up = dot(turned_ref[...], du_ref[...]).astype(BF)
    down = dot(dy_ref[...], hid_ref[...]).astype(BF)
    ends = (0, ny - 1, ny, 2 * ny - 1, 2 * ny)
    for ref, start, end in zip(refs, ends, ends[1:]):

        @pl.when(jnp.logical_and(step >= start, step < end))
        def _(ref=ref):
            ref[0, 0] = up
            ref[0, 1] = down


def expert_grads(kept, ids, ny, after):
    hid, du, rows, dy, _ = kept
    count, hidden = hid.shape
    width = rows.shape[0]
    part = hidden // (2 * ny)

    def chunk(s, ids):
        core = jnp.where(s < ny, 1 - ids[1], ids[1])
        away = jnp.where(s < ny, s, s - ny) + 1
        return jnp.bitwise_xor(jnp.where(away == ny, 0, away), ids[0]) * 2 + core

    whole = lambda *shape: pl.BlockSpec(shape, lambda s, ids: (0, 0))
    cols = pl.BlockSpec((count, part), lambda s, ids: (0, chunk(s, ids)))

    def block(start, number):
        return pl.BlockSpec(
            (1, 2, width, part), lambda s, ids: (jnp.clip(s - start, 0, number - 1), 0, 0, 0)
        )

    far, near = out((ny - 1, 2, width, part), BF), out((1, 2, width, part), BF)
    return pl.pallas_call(
        functools.partial(expert_grads_body, ny),
        grid_spec=pltpu.PrefetchScalarGridSpec(
            num_scalar_prefetch=1,
            grid=(2 * ny,),
            in_specs=[whole(width, count), cols, cols, whole(width, count), ANY],
            out_specs=[
                block(0, ny - 1),
                block(ny - 1, 1),
                block(ny, ny - 1),
                block(2 * ny - 1, 1),
            ],
        ),
        out_shape=[far, near, far, near],
        compiler_params=params(63),
        cost_estimate=cost(1e6, 1e5),
    )(ids, rows, du, hid, dy, after)


def far_grads_body(own_ref, received_ref, _, out_ref):
    out_ref[...] = (own_ref[...].astype(F32) + received_ref[...].astype(F32)).astype(BF)


def far_grads(own, received, after):
    number, _, width, part = own.shape
    tall = width // 2
    block = pl.BlockSpec((1, 2, tall, part), lambda j, r: (j, 0, r, 0))
    return pl.pallas_call(
        far_grads_body,
        grid=(number, 2),
        in_specs=[block, block, ANY],
        out_specs=block,
        out_shape=out(own.shape, BF),
        compiler_params=params(52),
        cost_estimate=cost(1e6, 1e5),
    )(own, received, after)


def near_grads_body(own_ref, received_ref, *refs):
    parts, (_, up_ref, down_ref) = refs[:-3], refs[-3:]
    total = own_ref[0].astype(F32) + received_ref[0].astype(F32)
    for ref in parts:
        total = total + ref[...].astype(F32)
    up_ref[...] = total[0]
    down_ref[...] = jnp.transpose(total[1])


def near_grads(own, received, parts, after):
    _, _, width, part = own.shape
    tall = 384
    first = pl.BlockSpec((1, 2, tall, part), lambda j: (0, 0, j, 0))
    return pl.pallas_call(
        near_grads_body,
        grid=(width // tall,),
        in_specs=[first, first]
        + [pl.BlockSpec((2, tall, part), lambda j: (0, j, 0))] * len(parts)
        + [ANY],
        out_specs=[
            pl.BlockSpec((tall, part), lambda j: (j, 0)),
            pl.BlockSpec((part, tall), lambda j: (0, j)),
        ],
        out_shape=[out((width, part), F32), out((part, width), F32)],
        compiler_params=params(52),
        cost_estimate=cost(own.size, 3 * own.size),
    )(own, received, *parts, after)


def gather_rows(slot_ref, first, second):
    count = first.shape[0]
    select = slot_matrix(slot_ref[...], 2 * count)
    return dot(select[:count], first, TN) + dot(select[count:], second, TN)


def combine_body(slot_ref, resid_ref, rows_ref, _, out_ref):
    width = resid_ref.shape[1]
    rows = gather_rows(slot_ref, rows_ref[:, :width], rows_ref[:, width:])
    out_ref[...] = (resid_ref[...] + rows).astype(BF)


def combine(slot, resid, rows, after):
    return pl.pallas_call(
        combine_body,
        in_specs=[VMEM] * 3 + [ANY],
        out_specs=VMEM,
        out_shape=out(resid.shape, BF),
        compiler_params=params(52),
        cost_estimate=cost(1e6, 1e5),
    )(slot, resid, rows, after)


def back_out_body(
    first_ref,
    second_ref,
    slot_ref,
    resid_ref,
    cot_ref,
    gain_ref,
    wout_ref,
    mixed_ref,
    _,
    dresid_ref,
    dmixed_ref,
    gain_grad_ref,
    own_ref,
    send_ref,
    send_far_ref,
):
    width = first_ref.shape[1]
    grad = gather_rows(slot_ref, first_ref[...], second_ref[...])
    gain = as_row(gain_ref)
    normed, inverse, _ = norm(resid_ref[...], gain)
    gain_grad_ref[...] = jnp.sum(grad * normed, 0, keepdims=True)
    dresid = cot_ref[...].astype(F32) + norm_pull(grad * gain, normed, inverse)
    dresid_ref[...] = dresid
    low = dresid.astype(BF)
    dmixed_ref[...] = dot(low, wout_ref[...], NT).astype(BF)
    weight_grad = dot(mixed_ref[...], low).astype(BF)
    rows = width // 4
    own_ref[...] = weight_grad[: 2 * rows]
    send_ref[...] = weight_grad[2 * rows : 3 * rows]
    send_far_ref[...] = weight_grad[3 * rows :]


def back_out(first, second, slot, resid, cot, gain, wout, mixed, after):
    tok, width = cot.shape
    quarter = out((width // 4, width), BF)
    return pl.pallas_call(
        back_out_body,
        in_specs=[VMEM] * 8 + [ANY],
        out_specs=[VMEM] * 6,
        out_shape=[
            out((tok, width), F32),
            out((tok, width), BF),
            out((1, width), F32),
            out((width // 2, width), BF),
            quarter,
            quarter,
        ],
        compiler_params=params(52),
        cost_estimate=cost(30e9, 8e6),
    )(first, second, slot, resid, cot, gain, wout, mixed, after)


def back_heads_body(
    first,
    query_ref,
    key_ref,
    value_ref,
    dmixed_ref,
    mixed_ref,
    lse_ref,
    act_ref,
    _,
    *refs,
):
    *more_refs, dqkv_ref, own_ref, send_ref, send_far_ref = refs
    tok, width = query_ref.shape
    pairs = width // 128
    lane = lax.broadcasted_iota(jnp.int32, (1, 128), 1)
    causal = lax.broadcasted_iota(jnp.int32, (tok, tok), 1) >= lax.broadcasted_iota(
        jnp.int32, (tok, tok), 0
    )
    lse = jnp.transpose(lse_ref[...])
    shift = jnp.zeros((tok, 128), F32)
    for p in range(pairs):
        cols = slice(128 * p, 128 * p + 128)
        product = dmixed_ref[:, cols].astype(F32) * mixed_ref[:, cols].astype(F32)
        for h in range(2):
            mine = (lane < HDIM) if h == 0 else (lane >= HDIM)
            total = jnp.sum(jnp.where(mine, product, 0.0), -1, keepdims=True)
            shift = jnp.where(lane == 2 * p + h, total, shift)
    shift = jnp.transpose(shift)
    for p in range(pairs):
        cols = slice(128 * p, 128 * p + 128)
        query = query_ref[:, cols] * jnp.asarray(HDIM**-0.5, BF)
        keys, values, dmixed = key_ref[:, cols], value_ref[:, cols], dmixed_ref[:, cols]
        dquery, dkeys, dvalues = [], [], []
        for h in range(2):
            mine = (lane < HDIM) if h == 0 else (lane >= HDIM)
            own_keys = jnp.where(mine, keys, jnp.zeros_like(keys))
            own_values = jnp.where(mine, values, jnp.zeros_like(values))
            i = 2 * p + h
            scores = dot(own_keys, query, NT)
            probs = jnp.where(causal, jnp.exp(scores - lse[first + i : first + i + 1]), 0.0)
            dprobs = dot(own_values, dmixed, NT)
            dscores = (probs * (dprobs - shift[i : i + 1])).astype(BF)
            dvalues.append(dot(probs.astype(BF), dmixed))
            dkeys.append(dot(dscores, query))
            dquery.append(dot(dscores, keys, TN))
        dquery = jnp.where(lane < HDIM, *dquery) * HDIM**-0.5
        parts = (dquery, jnp.where(lane < HDIM, *dkeys), jnp.where(lane < HDIM, *dvalues))
        for j, part in enumerate(parts):
            start = j * width + 128 * p
            dqkv_ref[:, start : start + 128] = part.astype(BF)
    grad = dot(act_ref[...], dqkv_ref[...]).astype(BF)
    rows = grad.shape[0] // 4
    places = [slice(0, 2 * rows), slice(2 * rows, 3 * rows), slice(3 * rows, 4 * rows)]
    for ref, place in zip((own_ref, send_ref, send_far_ref), places):
        ref[:, : 3 * width] = grad[place]
    if more_refs:
        order_ref, gain_grad_ref, turned_ref, score_ref = more_refs
        router_grad = dot(turned_ref[...], score_ref[...])
        column = jnp.transpose(jnp.broadcast_to(gain_grad_ref[...], (128, 4 * rows)))
        more = jnp.where(lane == 0, column, router_grad).astype(BF)
        more = dot(order_matrix(order_ref), more).astype(BF)
        for ref, place in zip((own_ref, send_ref, send_far_ref), places):
            ref[:, 3 * width :] = more[place]


def back_heads(group, qkv, dmixed, mixed, lse, act, after, *more):
    width, tok = act.shape
    cols = width // GROUPS
    block = lambda j: pl.BlockSpec((tok, cols), lambda i: (0, j))
    whole = lambda *s: pl.BlockSpec(s, lambda i: (0,) * len(s))
    half = (width // 2, 3 * cols + (128 if more else 0))
    quarter = (width // 4, half[1])
    return pl.pallas_call(
        functools.partial(back_heads_body, group * HEADS // GROUPS),
        grid=(1,),
        in_specs=[
            block(group),
            block(GROUPS + group),
            block(2 * GROUPS + group),
            block(group),
            block(group),
            whole(tok, 128),
            whole(width, tok),
            ANY,
        ]
        + [whole(*a.shape) for a in more],
        out_specs=[whole(tok, 3 * cols), whole(*half), whole(*quarter), whole(*quarter)],
        out_shape=[out((tok, 3 * cols), BF), out(half, BF), out(quarter, BF), out(quarter, BF)],
        compiler_params=params(52),
        cost_estimate=cost(1e6, 1e5),
    )(qkv, qkv, qkv, dmixed, mixed, lse, act, after, *more)


def back_in_body(*refs):
    number = 3 * GROUPS
    part_refs, weight_refs = refs[:GROUPS], refs[GROUPS : GROUPS + number]
    tok_ref, gain_ref, dresid_ref, _, out_ref = refs[GROUPS + number :]
    cols = part_refs[0].shape[1] // 3
    grad = sum(
        dot(part_refs[k // 3][:, k % 3 * cols : (k % 3 + 1) * cols], ref[...], NT)
        for k, ref in enumerate(weight_refs)
    )
    gain = as_row(gain_ref)
    normed, inverse, _ = norm(tok_ref[...].astype(F32), gain)
    out_ref[...] = dresid_ref[...] + norm_pull(grad * gain, normed, inverse)


def back_in(dqkv, wqkv, tokens, gain, dresid, after):
    tok, width = tokens.shape
    cols = width // GROUPS
    whole = lambda *s: pl.BlockSpec(s, lambda i: (0,) * len(s))
    weights = [
        pl.BlockSpec((width, cols), lambda i, j=j, g=g: (0, j * GROUPS + g))
        for g in range(GROUPS)
        for j in range(3)
    ]
    return pl.pallas_call(
        back_in_body,
        grid=(1,),
        in_specs=[whole(*part.shape) for part in dqkv]
        + weights
        + [whole(*a.shape) for a in (tokens, gain, dresid)]
        + [ANY],
        out_specs=whole(tok, width),
        out_shape=out((tok, width), F32),
        compiler_params=params(52),
        cost_estimate=cost(1e6, 1e5),
    )(*dqkv, *[wqkv] * len(weights), tokens, gain, dresid, after)


def side_by_side(groups, out_ref):
    start = 0
    for group in groups:
        place = slice(start, start + group[0].shape[1])
        start = place.stop
        out_ref[:, place] = sum(ref[...].astype(F32) for ref in group).astype(BF)


def core_sum_body(number, *refs):
    side_by_side(list(zip(refs[:number], refs[number : 2 * number])), refs[-1])


def half_rows(part, i):
    rows, cols = part.shape
    return pl.BlockSpec((rows // 2, cols), lambda g: (i, 0))


def core_sum(own, received, after):
    rows = own[0].shape[0] // 2
    cols = sum(part.shape[1] for part in own)
    whole = pl.BlockSpec((rows, cols), lambda g: (0, 0))
    return pl.pallas_call(
        functools.partial(core_sum_body, len(own)),
        grid=(1,),
        in_specs=[half_rows(part, 1) for part in own]
        + [pl.BlockSpec(part.shape, lambda g: (0, 0)) for part in received]
        + [ANY],
        out_specs=whole,
        out_shape=out((rows, cols), BF),
        compiler_params=params(52),
        cost_estimate=cost(1e6, 1e5),
    )(*own, *received, after)


def pair_sum_body(number, *refs):
    *refs, far_ref, _, out_ref = refs
    start = 0
    groups = []
    for own_ref, received_ref in zip(refs[:number], refs[number:]):
        end = start + own_ref.shape[1]
        groups.append((own_ref, received_ref, far_ref.at[:, start:end]))
        start = end
    side_by_side(groups, out_ref)


def pair_sum(own, received, far, after):
    whole = pl.BlockSpec(far.shape, lambda g: (0, 0))
    return pl.pallas_call(
        functools.partial(pair_sum_body, len(own)),
        grid=(1,),
        in_specs=[half_rows(part, 0) for part in own]
        + [pl.BlockSpec(part.shape, lambda g: (0, 0)) for part in received]
        + [whole, ANY],
        out_specs=whole,
        out_shape=out(far.shape, BF),
        compiler_params=params(52),
        cost_estimate=cost(1e6, 1e5),
    )(*own, *received, far, after)


def split_sum_body(index_ref, own_ref, received_ref, far_ref, _, *out_refs):
    for d, ref in enumerate(out_refs):
        place = jnp.bitwise_xor(index_ref[3], d)
        parts = (own_ref, received_ref, far_ref)
        ref[...] = sum(part[place].astype(F32) for part in parts).astype(BF)


def split_sum(ids, own, received, far, after, nz):
    rows, cols = far.shape
    shape = (nz, rows // nz, cols)
    whole = pl.BlockSpec(shape, lambda g: (0, 0, 0))
    return pl.pallas_call(
        split_sum_body,
        grid=(1,),
        in_specs=[SMEM, whole, whole, whole, ANY],
        out_specs=[pl.BlockSpec(shape[1:], lambda g: (0, 0))] * nz,
        out_shape=[out(shape[1:], BF)] * nz,
        compiler_params=params(52),
        cost_estimate=cost(1e6, 1e5),
    )(ids, own.reshape(2 * nz, *shape[1:]), received.reshape(shape), far.reshape(shape), after)


def z_parts_body(ny, number, *refs):
    part_refs, (_, *out_refs) = refs[:number], refs[number:]
    total = sum(ref[...].astype(F32) for ref in part_refs)
    rows = total.shape[0] // ny
    for j, ref in enumerate(out_refs):
        ref[...] = total[j * rows : (j + 1) * rows].astype(ref.dtype)


def z_parts(parts, ny, after):
    rows, cols = parts[0].shape
    shape = (rows // ny, cols)
    return pl.pallas_call(
        functools.partial(z_parts_body, ny, len(parts)),
        in_specs=[VMEM] * len(parts) + [ANY],
        out_specs=[VMEM] * ny,
        out_shape=[out(shape, F32)] + [out(shape, BF)] * (ny - 1),
        compiler_params=params(52),
        cost_estimate=cost(1e6, 1e5),
    )(*parts, after)


def z_sum_body(blocks_ref, _, near_ref, *far_refs):
    near_ref[...] = jnp.sum(blocks_ref[:, 0].astype(F32), 0)
    for j, ref in enumerate(far_refs):
        ref[...] = jnp.sum(blocks_ref[:, j + 1].astype(F32), 0).astype(BF)


def z_sum(blocks, after):
    _, ny, rows, cols = blocks.shape
    return pl.pallas_call(
        z_sum_body,
        in_specs=[VMEM, ANY],
        out_specs=[VMEM] * ny,
        out_shape=[out((rows, cols), F32)] + [out((rows, cols), BF)] * (ny - 1),
        compiler_params=params(52),
        cost_estimate=cost(blocks.size, blocks.size),
    )(blocks, after)


def finish_body(ny, weight_ref, gain_ref, *refs):
    part_refs, refs = refs[: 2 * ny], refs[2 * ny + 1 :]
    grad_ref, out_ref, router_ref, gain1_ref, gain2_ref = refs
    rows, width = out_ref.shape
    cols = width // GROUPS
    first, second = (
        sum(ref[...].astype(F32) for ref in part_refs[i : i + ny]) for i in (0, ny)
    )
    out_ref[...] = first[:, :width]
    extra = second[:, 3 * cols :]
    experts = router_ref.shape[0]
    groups = [first[:, width:], second]
    gain_grad = 0.0
    for g, total in enumerate(groups):
        for j in range(3):
            piece = total[:, j * cols : (j + 1) * cols]
            place = slice((j * GROUPS + g) * cols, (j * GROUPS + g + 1) * cols)
            grad_ref[:, place] = piece
            weight = weight_ref[:, place].astype(F32)
            gain_grad += jnp.sum(piece * weight, -1, keepdims=True)
    lane = lax.broadcasted_iota(jnp.int32, (rows, 128), 1)
    turned = jnp.transpose(jnp.where(lane == experts + 1, gain_grad / gain_ref[...], extra))
    gain2_ref[...] = turned[:1]
    router_ref[...] = turned[1 : experts + 1]
    gain1_ref[...] = turned[experts + 1 : experts + 2]


def finish(weight, gain, first, second, experts, after):
    rows, width = weight.shape
    return pl.pallas_call(
        functools.partial(finish_body, len(first)),
        in_specs=[VMEM] * (2 + len(first) + len(second)) + [ANY],
        out_specs=[VMEM] * 5,
        out_shape=[
            out((rows, width), F32),
            out((rows, width // 3), F32),
            out((experts, rows), F32),
            out((1, rows), F32),
            out((1, rows), F32),
        ],
        compiler_params=params(52),
        cost_estimate=cost(first[0].size, 4 * first[0].size),
    )(weight, gain, *first, *second, after)


def per_device(
    sizes,
    tokens,
    cotangent,
    norm1_gain,
    qkv_weight,
    out_weight,
    norm2_gain,
    router_weight,
    up_weight,
    down_weight,
    routes,
    capacity,
):
    n_dp, n_ex = sizes
    ny = n_dp // 2
    tok, width = tokens.shape
    experts = router_weight.shape[1]
    cap = 3 * tok // (4 * experts)
    dp = lax.axis_index("dp")
    ex = lax.axis_index("expert")
    ids = jnp.stack([dp // 2, dp % 2, ex, ex // 2]).astype(jnp.int32)
    gain1, gain2 = norm1_gain, norm2_gain
    router = lax.dynamic_slice(router_weight, (0, ex), (width, 1)).reshape(1, width)
    up, down = up_weight[0], down_weight[0]
    rows_dev = width // (n_dp * n_ex)
    start = (dp * n_ex + ex) * rows_dev
    weight_rows = lax.dynamic_slice(qkv_weight, (start, 0), (rows_dev, 3 * width))
    gain_rows = lax.dynamic_slice(norm1_gain, (start,), (rows_dev,)).reshape(rows_dev, 1)
    nz = n_ex // 2
    row = jnp.arange(width, dtype=jnp.int32)
    chunk = row // rows_dev
    y, core, z, x = chunk // (2 * n_ex), chunk // n_ex % 2, chunk // 2 % nz, chunk % 2
    order = ((core ^ (dp % 2)) * 2 + (x ^ (ex % 2))) * nz + z
    order = ((order * ny + (y ^ (dp // 2))) * rows_dev + row % rows_dev).reshape(1, width)

    z_groups = [list(range(0, n_ex, 2)), list(range(1, n_ex, 2))]

    def exchange(value):
        return lax.all_to_all(value, "expert", split_axis=0, concat_axis=0, tiled=True)

    def exchange_z(value):
        return lax.all_to_all(
            value, "expert", split_axis=0, concat_axis=0, tiled=True, axis_index_groups=z_groups
        )

    def to_core(value):
        return lax.ppermute(value, "dp", [(i, i ^ 1) for i in range(n_dp)])

    def to_y(values):
        return [
            lax.ppermute(values[j - 1], "dp", [(i, i ^ (2 * j)) for i in range(n_dp)])
            for j in range(1, ny)
        ]

    def to_core_all(values):
        return [to_core(value) for value in values]

    def to_x(value):
        return lax.ppermute(value, "expert", [(i, i ^ 1) for i in range(n_ex)])

    def sum_z(blocks, after):
        near, *far = z_sum(blocks.reshape(nz, ny, rows_dev, blocks.shape[1]), after)
        return [near] + to_y(far)

    slot, cots = plan(routes, capacity, cotangent, cap)
    cots = exchange(cots)
    act, qkv, mixed, lse, resid, first, second = attend(
        tokens, gain1, qkv_weight, out_weight, gain2, slot, experts * cap
    )
    first, cots = lax.optimization_barrier((first, cots))
    first = exchange(first)
    act, mixed_turned = turn(order, act, mixed)
    first, order, weight_rows, gain_rows, second, act, mixed_turned, ids = lax.optimization_barrier(
        (first, order, weight_rows, gain_rows, second, act, mixed_turned, ids)
    )
    second = exchange(second)
    first, *kept = expert(ids, first, cots, router, up, down, None)
    first = exchange(first)
    second, gated, *kept = expert(ids, second, cots, router, up, down, kept)
    second = exchange(second)

    far_send, near_send, far_own, near_own = expert_grads(kept, ids, ny, first)
    second, gated = lax.optimization_barrier((second, gated))
    gated = exchange(gated)

    dresid, dmixed, gain2_row, own, *sent = back_out(
        first, second, slot, resid, cotangent, gain2, out_weight, mixed_turned, near_own
    )
    part1, own1, *sent1 = back_heads(0, qkv, dmixed, mixed, lse, act, ids)
    far_own, own1 = lax.optimization_barrier((far_own, own1))
    grads_far = far_grads(far_own, to_core(far_send), ids)
    grads_y = to_y(grads_far)
    near1, far1 = zip(to_core_all(sent), to_core_all(sent1))
    near1, far1 = lax.optimization_barrier((near1, far1))
    own1 = [own, own1]
    far1 = core_sum(own1, far1, grads_far)
    part2, own2, *sent2 = back_heads(
        1, qkv, dmixed, mixed, lse, act, far1, order, gain2_row, kept[2], kept[4]
    )
    far1 = to_x(far1)
    near2, far2 = to_core_all(sent2)
    block_out = combine(slot, resid, gated, part2)
    far2 = core_sum([own2], [far2], block_out)
    total1 = pair_sum(own1, near1, far1, far2)
    far2 = to_x(far2)
    blocks1 = exchange_z(total1)
    tokens_grad = back_in([part1, part2], qkv_weight, tokens, gain1, dresid, total1)
    own, *sent = split_sum(ids, own2, near2, far2, tokens_grad, nz)
    parts = [own] + [
        lax.ppermute(value, "expert", [(i, i ^ (2 * d + 2)) for i in range(n_ex)])
        for d, value in enumerate(sent)
    ]
    up_grad, down_grad = near_grads(near_own, to_core(near_send), grads_y, own)
    near, *far = z_parts(parts, ny, up_grad)
    second = [near] + to_y(far)
    first = sum_z(blocks1, near)
    qkv_grad, out_grad, router_grad, gain1_grad, gain2_grad = finish(
        weight_rows, gain_rows, first, second, experts, up_grad
    )
    return (
        block_out,
        tokens_grad,
        gain1_grad[0],
        qkv_grad,
        out_grad,
        gain2_grad[0],
        router_grad.T,
        up_grad[None],
        down_grad[None],
    )


def solution(mesh):
    sizes = (mesh.shape["dp"], mesh.shape["expert"])
    return jax.shard_map(
        functools.partial(per_device, sizes),
        mesh=mesh,
        in_specs=(
            P(("dp", "expert"), None),
            P(("dp", "expert"), None),
            P(),
            P(),
            P(),
            P(),
            P(),
            P("expert", None, None),
            P("expert", None, None),
            P(("dp", "expert")),
            P(),
        ),
        out_specs=(
            P(("dp", "expert"), None),
            P(("dp", "expert"), None),
            P(("dp", "expert")),
            P(("dp", "expert"), None),
            P(("dp", "expert"), None),
            P(("dp", "expert")),
            P(("dp", "expert"), None),
            P("expert", None, "dp"),
            P("expert", "dp", None),
        ),
        check_vma=False,
    )
```

```python
import functools

import jax
import jax.numpy as jnp
from jax import lax
from jax.experimental import pallas as pl
from jax.experimental.pallas import tpu as pltpu
from jax.sharding import PartitionSpec as P

HEADS = 12
HDIM = 64
EPS = 1e-05
F32 = jnp.float32
BF = jnp.bfloat16
NT = (((1,), (1,)), ((), ()))
TN = (((0,), (0,)), ((), ()))
MIB = 2**20
VMEM = pl.BlockSpec(memory_space=pltpu.VMEM)
SMEM = pl.BlockSpec(memory_space=pltpu.SMEM)
GROUPS = 2
SCALE = 1
LIMIT = 52
ANY = pl.BlockSpec(memory_space=pltpu.HBM)


def out(shape, dtype):
    return jax.ShapeDtypeStruct(shape, dtype)


def params(mib=LIMIT):
    return pltpu.CompilerParams(vmem_limit_bytes=mib * MIB)


def cost(flops, nbytes):
    return pl.CostEstimate(
        flops=int(flops / SCALE), bytes_accessed=int(nbytes / SCALE), transcendentals=0
    )


def dot(a, b, dims=None):
    if dims is None:
        return jnp.dot(a, b, preferred_element_type=F32)
    return lax.dot_general(a, b, dims, preferred_element_type=F32)


def norm(value, gain):
    center = value - jnp.mean(value, -1, keepdims=True)
    inverse = lax.rsqrt(jnp.mean(center * center, -1, keepdims=True) + EPS)
    normed = center * inverse
    return normed, inverse, normed * gain


def as_row(ref):
    return ref[...].reshape(1, ref.shape[0])


def norm_pull(scaled, normed, inverse):
    return inverse * (
        scaled
        - jnp.mean(scaled, -1, keepdims=True)
        - normed * jnp.mean(scaled * normed, -1, keepdims=True)
    )


def slot_matrix(slot, slots):
    ids = lax.broadcasted_iota(jnp.int32, (slots, slot.shape[1]), 0)
    return jnp.where(ids == slot, 1.0, 0.0).astype(BF)


def plan_body(cap, cap_ref, routes_ref, cot_ref, slot_ref, send_ref):
    experts = cap_ref.shape[0]
    tok, width = cot_ref.shape
    count = experts * cap
    ids = lax.broadcasted_iota(jnp.int32, (experts, tok), 0)
    hot = routes_ref[...] == ids
    limit = jnp.zeros((experts, tok), F32)
    for e in range(experts):
        limit = jnp.where(ids == e, cap_ref[e].astype(F32), limit)
    before = lax.broadcasted_iota(jnp.int32, (tok, tok), 0) < lax.broadcasted_iota(
        jnp.int32, (tok, tok), 1
    )
    position = dot(
        jnp.where(hot, 1.0, 0.0).astype(BF), jnp.where(before, 1.0, 0.0).astype(BF)
    )
    kept = jnp.logical_and(hot, position < limit)
    number = position + (ids * cap).astype(F32) + 1.0
    number += jnp.where(position < cap, 0.0, float(count - cap))
    slot = (jnp.sum(jnp.where(kept, number, 0.0), 0, keepdims=True) - 1.0).astype(jnp.int32)
    slot_ref[...] = slot
    rows = dot(slot_matrix(slot, 2 * count), cot_ref[...]).astype(BF)
    send_ref[:, :width] = rows[:count]
    send_ref[:, width:] = rows[count:]


def plan(routes, capacity, cotangent, cap):
    tok, width = cotangent.shape
    count = capacity.shape[0] * cap
    return pl.pallas_call(
        functools.partial(plan_body, cap),
        in_specs=[SMEM, VMEM, VMEM],
        out_specs=[VMEM] * 2,
        out_shape=[out((1, tok), jnp.int32), out((count, 2 * width), BF)],
        compiler_params=params(63),
        cost_estimate=cost(4 * count * tok * width, 8 * count * width),
    )(capacity, routes.reshape(1, tok), cotangent)


def attend_body(
    tok_ref,
    gain1_ref,
    wqkv_ref,
    wout_ref,
    gain2_ref,
    slot_ref,
    act_ref,
    qkv_ref,
    mixed_ref,
    lse_ref,
    resid_ref,
    first_ref,
    second_ref,
):
    tok, width = tok_ref.shape
    inputs = tok_ref[...].astype(F32)
    act = norm(inputs, as_row(gain1_ref))[2].astype(BF)
    act_ref[...] = act
    for j in range(3):
        cols = pl.ds(j * width, width)
        qkv_ref[:, cols] = dot(act, wqkv_ref[:, cols]).astype(BF)
    lane = lax.broadcasted_iota(jnp.int32, (1, 128), 1)
    causal = lax.broadcasted_iota(jnp.int32, (tok, tok), 0) >= lax.broadcasted_iota(
        jnp.int32, (tok, tok), 1
    )
    lse = jnp.zeros((tok, 128), F32)
    for p in range(HEADS // 2):
        query = qkv_ref[:, 128 * p : 128 * p + 128] * jnp.asarray(HDIM**-0.5, BF)
        keys = qkv_ref[:, width + 128 * p : width + 128 * p + 128]
        values = qkv_ref[:, 2 * width + 128 * p : 2 * width + 128 * p + 128]
        parts = []
        for h in range(2):
            mine = (lane < HDIM) if h == 0 else (lane >= HDIM)
            scores = dot(jnp.where(mine, query, jnp.zeros_like(query)), keys, NT)
            scores = jnp.where(causal, scores, -1e30)
            top = jnp.max(scores, -1, keepdims=True)
            expo = jnp.exp(scores - top)
            total = jnp.sum(expo, -1, keepdims=True)
            parts.append(dot(expo.astype(BF), values) * (1.0 / total))
            lse = jnp.where(lane == 2 * p + h, top + jnp.log(total), lse)
        mixed_ref[:, 128 * p : 128 * p + 128] = jnp.where(lane < HDIM, *parts).astype(BF)
    lse_ref[...] = lse
    resid = inputs + dot(mixed_ref[...], wout_ref[...])
    resid_ref[...] = resid
    rows = norm(resid, as_row(gain2_ref))[2].astype(BF)
    count = first_ref.shape[0]
    send = dot(slot_matrix(slot_ref[...], 2 * count), rows).astype(BF)
    first_ref[...] = send[:count]
    second_ref[...] = send[count:]


def attend(tokens, gain1, wqkv, wout, gain2, slot, count):
    tok, width = tokens.shape
    return pl.pallas_call(
        attend_body,
        in_specs=[VMEM] * 6,
        out_specs=[VMEM] * 7,
        out_shape=[
            out((tok, width), BF),
            out((tok, 3 * width), BF),
            out((tok, width), BF),
            out((tok, 128), F32),
            out((tok, width), F32),
            out((count, width), BF),
            out((count, width), BF),
        ],
        compiler_params=params(63),
        cost_estimate=cost(12e9, 12e6),
    )(tokens, gain1, wqkv, wout, gain2, slot)


def turn_body(order_ref, act_ref, mixed_ref, act_turned_ref, mixed_turned_ref):
    order = order_matrix(order_ref)
    act_turned_ref[...] = dot(order, act_ref[...], NT).astype(BF)
    mixed_turned_ref[...] = dot(order, mixed_ref[...], NT).astype(BF)


def order_matrix(order_ref):
    width = order_ref.shape[1]
    ids = lax.broadcasted_iota(jnp.int32, (width, width), 0)
    return jnp.where(ids == order_ref[...], 1.0, 0.0).astype(BF)


def turn(order, act, mixed):
    tok, width = act.shape
    return pl.pallas_call(
        turn_body,
        in_specs=[VMEM] * 3,
        out_specs=[VMEM] * 2,
        out_shape=[out((width, tok), BF)] * 2,
        compiler_params=params(63),
        cost_estimate=cost(4 * tok * width * width, 8 * tok * width),
    )(order, act, mixed)


def expert_body(
    steps,
    ids_ref,
    rows_ref,
    cot_ref,
    router_ref,
    up_ref,
    down_ref,
    put,
    hid_ref,
    du_ref,
    rows_turned_ref,
    dy_turned_ref,
    dscore_ref,
    dy_ref,
    sum_ref,
    grad_ref,
    gate_ref,
):
    step = pl.program_id(0)

    @pl.when(step == 0)
    def _():
        score = jnp.sum(rows_ref[...].astype(F32) * router_ref[...], -1, keepdims=True)
        gate = jax.nn.sigmoid(score)
        gate_ref[...] = gate
        dy = (cot_ref[...].astype(F32) * gate).astype(BF)
        dy_ref[...] = dy
        rows_turned_ref[...] = jnp.transpose(rows_ref[...])
        dy_turned_ref[...] = jnp.transpose(dy)

    upper = dot(rows_ref[...], up_ref[...])
    hidden_grad = dot(dy_ref[...], down_ref[...], NT)
    cdf = 0.5 + 0.5 * lax.erf(upper * 0.7071067811865476)
    density = jnp.exp(-0.5 * upper * upper) * 0.3989422804014327
    hidden = (upper * cdf).astype(BF)
    upper_grad = (hidden_grad * (cdf + upper * density)).astype(BF)
    hid_ref[...] = hidden
    du_ref[...] = upper_grad
    part = dot(hidden, down_ref[...])
    part_grad = dot(upper_grad, up_ref[...], NT)

    @pl.when(step == 0)
    def _():
        sum_ref[...] = part
        grad_ref[...] = part_grad

    @pl.when(step > 0)
    def _():
        sum_ref[...] += part
        grad_ref[...] += part_grad

    @pl.when(step == steps - 1)
    def _():
        gate = gate_ref[...]
        gated = sum_ref[...] * gate
        dscore = jnp.sum(cot_ref[...].astype(F32) * gated, -1, keepdims=True) * (1.0 - gate)
        put(grad_ref[...] + dscore * router_ref[...], gated)
        lane = lax.broadcasted_iota(jnp.int32, dscore_ref.shape, 1)
        dscore_ref[...] = jnp.where(lane == ids_ref[2] + 1, dscore, 0.0).astype(BF)


def batch_body(first, steps, *refs):
    *ins, back_ref, gated_ref = refs[: (8 if first else 14)]

    def put(back, gated):
        back_ref[...] = back.astype(BF)
        gated_ref[...] = gated.astype(BF)

    expert_body(steps, *ins[:6], put, *refs[8 if first else 14 :])


def expert(ids, rows, cots, router, up, down, kept):
    i = 0 if kept is None else 1
    width, hidden = up.shape
    tile = 768
    steps = hidden // tile
    count = rows.shape[0]
    whole = lambda *s: pl.BlockSpec(s, lambda f: (0,) * len(s))
    side = pl.BlockSpec((count, width), lambda f: (0, i))
    tiles = pl.BlockSpec((count, tile), lambda f: (i, f))
    turned = pl.BlockSpec((width, count), lambda f: (0, i))
    return pl.pallas_call(
        functools.partial(batch_body, kept is None, steps),
        grid=(steps,),
        in_specs=[
            SMEM,
            whole(count, width),
            side,
            whole(1, width),
            pl.BlockSpec((width, tile), lambda f: (0, f)),
            pl.BlockSpec((tile, width), lambda f: (f, 0)),
        ]
        + [ANY] * (6 * i),
        out_specs=[
            whole(count, width),
            side,
            tiles,
            tiles,
            turned,
            turned,
            pl.BlockSpec((count, 128), lambda f: (i, 0)),
        ],
        out_shape=[
            out((count, width), BF),
            out((count, 2 * width), BF),
            out((2 * count, hidden), BF),
            out((2 * count, hidden), BF),
            out((width, 2 * count), BF),
            out((width, 2 * count), BF),
            out((2 * count, 128), BF),
        ],
        scratch_shapes=[
            pltpu.VMEM((count, width), BF),
            pltpu.VMEM((count, width), F32),
            pltpu.VMEM((count, width), F32),
            pltpu.VMEM((count, 1), F32),
        ],
        input_output_aliases={6 + j: 1 + j for j in range(6 * i)},
        compiler_params=params(63),
        cost_estimate=cost(8 * count * width * hidden, 10 * width * hidden),
    )(ids, rows, cots, router, up, down, *(kept or ()))


def expert_grads_body(ny, ids_ref, turned_ref, du_ref, hid_ref, dy_ref, _, *refs):
    step = pl.program_id(0)
    up = dot(turned_ref[...], du_ref[...]).astype(BF)
    down = dot(dy_ref[...], hid_ref[...]).astype(BF)
    ends = (0, ny - 1, ny, 2 * ny - 1, 2 * ny)
    for ref, start, end in zip(refs, ends, ends[1:]):

        @pl.when(jnp.logical_and(step >= start, step < end))
        def _(ref=ref):
            ref[0, 0] = up
            ref[0, 1] = down


def expert_grads(kept, ids, ny, after):
    hid, du, rows, dy, _ = kept
    count, hidden = hid.shape
    width = rows.shape[0]
    part = hidden // (2 * ny)

    def chunk(s, ids):
        core = jnp.where(s < ny, 1 - ids[1], ids[1])
        away = jnp.where(s < ny, s, s - ny) + 1
        return jnp.bitwise_xor(jnp.where(away == ny, 0, away), ids[0]) * 2 + core

    whole = lambda *shape: pl.BlockSpec(shape, lambda s, ids: (0, 0))
    cols = pl.BlockSpec((count, part), lambda s, ids: (0, chunk(s, ids)))

    def block(start, number):
        return pl.BlockSpec(
            (1, 2, width, part), lambda s, ids: (jnp.clip(s - start, 0, number - 1), 0, 0, 0)
        )

    far, near = out((ny - 1, 2, width, part), BF), out((1, 2, width, part), BF)
    return pl.pallas_call(
        functools.partial(expert_grads_body, ny),
        grid_spec=pltpu.PrefetchScalarGridSpec(
            num_scalar_prefetch=1,
            grid=(2 * ny,),
            in_specs=[whole(width, count), cols, cols, whole(width, count), ANY],
            out_specs=[
                block(0, ny - 1),
                block(ny - 1, 1),
                block(ny, ny - 1),
                block(2 * ny - 1, 1),
            ],
        ),
        out_shape=[far, near, far, near],
        compiler_params=params(63),
        cost_estimate=cost(1e6, 1e5),
    )(ids, rows, du, hid, dy, after)


def far_grads_body(own_ref, received_ref, _, out_ref):
    out_ref[...] = (own_ref[...].astype(F32) + received_ref[...].astype(F32)).astype(BF)


def far_grads(own, received, after):
    number, _, width, part = own.shape
    tall = width // 2
    block = pl.BlockSpec((1, 2, tall, part), lambda j, r: (j, 0, r, 0))
    return pl.pallas_call(
        far_grads_body,
        grid=(number, 2),
        in_specs=[block, block, ANY],
        out_specs=block,
        out_shape=out(own.shape, BF),
        compiler_params=params(52),
        cost_estimate=cost(1e6, 1e5),
    )(own, received, after)


def near_grads_body(own_ref, received_ref, *refs):
    parts, (_, up_ref, down_ref) = refs[:-3], refs[-3:]
    total = own_ref[0].astype(F32) + received_ref[0].astype(F32)
    for ref in parts:
        total = total + ref[...].astype(F32)
    up_ref[...] = total[0]
    down_ref[...] = jnp.transpose(total[1])


def near_grads(own, received, parts, after):
    _, _, width, part = own.shape
    tall = 384
    first = pl.BlockSpec((1, 2, tall, part), lambda j: (0, 0, j, 0))
    return pl.pallas_call(
        near_grads_body,
        grid=(width // tall,),
        in_specs=[first, first]
        + [pl.BlockSpec((2, tall, part), lambda j: (0, j, 0))] * len(parts)
        + [ANY],
        out_specs=[
            pl.BlockSpec((tall, part), lambda j: (j, 0)),
            pl.BlockSpec((part, tall), lambda j: (0, j)),
        ],
        out_shape=[out((width, part), F32), out((part, width), F32)],
        compiler_params=params(52),
        cost_estimate=cost(own.size, 3 * own.size),
    )(own, received, *parts, after)


def gather_rows(slot_ref, first, second):
    count = first.shape[0]
    select = slot_matrix(slot_ref[...], 2 * count)
    return dot(select[:count], first, TN) + dot(select[count:], second, TN)


def combine_body(slot_ref, resid_ref, rows_ref, _, out_ref):
    width = resid_ref.shape[1]
    rows = gather_rows(slot_ref, rows_ref[:, :width], rows_ref[:, width:])
    out_ref[...] = (resid_ref[...] + rows).astype(BF)


def combine(slot, resid, rows, after):
    return pl.pallas_call(
        combine_body,
        in_specs=[VMEM] * 3 + [ANY],
        out_specs=VMEM,
        out_shape=out(resid.shape, BF),
        compiler_params=params(52),
        cost_estimate=cost(1e6, 1e5),
    )(slot, resid, rows, after)


def back_out_body(
    first_ref,
    second_ref,
    slot_ref,
    resid_ref,
    cot_ref,
    gain_ref,
    wout_ref,
    mixed_ref,
    _,
    dresid_ref,
    dmixed_ref,
    gain_grad_ref,
    own_ref,
    send_ref,
    send_far_ref,
):
    width = first_ref.shape[1]
    grad = gather_rows(slot_ref, first_ref[...], second_ref[...])
    gain = as_row(gain_ref)
    normed, inverse, _ = norm(resid_ref[...], gain)
    gain_grad_ref[...] = jnp.sum(grad * normed, 0, keepdims=True)
    dresid = cot_ref[...].astype(F32) + norm_pull(grad * gain, normed, inverse)
    dresid_ref[...] = dresid
    low = dresid.astype(BF)
    dmixed_ref[...] = dot(low, wout_ref[...], NT).astype(BF)
    weight_grad = dot(mixed_ref[...], low).astype(BF)
    rows = width // 4
    own_ref[...] = weight_grad[: 2 * rows]
    send_ref[...] = weight_grad[2 * rows : 3 * rows]
    send_far_ref[...] = weight_grad[3 * rows :]


def back_out(first, second, slot, resid, cot, gain, wout, mixed, after):
    tok, width = cot.shape
    quarter = out((width // 4, width), BF)
    return pl.pallas_call(
        back_out_body,
        in_specs=[VMEM] * 8 + [ANY],
        out_specs=[VMEM] * 6,
        out_shape=[
            out((tok, width), F32),
            out((tok, width), BF),
            out((1, width), F32),
            out((width // 2, width), BF),
            quarter,
            quarter,
        ],
        compiler_params=params(52),
        cost_estimate=cost(30e9, 8e6),
    )(first, second, slot, resid, cot, gain, wout, mixed, after)


def back_heads_body(
    first,
    query_ref,
    key_ref,
    value_ref,
    dmixed_ref,
    mixed_ref,
    lse_ref,
    act_ref,
    _,
    *refs,
):
    *more_refs, dqkv_ref, own_ref, send_ref, send_far_ref = refs
    tok, width = query_ref.shape
    pairs = width // 128
    lane = lax.broadcasted_iota(jnp.int32, (1, 128), 1)
    causal = lax.broadcasted_iota(jnp.int32, (tok, tok), 1) >= lax.broadcasted_iota(
        jnp.int32, (tok, tok), 0
    )
    lse = jnp.transpose(lse_ref[...])
    shift = jnp.zeros((tok, 128), F32)
    for p in range(pairs):
        cols = slice(128 * p, 128 * p + 128)
        product = dmixed_ref[:, cols].astype(F32) * mixed_ref[:, cols].astype(F32)
        for h in range(2):
            mine = (lane < HDIM) if h == 0 else (lane >= HDIM)
            total = jnp.sum(jnp.where(mine, product, 0.0), -1, keepdims=True)
            shift = jnp.where(lane == 2 * p + h, total, shift)
    shift = jnp.transpose(shift)
    for p in range(pairs):
        cols = slice(128 * p, 128 * p + 128)
        query = query_ref[:, cols] * jnp.asarray(HDIM**-0.5, BF)
        keys, values, dmixed = key_ref[:, cols], value_ref[:, cols], dmixed_ref[:, cols]
        dquery, dkeys, dvalues = [], [], []
        for h in range(2):
            mine = (lane < HDIM) if h == 0 else (lane >= HDIM)
            own_keys = jnp.where(mine, keys, jnp.zeros_like(keys))
            own_values = jnp.where(mine, values, jnp.zeros_like(values))
            i = 2 * p + h
            scores = dot(own_keys, query, NT)
            probs = jnp.where(causal, jnp.exp(scores - lse[first + i : first + i + 1]), 0.0)
            dprobs = dot(own_values, dmixed, NT)
            dscores = (probs * (dprobs - shift[i : i + 1])).astype(BF)
            dvalues.append(dot(probs.astype(BF), dmixed))
            dkeys.append(dot(dscores, query))
            dquery.append(dot(dscores, keys, TN))
        dquery = jnp.where(lane < HDIM, *dquery) * HDIM**-0.5
        parts = (dquery, jnp.where(lane < HDIM, *dkeys), jnp.where(lane < HDIM, *dvalues))
        for j, part in enumerate(parts):
            start = j * width + 128 * p
            dqkv_ref[:, start : start + 128] = part.astype(BF)
    grad = dot(act_ref[...], dqkv_ref[...]).astype(BF)
    rows = grad.shape[0] // 4
    places = [slice(0, 2 * rows), slice(2 * rows, 3 * rows), slice(3 * rows, 4 * rows)]
    for ref, place in zip((own_ref, send_ref, send_far_ref), places):
        ref[:, : 3 * width] = grad[place]
    if more_refs:
        order_ref, gain_grad_ref, turned_ref, score_ref = more_refs
        router_grad = dot(turned_ref[...], score_ref[...])
        column = jnp.transpose(jnp.broadcast_to(gain_grad_ref[...], (128, 4 * rows)))
        more = jnp.where(lane == 0, column, router_grad).astype(BF)
        more = dot(order_matrix(order_ref), more).astype(BF)
        for ref, place in zip((own_ref, send_ref, send_far_ref), places):
            ref[:, 3 * width :] = more[place]


def back_heads(group, qkv, dmixed, mixed, lse, act, after, *more):
    width, tok = act.shape
    cols = width // GROUPS
    block = lambda j: pl.BlockSpec((tok, cols), lambda i: (0, j))
    whole = lambda *s: pl.BlockSpec(s, lambda i: (0,) * len(s))
    half = (width // 2, 3 * cols + (128 if more else 0))
    quarter = (width // 4, half[1])
    return pl.pallas_call(
        functools.partial(back_heads_body, group * HEADS // GROUPS),
        grid=(1,),
        in_specs=[
            block(group),
            block(GROUPS + group),
            block(2 * GROUPS + group),
            block(group),
            block(group),
            whole(tok, 128),
            whole(width, tok),
            ANY,
        ]
        + [whole(*a.shape) for a in more],
        out_specs=[whole(tok, 3 * cols), whole(*half), whole(*quarter), whole(*quarter)],
        out_shape=[out((tok, 3 * cols), BF), out(half, BF), out(quarter, BF), out(quarter, BF)],
        compiler_params=params(52),
        cost_estimate=cost(1e6, 1e5),
    )(qkv, qkv, qkv, dmixed, mixed, lse, act, after, *more)


def back_in_body(*refs):
    number = 3 * GROUPS
    part_refs, weight_refs = refs[:GROUPS], refs[GROUPS : GROUPS + number]
    tok_ref, gain_ref, dresid_ref, _, out_ref = refs[GROUPS + number :]
    cols = part_refs[0].shape[1] // 3
    grad = sum(
        dot(part_refs[k // 3][:, k % 3 * cols : (k % 3 + 1) * cols], ref[...], NT)
        for k, ref in enumerate(weight_refs)
    )
    gain = as_row(gain_ref)
    normed, inverse, _ = norm(tok_ref[...].astype(F32), gain)
    out_ref[...] = dresid_ref[...] + norm_pull(grad * gain, normed, inverse)


def back_in(dqkv, wqkv, tokens, gain, dresid, after):
    tok, width = tokens.shape
    cols = width // GROUPS
    whole = lambda *s: pl.BlockSpec(s, lambda i: (0,) * len(s))
    weights = [
        pl.BlockSpec((width, cols), lambda i, j=j, g=g: (0, j * GROUPS + g))
        for g in range(GROUPS)
        for j in range(3)
    ]
    return pl.pallas_call(
        back_in_body,
        grid=(1,),
        in_specs=[whole(*part.shape) for part in dqkv]
        + weights
        + [whole(*a.shape) for a in (tokens, gain, dresid)]
        + [ANY],
        out_specs=whole(tok, width),
        out_shape=out((tok, width), F32),
        compiler_params=params(52),
        cost_estimate=cost(1e6, 1e5),
    )(*dqkv, *[wqkv] * len(weights), tokens, gain, dresid, after)


def side_by_side(groups, out_ref):
    start = 0
    for group in groups:
        place = slice(start, start + group[0].shape[1])
        start = place.stop
        out_ref[:, place] = sum(ref[...].astype(F32) for ref in group).astype(BF)


def core_sum_body(number, *refs):
    side_by_side(list(zip(refs[:number], refs[number : 2 * number])), refs[-1])


def half_rows(part, i):
    rows, cols = part.shape
    return pl.BlockSpec((rows // 2, cols), lambda g: (i, 0))


def core_sum(own, received, after):
    rows = own[0].shape[0] // 2
    cols = sum(part.shape[1] for part in own)
    whole = pl.BlockSpec((rows, cols), lambda g: (0, 0))
    return pl.pallas_call(
        functools.partial(core_sum_body, len(own)),
        grid=(1,),
        in_specs=[half_rows(part, 1) for part in own]
        + [pl.BlockSpec(part.shape, lambda g: (0, 0)) for part in received]
        + [ANY],
        out_specs=whole,
        out_shape=out((rows, cols), BF),
        compiler_params=params(52),
        cost_estimate=cost(1e6, 1e5),
    )(*own, *received, after)


def pair_sum_body(number, *refs):
    *refs, far_ref, _, out_ref = refs
    start = 0
    groups = []
    for own_ref, received_ref in zip(refs[:number], refs[number:]):
        end = start + own_ref.shape[1]
        groups.append((own_ref, received_ref, far_ref.at[:, start:end]))
        start = end
    side_by_side(groups, out_ref)


def pair_sum(own, received, far, after):
    whole = pl.BlockSpec(far.shape, lambda g: (0, 0))
    return pl.pallas_call(
        functools.partial(pair_sum_body, len(own)),
        grid=(1,),
        in_specs=[half_rows(part, 0) for part in own]
        + [pl.BlockSpec(part.shape, lambda g: (0, 0)) for part in received]
        + [whole, ANY],
        out_specs=whole,
        out_shape=out(far.shape, BF),
        compiler_params=params(52),
        cost_estimate=cost(1e6, 1e5),
    )(*own, *received, far, after)


def split_sum_body(index_ref, own_ref, received_ref, far_ref, _, *out_refs):
    for d, ref in enumerate(out_refs):
        place = jnp.bitwise_xor(index_ref[3], d)
        parts = (own_ref, received_ref, far_ref)
        ref[...] = sum(part[place].astype(F32) for part in parts).astype(BF)


def split_sum(ids, own, received, far, after, nz):
    rows, cols = far.shape
    shape = (nz, rows // nz, cols)
    whole = pl.BlockSpec(shape, lambda g: (0, 0, 0))
    return pl.pallas_call(
        split_sum_body,
        grid=(1,),
        in_specs=[SMEM, whole, whole, whole, ANY],
        out_specs=[pl.BlockSpec(shape[1:], lambda g: (0, 0))] * nz,
        out_shape=[out(shape[1:], BF)] * nz,
        compiler_params=params(52),
        cost_estimate=cost(1e6, 1e5),
    )(ids, own.reshape(2 * nz, *shape[1:]), received.reshape(shape), far.reshape(shape), after)


def z_sum_body(ny, number, blocks_ref, *refs):
    part_refs, (_, *out_refs) = refs[:number], refs[number:]
    first = jnp.sum(blocks_ref[...].astype(F32), 0)
    second = sum(ref[...].astype(F32) for ref in part_refs)
    cols = first.shape[1]
    rows = first.shape[0] // ny
    for j, ref in enumerate(out_refs):
        ref[:, :cols] = first[j * rows : (j + 1) * rows].astype(ref.dtype)
        ref[:, cols:] = second[j * rows : (j + 1) * rows].astype(ref.dtype)


def z_sum(blocks, parts, ny, after):
    rows, cols = parts[0].shape
    shape = (rows // ny, blocks.shape[2] + cols)
    return pl.pallas_call(
        functools.partial(z_sum_body, ny, len(parts)),
        in_specs=[VMEM] * (1 + len(parts)) + [ANY],
        out_specs=[VMEM] * ny,
        out_shape=[out(shape, F32)] + [out(shape, BF)] * (ny - 1),
        compiler_params=params(52),
        cost_estimate=cost(1e6, 1e5),
    )(blocks, *parts, after)


def finish_body(ny, weight_ref, gain_ref, *refs):
    part_refs, refs = refs[:ny], refs[ny + 1 :]
    grad_ref, out_ref, router_ref, gain1_ref, gain2_ref = refs
    rows, width = out_ref.shape
    cols = width // GROUPS
    total = sum(ref[...].astype(F32) for ref in part_refs)
    first, second = total[:, : width + 3 * cols], total[:, width + 3 * cols :]
    out_ref[...] = first[:, :width]
    extra = second[:, 3 * cols :]
    experts = router_ref.shape[0]
    groups = [first[:, width:], second]
    gain_grad = 0.0
    for g, total in enumerate(groups):
        for j in range(3):
            piece = total[:, j * cols : (j + 1) * cols]
            place = slice((j * GROUPS + g) * cols, (j * GROUPS + g + 1) * cols)
            grad_ref[:, place] = piece
            weight = weight_ref[:, place].astype(F32)
            gain_grad += jnp.sum(piece * weight, -1, keepdims=True)
    lane = lax.broadcasted_iota(jnp.int32, (rows, 128), 1)
    turned = jnp.transpose(jnp.where(lane == experts + 1, gain_grad / gain_ref[...], extra))
    gain2_ref[...] = turned[:1]
    router_ref[...] = turned[1 : experts + 1]
    gain1_ref[...] = turned[experts + 1 : experts + 2]


def finish(weight, gain, parts, experts, after):
    rows, width = weight.shape
    return pl.pallas_call(
        functools.partial(finish_body, len(parts)),
        in_specs=[VMEM] * (2 + len(parts)) + [ANY],
        out_specs=[VMEM] * 5,
        out_shape=[
            out((rows, width), F32),
            out((rows, width // 3), F32),
            out((experts, rows), F32),
            out((1, rows), F32),
            out((1, rows), F32),
        ],
        compiler_params=params(52),
        cost_estimate=cost(parts[0].size, 4 * parts[0].size),
    )(weight, gain, *parts, after)


def per_device(
    sizes,
    tokens,
    cotangent,
    norm1_gain,
    qkv_weight,
    out_weight,
    norm2_gain,
    router_weight,
    up_weight,
    down_weight,
    routes,
    capacity,
):
    n_dp, n_ex = sizes
    ny = n_dp // 2
    tok, width = tokens.shape
    experts = router_weight.shape[1]
    cap = 3 * tok // (4 * experts)
    dp = lax.axis_index("dp")
    ex = lax.axis_index("expert")
    ids = jnp.stack([dp // 2, dp % 2, ex, ex // 2]).astype(jnp.int32)
    gain1, gain2 = norm1_gain, norm2_gain
    router = lax.dynamic_slice(router_weight, (0, ex), (width, 1)).reshape(1, width)
    up, down = up_weight[0], down_weight[0]
    rows_dev = width // (n_dp * n_ex)
    start = (dp * n_ex + ex) * rows_dev
    weight_rows = lax.dynamic_slice(qkv_weight, (start, 0), (rows_dev, 3 * width))
    gain_rows = lax.dynamic_slice(norm1_gain, (start,), (rows_dev,)).reshape(rows_dev, 1)
    nz = n_ex // 2
    row = jnp.arange(width, dtype=jnp.int32)
    chunk = row // rows_dev
    y, core, z, x = chunk // (2 * n_ex), chunk // n_ex % 2, chunk // 2 % nz, chunk % 2
    order = ((core ^ (dp % 2)) * 2 + (x ^ (ex % 2))) * nz + z
    order = ((order * ny + (y ^ (dp // 2))) * rows_dev + row % rows_dev).reshape(1, width)

    z_groups = [list(range(0, n_ex, 2)), list(range(1, n_ex, 2))]

    def exchange(value):
        return lax.all_to_all(value, "expert", split_axis=0, concat_axis=0, tiled=True)

    def exchange_z(value):
        return lax.all_to_all(
            value, "expert", split_axis=0, concat_axis=0, tiled=True, axis_index_groups=z_groups
        )

    def to_core(value):
        return lax.ppermute(value, "dp", [(i, i ^ 1) for i in range(n_dp)])

    def to_y(values):
        return [
            lax.ppermute(values[j - 1], "dp", [(i, i ^ (2 * j)) for i in range(n_dp)])
            for j in range(1, ny)
        ]

    def to_core_all(values):
        return [to_core(value) for value in values]

    def to_x(value):
        return lax.ppermute(value, "expert", [(i, i ^ 1) for i in range(n_ex)])

    slot, cots = plan(routes, capacity, cotangent, cap)
    cots = exchange(cots)
    act, qkv, mixed, lse, resid, first, second = attend(
        tokens, gain1, qkv_weight, out_weight, gain2, slot, experts * cap
    )
    first, cots = lax.optimization_barrier((first, cots))
    first = exchange(first)
    act, mixed_turned = turn(order, act, mixed)
    first, order, weight_rows, gain_rows, second, act, mixed_turned, ids = lax.optimization_barrier(
        (first, order, weight_rows, gain_rows, second, act, mixed_turned, ids)
    )
    second = exchange(second)
    first, *kept = expert(ids, first, cots, router, up, down, None)
    first = exchange(first)
    second, gated, *kept = expert(ids, second, cots, router, up, down, kept)
    second = exchange(second)

    far_send, near_send, far_own, near_own = expert_grads(kept, ids, ny, first)
    second, gated = lax.optimization_barrier((second, gated))
    gated = exchange(gated)

    dresid, dmixed, gain2_row, own, *sent = back_out(
        first, second, slot, resid, cotangent, gain2, out_weight, mixed_turned, near_own
    )
    part1, own1, *sent1 = back_heads(0, qkv, dmixed, mixed, lse, act, ids)
    far_own, own1 = lax.optimization_barrier((far_own, own1))
    grads_far = far_grads(far_own, to_core(far_send), ids)
    grads_y = to_y(grads_far)
    near1, far1 = zip(to_core_all(sent), to_core_all(sent1))
    near1, far1 = lax.optimization_barrier((near1, far1))
    own1 = [own, own1]
    far1 = core_sum(own1, far1, grads_far)
    part2, own2, *sent2 = back_heads(
        1, qkv, dmixed, mixed, lse, act, far1, order, gain2_row, kept[2], kept[4]
    )
    far1 = to_x(far1)
    near2, far2 = to_core_all(sent2)
    block_out = combine(slot, resid, gated, part2)
    far2 = core_sum([own2], [far2], block_out)
    total1 = pair_sum(own1, near1, far1, far2)
    far2 = to_x(far2)
    blocks1 = exchange_z(total1)
    tokens_grad = back_in([part1, part2], qkv_weight, tokens, gain1, dresid, total1)
    own, *sent = split_sum(ids, own2, near2, far2, tokens_grad, nz)
    parts = [own] + [
        lax.ppermute(value, "expert", [(i, i ^ (2 * d + 2)) for i in range(n_ex)])
        for d, value in enumerate(sent)
    ]
    blocks1 = blocks1.reshape(nz, ny * rows_dev, blocks1.shape[1])
    near, *far = z_sum(blocks1, parts, ny, tokens_grad)
    total = [near] + to_y(far)
    up_grad, down_grad = near_grads(near_own, to_core(near_send), grads_y, near)
    qkv_grad, out_grad, router_grad, gain1_grad, gain2_grad = finish(
        weight_rows, gain_rows, total, experts, up_grad
    )
    return (
        block_out,
        tokens_grad,
        gain1_grad[0],
        qkv_grad,
        out_grad,
        gain2_grad[0],
        router_grad.T,
        up_grad[None],
        down_grad[None],
    )


def solution(mesh):
    sizes = (mesh.shape["dp"], mesh.shape["expert"])
    return jax.shard_map(
        functools.partial(per_device, sizes),
        mesh=mesh,
        in_specs=(
            P(("dp", "expert"), None),
            P(("dp", "expert"), None),
            P(),
            P(),
            P(),
            P(),
            P(),
            P("expert", None, None),
            P("expert", None, None),
            P(("dp", "expert")),
            P(),
        ),
        out_specs=(
            P(("dp", "expert"), None),
            P(("dp", "expert"), None),
            P(("dp", "expert")),
            P(("dp", "expert"), None),
            P(("dp", "expert"), None),
            P(("dp", "expert")),
            P(("dp", "expert"), None),
            P("expert", None, "dp"),
            P("expert", "dp", None),
        ),
        check_vma=False,
    )
```
